32 devices in a mesh: rep: 16 (over z, x, core), fsdp: 2 (over y).
Axes of the slice: x: 2, y: 2, z: 4, core: 2. Of those that a mesh axis runs over, the one named last changes fastest.
Arguments:
- global_weights: bfloat16 [8192, 1024], P(None, 'fsdp'), may hold values from -0.75 to 0.75
- momentum: float32 [8192, 1024], P('rep', 'fsdp'), may hold values from -0.3125 to 0.3125
- first_moment: float32 [16, 8192, 1024], P('rep', None, 'fsdp'), may hold values from -0.0029296875 to 0.0029296875
- second_moment: float32 [16, 8192, 1024], P('rep', None, 'fsdp'), may hold values from 1e-08 to 1e-07
- hidden_bank: bfloat16 [16, 256, 8192], P('rep', 'fsdp'), may hold values from -0.15625 to 0.15625
- target_bank: bfloat16 [16, 256, 1024], P('rep', None, 'fsdp'), may hold values from -6 to 6
- token_ids: int32 [16, 2, 512], P('rep'), may hold values from 0 to 255
Outputs:
- new_weights: bfloat16 [8192, 1024], P(None, 'fsdp')
- new_momentum: float32 [8192, 1024], P('rep', 'fsdp')
The draws below stay inside these ranges and needn't reach their ends.
All inputs are finite; a program needn't handle non-finite values.
Results may differ from the reference program's by a relative error of at most 0.0034.
Values may be sent and summed in bfloat16 or wider, within the bound.
No kernel may reach another device: no remote copies, remote signals or barrier semaphores. Data moves between devices by JAX's collectives and lax.ppermute only.
A program may use at most 192 MiB of HBM per device.

```python
import math
import jax
import jax.numpy as jnp
from jax import lax

D = 8192
KVW = 1024
TOK = 512
INNER = 2
STORE = 256
REPLICAS = 16


def with_ends(array, key, low, high):
    place = [jax.random.randint(jax.random.fold_in(key, axis), (), 0, length) for axis, length in enumerate(array.shape)]
    main_axis = array.shape.index(max(array.shape))
    beside = place[:main_axis] + [(place[main_axis] + 1) % array.shape[main_axis]] + place[main_axis + 1:]
    return array.at[tuple(place)].set(low).at[tuple(beside)].set(high)


def levels(own_key, shape, cuts, least, largest):
    def one(dim, shards_of):
        heights = jax.random.uniform(jax.random.fold_in(jax.random.fold_in(own_key, 6), dim), (shards_of,), jnp.float32, least / len(cuts), largest / len(cuts))
        return jnp.repeat(jnp.exp(heights), shape[dim] // shards_of).reshape((-1,) + (1,) * (len(shape) - dim - 1))

    factor_of = one(*cuts[0])
    for cut in cuts[1:]:
        factor_of = factor_of * one(*cut)
    return factor_of


def bell_draw(own_key, dims, deviation, bound, cuts=(), held_as=jnp.bfloat16):
    array = deviation * jax.random.normal(own_key, dims, jnp.float32)
    if cuts:
        array = array * levels(own_key, dims, cuts, -0.22, 0.18)
    return jnp.clip(array, -bound, bound).astype(held_as)


def setup_inputs(seed: int = 0) -> dict:
    key_list = jax.random.split(jax.random.key(seed), 8)
    global_weights = bell_draw(key_list[0], (D, KVW), 0.05, 0.75, ((1, 2),))
    momentum = bell_draw(key_list[1], (D, KVW), 0.02, 0.3125, ((0, 16), (1, 2)), jnp.float32)
    first_moment = bell_draw(key_list[2], (REPLICAS, D, KVW), 0.0002, 0.0029296875, ((0, 16), (2, 2)), jnp.float32)
    second_moment = jnp.clip(jnp.exp(math.log(1.0000000116860974e-07) - 2.3025851 * jax.random.uniform(key_list[3], (REPLICAS, D, KVW), jnp.float32) ** levels(key_list[3], (REPLICAS, D, KVW), ((0, 16), (2, 2)), -0.2, 0.2)), 9.99999993922529e-09, 1.0000000116860974e-07)
    hidden_bank = bell_draw(key_list[4], (REPLICAS, STORE, D), (D ** -0.5), 0.15625, ((0, 16), (1, 2)))
    target_bank = bell_draw(key_list[5], (REPLICAS, STORE, KVW), 1.0, 6.0, ((0, 16), (2, 2)))
    token_ids = with_ends(jax.random.randint(key_list[6], (REPLICAS, INNER, TOK), 0, STORE), jax.random.fold_in(key_list[6], 1), 0, STORE - 1).astype(jnp.int32)
    return {"global_weights": global_weights, "momentum": momentum, "first_moment": first_moment, "second_moment": second_moment, "hidden_bank": hidden_bank, "target_bank": target_bank, "token_ids": token_ids}


def reference(global_weights, momentum, first_moment, second_moment, hidden_bank, target_bank, token_ids):
    start = global_weights.astype(jnp.float32)

    def replica(total, members):
        first_state, second_state, bank_rows, targets, ids_all = members
        weights = start
        for inner_step in range(INNER):
            chosen = ids_all[inner_step].astype(jnp.int32)
            picked = jnp.take(bank_rows, chosen, axis=0)
            wanted = jnp.take(targets, chosen, axis=0)
            output = jnp.dot(picked, weights.astype(jnp.bfloat16), preferred_element_type=jnp.float32)
            residual_out = ((output - wanted.astype(jnp.float32)) / TOK).astype(jnp.bfloat16)
            gradient = jnp.dot(picked.T, residual_out, preferred_element_type=jnp.float32)
            first_state = 0.9 * first_state + 0.1 * gradient
            second_state = 0.95 * second_state + 0.05 * gradient * gradient
            weights = weights - 0.1 * (first_state / (jnp.sqrt(second_state) + 1e-08) + 0.1 * weights)
        return (total + (start - weights), None)
    summed, unused = lax.scan(replica, jnp.zeros_like(start), (first_moment, second_moment, hidden_bank, target_bank, token_ids))
    average = summed / REPLICAS
    new_momentum = 0.9 * momentum + average
    new_weights = (start - 0.7 * (average + 0.9 * new_momentum)).astype(jnp.bfloat16)
    return (new_weights, new_momentum)
```

```python
import functools
import jax
import jax.numpy as jnp
from jax import lax
from jax.experimental import pallas as pl
from jax.experimental.pallas import tpu as pltpu
from jax.sharding import PartitionSpec as P

F32 = jnp.float32
BF16 = jnp.bfloat16
WIRE = jnp.float16
WIRE_SCALE = 64.0
CORES = 2
LANES = 128
VMEM_LIMIT = 50 * 1024 * 1024


def forward_kernel(part_ref, weights_ref, turned_ref, product_ref):
    @pl.when(pl.program_id(0) == 0)
    def _():
        product_ref[...] = jnp.zeros_like(product_ref)

    part = part_ref[...]
    turned_ref[...] = part.T
    product_ref[...] += jnp.dot(part, weights_ref[...], preferred_element_type=F32)


def forward(part, weights):
    rows, depth = part.shape
    columns = weights.shape[1]
    block = min(depth, 2048)
    return pl.pallas_call(
        forward_kernel,
        grid=(depth // block,),
        in_specs=[
            pl.BlockSpec((rows, block), lambda d: (0, d)),
            pl.BlockSpec((block, columns), lambda d: (d, 0)),
        ],
        out_specs=[
            pl.BlockSpec((block, rows), lambda d: (d, 0)),
            pl.BlockSpec((rows, columns), lambda d: (0, 0)),
        ],
        out_shape=[
            jax.ShapeDtypeStruct((depth, rows), BF16),
            jax.ShapeDtypeStruct((rows, columns), F32),
        ],
        compiler_params=pltpu.CompilerParams(vmem_limit_bytes=VMEM_LIMIT),
        cost_estimate=pl.CostEstimate(
            flops=2 * rows * depth * columns,
            bytes_accessed=2 * depth * columns + 4 * rows * depth,
            transcendentals=0,
        ),
        name="forward",
    )(part, weights)


def inner_kernel(
    tokens,
    core_ref,
    low_ref,
    high_ref,
    low_turned_ref,
    high_turned_ref,
    start_ref,
    first_ref,
    second_ref,
    low_product_ref,
    high_product_ref,
    target_ref,
    count_ref,
    send_ref,
    keep_ref,
    first_state,
    second_state,
    weights_state,
    output_state,
    residual_state,
):
    step = pl.program_id(0)
    slab = pl.program_id(1)
    groups, cores, rows, columns = start_ref.shape
    core = core_ref[0]

    def weigh(output, which):
        residual = ((output - target_ref[...].astype(F32)) / tokens).astype(BF16)
        residual_state[...] = (residual.astype(F32) * count_ref[which]).astype(BF16)

    def update(first, second, weights, gradient):
        first = 0.9 * first + 0.1 * gradient
        second = 0.95 * second + 0.05 * gradient * gradient
        weights = weights - 0.1 * (first / (jnp.sqrt(second) + 1e-08) + 0.1 * weights)
        return first, second, weights

    def gradient_of(group, which):
        turned = jnp.concatenate(
            [low_turned_ref[group, which], high_turned_ref[group, which]], axis=1
        )
        return jnp.dot(turned, residual_state[...], preferred_element_type=F32)

    @pl.when((step == 0) & (slab == 0))
    def _():
        weigh(jnp.concatenate([low_product_ref[...], high_product_ref[...]], axis=0), 0)
        output_state[...] = jnp.zeros_like(output_state)

    @pl.when((step == 1) & (slab == 0))
    def _():
        weigh(output_state[...], 1)

    @pl.when(step == 0)
    def _():
        total = jnp.zeros(output_state.shape, F32)
        for group in range(groups):
            for which in range(cores):
                first, second, weights = update(
                    first_ref[group, which],
                    second_ref[group, which],
                    start_ref[group, which].astype(F32),
                    gradient_of(group, which),
                )
                first_state[slab, group, which] = first
                second_state[slab, group, which] = second
                weights_state[slab, group, which] = weights
                place = pl.ds((group * cores + which) * rows, rows)
                picked = jnp.concatenate([low_ref[:, place], high_ref[:, place]], axis=0)
                total += jnp.dot(picked, weights.astype(BF16), preferred_element_type=F32)
        output_state[...] += total

    @pl.when(step == 1)
    def _():
        for group in range(groups):
            for which, out_ref in ((1 - core, send_ref), (core, keep_ref)):
                _, _, weights = update(
                    first_state[slab, group, which],
                    second_state[slab, group, which],
                    weights_state[slab, group, which],
                    gradient_of(group, which),
                )
                change = start_ref[group, which].astype(F32) - weights
                out_ref[group] = change * WIRE_SCALE


def inner(chunk, width, core, banks, turned, start, first, second, products, target, count, tokens):
    slabs, groups, cores, rows, _ = start.shape
    half, depth = banks[0].shape
    block = depth // slabs

    def held(step, slab):
        return jnp.where(step == 0, slab, slabs - 1)

    def drawn(step, slab):
        return jnp.where(step == 0, 0, slab)

    natural = pl.BlockSpec((half, block), lambda s, z, c: (0, held(s, z)))
    flipped = pl.BlockSpec((None, groups, cores, rows, half), lambda s, z, c: (z, 0, 0, 0, 0))
    state = pl.BlockSpec(
        (None, groups, cores, rows, width), lambda s, z, c: (held(s, z), 0, 0, 0, chunk)
    )
    product = pl.BlockSpec((half, width), lambda s, z, c: (0, chunk))
    change = pl.BlockSpec((None, groups, rows, width), lambda s, z, c: (drawn(s, z), 0, 0, 0))
    elements = depth * width
    return pl.pallas_call(
        functools.partial(inner_kernel, float(tokens)),
        grid_spec=pltpu.PrefetchScalarGridSpec(
            num_scalar_prefetch=1,
            grid=(2, slabs),
            in_specs=[
                natural,
                natural,
                flipped,
                flipped,
                pl.BlockSpec(
                    (None, groups, cores, rows, width), lambda s, z, c: (z, 0, 0, 0, chunk)
                ),
                state,
                state,
                product,
                product,
                pl.BlockSpec((2 * half, width), lambda s, z, c: (0, chunk)),
                pl.BlockSpec(count.shape, lambda s, z, c: (0, 0, 0)),
            ],
            out_specs=[change, change],
            scratch_shapes=[
                pltpu.VMEM((slabs, groups, cores, rows, width), F32),
                pltpu.VMEM((slabs, groups, cores, rows, width), F32),
                pltpu.VMEM((slabs, groups, cores, rows, width), F32),
                pltpu.VMEM((2 * half, width), F32),
                pltpu.VMEM((2 * half, width), BF16),
            ],
        ),
        out_shape=[
            jax.ShapeDtypeStruct((slabs, groups, rows, width), F32),
            jax.ShapeDtypeStruct((slabs, groups, rows, width), F32),
        ],
        compiler_params=pltpu.CompilerParams(vmem_limit_bytes=VMEM_LIMIT),
        cost_estimate=pl.CostEstimate(
            flops=12 * half * elements,
            bytes_accessed=16 * elements + 12 * half * depth,
            transcendentals=4 * elements,
        ),
        name="inner",
    )(core, *banks, *turned, start, first, second, *products, target, count)


def split_rep(mesh_size):
    slabs = 4 if mesh_size % 8 == 0 else 1
    return slabs, mesh_size // (slabs * CORES), CORES


def per_device(sizes, global_weights, momentum, first_moment, second_moment, hidden_bank, target_bank, token_ids):
    reps, shards = sizes
    slabs, groups, cores = split_rep(reps)
    depth, columns = global_weights.shape
    rows = depth // reps
    store = hidden_bank.shape[1] * shards
    ids = token_ids[0]
    tokens = ids.shape[1]
    width = min(columns, LANES)
    chunks = columns // width

    mine = lax.axis_index("rep")
    my_core = lax.rem(mine, cores)
    my_group = lax.rem(mine // cores, groups)
    my_slab = mine // (cores * groups)

    def index_of(slab, group, core):
        return (slab * groups + group) * cores + core

    places = [(s, g, c) for s in range(slabs) for g in range(groups) for c in range(cores)]

    def shifted(array, slab=0, group=0, core=0):
        pairs = [
            (
                index_of(s, g, c),
                index_of((s + slab) % slabs, (g + group) % groups, (c + core) % cores),
            )
            for s, g, c in places
        ]
        return lax.ppermute(array, "rep", pairs)

    own_bank = hidden_bank[0]
    target = target_bank[0]
    count = jnp.sum(
        ids[:, :, None] == jnp.arange(store, dtype=ids.dtype)[None, None, :], axis=1
    ).astype(F32)
    if shards == 2:
        banks = (own_bank, lax.ppermute(own_bank, "fsdp", [(0, 1), (1, 0)]))
        swap = lax.axis_index("fsdp") == 1
        half = store // 2
        target = jnp.where(swap, jnp.roll(target, half, axis=0), target)
        count = jnp.where(swap, jnp.roll(count, half, axis=1), count)
    else:
        whole = lax.all_gather(own_bank, "fsdp", axis=0, tiled=True)
        banks = (whole[: store // 2], whole[store // 2 :])
    count = count[:, :, None]

    turned, products = zip(*(forward(bank, global_weights) for bank in banks))
    turned = [array.reshape(slabs, groups, cores, rows, store // 2) for array in turned]
    cut = (slabs, groups, cores, rows, columns)
    start = global_weights.reshape(cut)
    first = first_moment.reshape(cut)
    second = second_moment.reshape(cut)
    core_operand = my_core.reshape(1).astype(jnp.int32)
    my_start = lax.dynamic_slice_in_dim(global_weights, mine * rows, rows, 0)

    def wire(array):
        return array.astype(WIRE)

    def pick(array, index):
        return lax.dynamic_index_in_dim(array, index, 0, keepdims=False)

    new_momentum = []
    new_weights = []
    for chunk in range(chunks):
        send, keep = inner(
            chunk, width, core_operand, banks, turned, start, first, second, products, target, count, tokens
        )
        total = keep + shifted(wire(send), core=1).astype(F32)

        by_group = jnp.swapaxes(total, 0, 1)
        total = pick(by_group, my_group)
        for ahead in range(1, groups):
            outgoing = wire(pick(by_group, lax.rem(my_group + ahead, groups)))
            total = total + shifted(outgoing, group=ahead).astype(F32)

        by_slab = total
        total = pick(by_slab, my_slab)
        for ahead in range(1, slabs):
            outgoing = wire(pick(by_slab, lax.rem(my_slab + ahead, slabs)))
            total = total + shifted(outgoing, slab=ahead).astype(F32)

        share = slice(chunk * width, (chunk + 1) * width)
        average = total * (1.0 / (WIRE_SCALE * reps))
        moved = 0.9 * momentum[:, share] + average
        new_momentum.append(moved)
        fresh = (my_start[:, share].astype(F32) - 0.7 * (average + 0.9 * moved)).astype(BF16)

        stack = jnp.stack([fresh] + [shifted(fresh, slab=ahead) for ahead in range(1, slabs)])
        stack = jnp.stack([stack] + [shifted(stack, group=ahead) for ahead in range(1, groups)])
        stack = jnp.stack([stack, shifted(stack, core=1)])
        new_weights.append(stack)

    place = jnp.stack([my_slab, my_group, my_core]).astype(jnp.int32)
    return assemble(place, new_weights, cut), jnp.concatenate(new_momentum, axis=1)


def assemble_kernel(chunks, width, place_ref, *refs):
    stacks, out_ref, semaphore = refs[:chunks], refs[chunks], refs[chunks + 1]
    cores, groups, slabs = stacks[0].shape[:3]
    copies = []
    for chunk, stack in enumerate(stacks):
        for c in range(cores):
            for g in range(groups):
                for s in range(slabs):
                    target = out_ref.at[
                        lax.rem(place_ref[0] + (slabs - s), slabs),
                        lax.rem(place_ref[1] + (groups - g), groups),
                        lax.rem(place_ref[2] + (cores - c), cores),
                        :,
                        pl.ds(chunk * width, width),
                    ]
                    copies.append(
                        pltpu.make_async_copy(stack.at[c, g, s], target, semaphore.at[len(copies)])
                    )
    for copy in copies:
        copy.start()
    for copy in copies:
        copy.wait()


def assemble(place, stacks, cut):
    count = len(stacks) * cut[0] * cut[1] * cut[2]
    width = stacks[0].shape[-1]
    out = pl.pallas_call(
        functools.partial(assemble_kernel, len(stacks), width),
        in_specs=[pl.BlockSpec(memory_space=pltpu.SMEM)]
        + [pl.BlockSpec(memory_space=pl.ANY)] * len(stacks),
        out_specs=pl.BlockSpec(memory_space=pl.ANY),
        out_shape=jax.ShapeDtypeStruct(cut, BF16),
        scratch_shapes=[pltpu.SemaphoreType.DMA((count,))],
        compiler_params=pltpu.CompilerParams(vmem_limit_bytes=VMEM_LIMIT),
        name="assemble",
    )(place, *stacks)
    return out.reshape(cut[0] * cut[1] * cut[2] * cut[3], cut[4])


def solution(mesh):
    sizes = (mesh.shape["rep"], mesh.shape["fsdp"])
    return jax.shard_map(
        functools.partial(per_device, sizes),
        mesh=mesh,
        in_specs=(
            P(None, "fsdp"),
            P("rep", "fsdp"),
            P("rep", None, "fsdp"),
            P("rep", None, "fsdp"),
            P("rep", "fsdp", None),
            P("rep", None, "fsdp"),
            P("rep", None, None),
        ),
        out_specs=(P(None, "fsdp"), P("rep", "fsdp")),
        check_vma=False,
    )
```

```python
import functools
import math
import jax
import jax.numpy as jnp
from jax import lax
from jax.experimental import pallas as pl
from jax.experimental.pallas import tpu as pltpu
from jax.sharding import PartitionSpec as P

F32 = jnp.float32
BF16 = jnp.bfloat16
WIRE = jnp.float16
WIRE_SCALE = 64.0
LANES = 128
SLABS = 4
PIECE = 64
MIB = 1024 * 1024


def forward_kernel(part_ref, weights_ref, turned_ref, product_ref):
    @pl.when(pl.program_id(0) == 0)
    def _():
        product_ref[...] = jnp.zeros_like(product_ref)

    part = part_ref[...]
    turned_ref[...] = part.T
    product_ref[...] += jnp.dot(part, weights_ref[...], preferred_element_type=F32)


def forward(part, weights):
    rows, depth = part.shape
    columns = weights.shape[1]
    block = depth // SLABS
    return pl.pallas_call(
        forward_kernel,
        grid=(SLABS,),
        in_specs=[
            pl.BlockSpec((rows, block), lambda d: (0, d)),
            pl.BlockSpec((block, columns), lambda d: (d, 0)),
        ],
        out_specs=[
            pl.BlockSpec((block, rows), lambda d: (d, 0)),
            pl.BlockSpec((rows, columns), lambda d: (0, 0)),
        ],
        out_shape=[
            jax.ShapeDtypeStruct((depth, rows), BF16),
            jax.ShapeDtypeStruct((rows, columns), F32),
        ],
        compiler_params=pltpu.CompilerParams(vmem_limit_bytes=24 * MIB),
        cost_estimate=pl.CostEstimate(
            flops=2 * rows * depth * columns,
            bytes_accessed=2 * depth * columns + 4 * rows * depth,
            transcendentals=0,
        ),
        name="forward",
    )(part, weights)


def arrive_kernel(part_ref, weights_ref, *refs):
    natural_ref, turned_ref, product_ref = refs[-3:]
    part = part_ref[...]
    natural_ref[...] = part
    turned_ref[...] = part.T
    product = jnp.dot(part, weights_ref[...], preferred_element_type=F32)
    if len(refs) > 3:
        product = product + refs[2][...]
    product_ref[...] = product


def arrive(piece, part, weights, before):
    rows, block = part.shape
    depth, columns = weights.shape
    whole = pl.BlockSpec((rows, columns), lambda d: (0, 0))
    return pl.pallas_call(
        arrive_kernel,
        grid=(1,),
        in_specs=[
            pl.BlockSpec((rows, block), lambda d: (0, 0)),
            pl.BlockSpec((block, columns), lambda d: (piece, 0)),
        ]
        + ([pl.BlockSpec(memory_space=pl.ANY)] * 2 + [whole] if before else []),
        out_specs=[
            pl.BlockSpec((rows, block), lambda d: (0, piece)),
            pl.BlockSpec((block, rows), lambda d: (piece, 0)),
            whole,
        ],
        out_shape=[
            jax.ShapeDtypeStruct((rows, depth), BF16),
            jax.ShapeDtypeStruct((depth, rows), BF16),
            jax.ShapeDtypeStruct((rows, columns), F32),
        ],
        input_output_aliases={2: 0, 3: 1} if before else {},
        compiler_params=pltpu.CompilerParams(vmem_limit_bytes=24 * MIB),
        cost_estimate=pl.CostEstimate(
            flops=2 * rows * block * columns,
            bytes_accessed=2 * block * columns + 6 * rows * block,
            transcendentals=0,
        ),
        name="arrive",
    )(part, weights, *before)


def inner_kernel(
    tokens,
    core_ref,
    low_ref,
    high_ref,
    low_turned_ref,
    high_turned_ref,
    start_ref,
    first_ref,
    second_ref,
    low_product_ref,
    high_product_ref,
    target_ref,
    count_ref,
    send_ref,
    keep_ref,
    first_state,
    second_state,
    weights_state,
    output_state,
    residual_state,
    gradient_state,
    rounded_state,
):
    step = pl.program_id(0)
    slab = pl.program_id(1)
    pairs, cores, rows, _ = start_ref.shape
    core = core_ref[0]
    pieces = [pl.ds(begin, PIECE) for begin in range(0, rows, PIECE)]

    def weigh(output, which):
        residual = ((output - target_ref[...].astype(F32)) / tokens).astype(BF16)
        residual_state[...] = (residual.astype(F32) * count_ref[which]).astype(BF16)

    def descend(first, second, weights):
        root = second * lax.rsqrt(second)
        below = (100.0 * math.sqrt(0.05)) * root + 1e-06
        return 0.99 * weights - first * lax.rsqrt(below * below)

    def gradient_of(pair, which, slot):
        turned = jnp.concatenate(
            [low_turned_ref[pair, which], high_turned_ref[pair, which]], axis=1
        )
        gradient_state[slot] = jnp.dot(
            turned, residual_state[...], preferred_element_type=F32
        )

    @pl.when((step == 0) & (slab == 0))
    def _():
        weigh(jnp.concatenate([low_product_ref[...], high_product_ref[...]], axis=0), 0)
        output_state[...] = jnp.zeros_like(output_state)

    @pl.when((step == 1) & (slab == 0))
    def _():
        weigh(output_state[...], 1)

    @pl.when(step == 0)
    def _():
        total = jnp.zeros(output_state.shape, F32)
        for pair in range(pairs):
            for which in range(cores):
                slot = pair * cores + which
                gradient_of(pair, which, slot)
                for piece in pieces:
                    gradient = gradient_state[slot, piece]
                    first = 9.0 * first_ref[pair, which, piece] + gradient
                    second = 19.0 * second_ref[pair, which, piece] + gradient * gradient
                    weights = descend(first, second, start_ref[pair, which, piece].astype(F32))
                    first_state[slab, pair, which, piece] = first
                    second_state[slab, pair, which, piece] = second
                    weights_state[slab, pair, which, piece] = weights
                    rounded_state[slot, piece] = weights.astype(BF16)
                place = pl.ds(slot * rows, rows)
                picked = jnp.concatenate([low_ref[:, place], high_ref[:, place]], axis=0)
                total += jnp.dot(picked, rounded_state[slot], preferred_element_type=F32)
        output_state[...] += total

    @pl.when(step == 1)
    def _():
        for pair in range(pairs):
            for slot, which, out_ref in ((0, 1 - core, send_ref), (1, core, keep_ref)):
                slot = pair * cores + slot
                gradient_of(pair, which, slot)
                for piece in pieces:
                    gradient = gradient_state[slot, piece]
                    first = 0.9 * first_state[slab, pair, which, piece] + gradient
                    second = 0.95 * second_state[slab, pair, which, piece] + gradient * gradient
                    weights = descend(first, second, weights_state[slab, pair, which, piece])
                    change = start_ref[pair, which, piece].astype(F32) - weights
                    out_ref[pair, piece] = change * WIRE_SCALE


def inner(chunk, width, core, banks, turned, start, first, second, products, target, count, tokens):
    slabs, pairs, cores, rows, _ = start.shape
    half, depth = banks[0].shape
    block = depth // slabs

    def held(step, slab):
        return jnp.where(step == 0, slab, slabs - 1)

    def drawn(step, slab):
        return jnp.where(step == 0, 0, slab)

    natural = pl.BlockSpec((half, block), lambda s, z, c: (0, held(s, z)))
    flipped = pl.BlockSpec((None, pairs, cores, rows, half), lambda s, z, c: (z, 0, 0, 0, 0))
    tile = (None, pairs, cores, rows, width)
    state = pl.BlockSpec(tile, lambda s, z, c: (held(s, z), 0, 0, 0, chunk))
    product = pl.BlockSpec((half, width), lambda s, z, c: (0, chunk))
    change = pl.BlockSpec((None, pairs, rows, width), lambda s, z, c: (drawn(s, z), 0, 0, 0))
    elements = depth * width
    return pl.pallas_call(
        functools.partial(inner_kernel, float(tokens)),
        grid_spec=pltpu.PrefetchScalarGridSpec(
            num_scalar_prefetch=1,
            grid=(2, slabs),
            in_specs=[
                natural,
                natural,
                flipped,
                flipped,
                pl.BlockSpec(tile, lambda s, z, c: (z, 0, 0, 0, chunk)),
                state,
                state,
                product,
                product,
                pl.BlockSpec((2 * half, width), lambda s, z, c: (0, chunk)),
                pl.BlockSpec(count.shape, lambda s, z, c: (0, 0, 0)),
            ],
            out_specs=[change, change],
            scratch_shapes=[
                pltpu.VMEM((slabs, pairs, cores, rows, width), F32),
                pltpu.VMEM((slabs, pairs, cores, rows, width), F32),
                pltpu.VMEM((slabs, pairs, cores, rows, width), F32),
                pltpu.VMEM((2 * half, width), F32),
                pltpu.VMEM((2 * half, width), BF16),
                pltpu.VMEM((pairs * cores, rows, width), F32),
                pltpu.VMEM((pairs * cores, rows, width), BF16),
            ],
        ),
        out_shape=[
            jax.ShapeDtypeStruct((slabs, pairs, rows, width), F32),
            jax.ShapeDtypeStruct((slabs, pairs, rows, width), F32),
        ],
        compiler_params=pltpu.CompilerParams(vmem_limit_bytes=36 * MIB),
        cost_estimate=pl.CostEstimate(
            flops=12 * half * elements,
            bytes_accessed=16 * elements + 12 * half * depth,
            transcendentals=4 * elements,
        ),
        name="inner",
    )(core, *banks, *turned, start, first, second, *products, target, count)


def assemble_kernel(chunk, offsets, place_ref, *refs):
    received = refs[: len(offsets)]
    out_ref, semaphore = refs[-2:]
    width = received[0].shape[-1]
    mine = place_ref[0]
    copies = []
    for ref, group in zip(received, offsets):
        for entry, offset in enumerate(group):
            copies.append(
                pltpu.make_async_copy(
                    ref.at[entry],
                    out_ref.at[lax.bitwise_xor(mine, offset), :, pl.ds(chunk * width, width)],
                    semaphore.at[len(copies)],
                )
            )
    for copy in copies:
        copy.start()
    for copy in copies:
        copy.wait()


def assemble(chunk, place, received, offsets, shape, before):
    vmem = pl.BlockSpec(memory_space=pltpu.VMEM)
    return pl.pallas_call(
        functools.partial(assemble_kernel, chunk, offsets),
        in_specs=[pl.BlockSpec(memory_space=pltpu.SMEM)]
        + [vmem] * len(received)
        + [pl.BlockSpec(memory_space=pl.ANY)] * len(before),
        out_specs=pl.BlockSpec(memory_space=pl.ANY),
        out_shape=jax.ShapeDtypeStruct(shape, BF16),
        input_output_aliases={1 + len(received): 0} if before else {},
        scratch_shapes=[pltpu.SemaphoreType.DMA((sum(map(len, offsets)),))],
        compiler_params=pltpu.CompilerParams(vmem_limit_bytes=12 * MIB),
        cost_estimate=pl.CostEstimate(
            flops=0, bytes_accessed=4 * shape[0] * shape[1] * received[0].shape[-1], transcendentals=0
        ),
        name="assemble",
    )(place, *received, *before)


def tied(first, second):
    return lax.optimization_barrier((first, second))


def per_device(sizes, global_weights, momentum, first_moment, second_moment, hidden_bank, target_bank, token_ids):
    reps, shards = sizes
    bits = reps.bit_length() - 1
    depth, columns = global_weights.shape
    rows = depth // reps
    store = hidden_bank.shape[1] * shards
    half = store // 2
    ids = token_ids[0]
    tokens = ids.shape[1]
    width = min(columns, LANES)
    chunks = columns // width
    mine = lax.axis_index("rep")

    def swapped(array, bit):
        pairs = [(index, index ^ (1 << bit)) for index in range(reps)]
        return lax.ppermute(array, "rep", pairs)

    own_bank = hidden_bank[0]
    target = target_bank[0]
    count = jnp.sum(
        ids[:, :, None] == jnp.arange(store, dtype=ids.dtype)[None, None, :], axis=1
    ).astype(F32)
    if shards == 2:
        block = depth // SLABS
        parts = [
            lax.ppermute(own_bank[:, d * block : (d + 1) * block], "fsdp", [(0, 1), (1, 0)])
            for d in range(SLABS)
        ]
        own_turned, own_product = forward(own_bank, global_weights)
        joined = ()
        for d, part in enumerate(parts):
            joined = arrive(d, part, global_weights, joined)
        banks = (own_bank, joined[0])
        turned = (own_turned, joined[1])
        products = (own_product, joined[2])
        swap = lax.axis_index("fsdp") == 1
        target = jnp.where(swap, jnp.roll(target, half, axis=0), target)
        count = jnp.where(swap, jnp.roll(count, half, axis=1), count)
    else:
        whole = lax.all_gather(own_bank, "fsdp", axis=0, tiled=True)
        banks = (whole[:half], whole[half:])
        turned, products = zip(*(forward(bank, global_weights) for bank in banks))
    count = count[:, :, None]

    cut = (SLABS, reps // (2 * SLABS), 2, rows, columns)
    turned = [array.reshape(cut[:4] + (half,)) for array in turned]
    start = global_weights.reshape(cut)
    first = first_moment.reshape(cut)
    second = second_moment.reshape(cut)
    core = (mine & 1).reshape(1).astype(jnp.int32)
    place = mine.reshape(1).astype(jnp.int32)
    my_start = lax.dynamic_slice_in_dim(global_weights, mine * rows, rows, 0)
    shares = [
        tied(momentum[:, begin : begin + width], my_start[:, begin : begin + width])
        for begin in range(0, columns, width)
    ]

    def halved(terms, bit):
        side = (mine >> bit) & 1
        terms = [term.reshape(-1, 2, rows, width) for term in terms]

        def half_of(which):
            return [
                lax.dynamic_index_in_dim(term, which, 1, keepdims=False).astype(F32)
                for term in terms
            ]

        outgoing = sum(half_of(1 - side)).astype(WIRE)
        return outgoing, [
            lax.dynamic_index_in_dim(term, side, 1, keepdims=False) for term in terms
        ]

    new_momentum = []
    result = ()

    live = {}
    for chunk in range(chunks):
        send, keep = inner(
            chunk, width, core, banks, turned, start, first, second, products, target, count, tokens
        )
        formed = [(chunk, 0, send.reshape(-1, rows, width).astype(WIRE), [keep.reshape(-1, rows, width)])]
        for earlier in range(max(chunk - bits + 1, 0), chunk):
            bit = chunk - earlier
            formed.append((earlier, bit, *halved(live[earlier], bit)))
        if chunk + 1 < chunks:
            outgoing, core = tied([entry[2] for entry in formed], core)
            formed = [entry[:2] + (out, entry[3]) for entry, out in zip(formed, outgoing)]
        for which, bit, outgoing, terms in formed:
            live[which] = terms + [swapped(outgoing, bit)]

    for chunk in range(chunks):
        terms = live[chunk]
        for bit in range(min(chunks - chunk, bits), bits):
            outgoing, terms = halved(terms, bit)
            terms = terms + [swapped(outgoing, bit)]
        total = sum(term.astype(F32) for term in terms)[0]

        average = total * (1.0 / (WIRE_SCALE * reps))
        moved = 0.9 * shares[chunk][0] + average
        new_momentum.append(moved)
        fresh = (shares[chunk][1].astype(F32) - 0.7 * (average + 0.9 * moved)).astype(BF16)

        stack = fresh[None]
        offsets = [0]
        for bit in range(bits - 1, 1, -1):
            stack = jnp.concatenate([stack, swapped(stack, bit)])
            offsets = offsets + [offset ^ (1 << bit) for offset in offsets]
        across = swapped(stack, 1)
        received = [stack, across, swapped(stack, 0), swapped(across, 0)]
        offsets = [[offset ^ low for offset in offsets] for low in (0, 2, 1, 3)]
        result = (
            assemble(chunk, place, received, offsets, (reps, rows, columns), result),
        )

    return result[0].reshape(depth, columns), jnp.concatenate(new_momentum, axis=1)


def solution(mesh):
    sizes = (mesh.shape["rep"], mesh.shape["fsdp"])
    return jax.shard_map(
        functools.partial(per_device, sizes),
        mesh=mesh,
        in_specs=(
            P(None, "fsdp"),
            P("rep", "fsdp"),
            P("rep", None, "fsdp"),
            P("rep", None, "fsdp"),
            P("rep", "fsdp", None),
            P("rep", None, "fsdp"),
            P("rep", None, None),
        ),
        out_specs=(P(None, "fsdp"), P("rep", "fsdp")),
        check_vma=False,
    )
```

```python
import functools
import math
import jax
import jax.numpy as jnp
from jax import lax
from jax.experimental import pallas as pl
from jax.experimental.pallas import tpu as pltpu
from jax.sharding import PartitionSpec as P

F32 = jnp.float32
BF16 = jnp.bfloat16
WIRE = jnp.float16
WIRE_SCALE = 64.0
LANES = 128
SLABS = 4
PIECE = 64
MIB = 1024 * 1024


def forward_kernel(part_ref, weights_ref, turned_ref, product_ref):
    @pl.when(pl.program_id(0) == 0)
    def _():
        product_ref[...] = jnp.zeros_like(product_ref)

    part = part_ref[...]
    turned_ref[...] = part.T
    product_ref[...] += jnp.dot(part, weights_ref[...], preferred_element_type=F32)


def forward(part, weights):
    rows, depth = part.shape
    columns = weights.shape[1]
    block = depth // SLABS
    return pl.pallas_call(
        forward_kernel,
        grid=(SLABS,),
        in_specs=[
            pl.BlockSpec((rows, block), lambda d: (0, d)),
            pl.BlockSpec((block, columns), lambda d: (d, 0)),
        ],
        out_specs=[
            pl.BlockSpec((block, rows), lambda d: (d, 0)),
            pl.BlockSpec((rows, columns), lambda d: (0, 0)),
        ],
        out_shape=[
            jax.ShapeDtypeStruct((depth, rows), BF16),
            jax.ShapeDtypeStruct((rows, columns), F32),
        ],
        compiler_params=pltpu.CompilerParams(vmem_limit_bytes=14 * MIB),
        cost_estimate=pl.CostEstimate(
            flops=2 * rows * depth * columns,
            bytes_accessed=2 * depth * columns + 4 * rows * depth,
            transcendentals=0,
        ),
        name="forward",
    )(part, pinned(weights))


def arrive_kernel(piece, part_ref, weights_ref, *refs):
    natural_ref, turned_ref, product_ref = refs[-3:]
    block = part_ref.shape[1]
    place = pl.ds(piece * block, block)
    part = part_ref[...]
    natural_ref[:, place] = part
    turned_ref[place, :] = part.T
    product = jnp.dot(part, weights_ref[...], preferred_element_type=F32)
    if len(refs) > 3:
        product = product + refs[2][...]
    product_ref[...] = product


def arrive(piece, part, weights, before):
    rows, block = part.shape
    depth, columns = weights.shape
    whole = pl.BlockSpec(memory_space=pltpu.VMEM)
    return pl.pallas_call(
        functools.partial(arrive_kernel, piece),
        grid=(1,),
        in_specs=[whole, pl.BlockSpec((block, columns), lambda d: (piece, 0))]
        + [whole] * len(before),
        out_specs=[whole] * 3,
        out_shape=[
            jax.ShapeDtypeStruct((rows, depth), BF16),
            jax.ShapeDtypeStruct((depth, rows), BF16),
            jax.ShapeDtypeStruct((rows, columns), F32),
        ],
        input_output_aliases={2: 0, 3: 1, 4: 2} if before else {},
        compiler_params=pltpu.CompilerParams(vmem_limit_bytes=10 * MIB),
        cost_estimate=pl.CostEstimate(
            flops=2 * rows * block * columns,
            bytes_accessed=2 * block * columns + 6 * rows * block,
            transcendentals=0,
        ),
        name="arrive",
    )(part, pinned(weights), *before)


def pinned(array):
    return pltpu.with_memory_space_constraint(array, pltpu.HBM)


def changed_place(mine, slab, pair, pairs):
    offset = lax.bitwise_xor(slab * pairs + pair, mine // 2)
    bits = (SLABS * pairs).bit_length() - 1
    place = jnp.int32(0)
    for bit in range(bits):
        place = place * 2 + lax.rem(lax.shift_right_logical(offset, bit), 2)
    return place


def inner_kernel(
    tokens,
    mine_ref,
    low_ref,
    high_ref,
    low_turned_ref,
    high_turned_ref,
    start_ref,
    first_ref,
    second_ref,
    low_product_ref,
    high_product_ref,
    target_ref,
    count_ref,
    send_ref,
    keep_ref,
    first_state,
    second_state,
    weights_state,
    output_state,
    residual_state,
    gradient_state,
    rounded_state,
):
    step = pl.program_id(0)
    slab = pl.program_id(1)
    pairs, cores, rows, _ = start_ref.shape
    mine = mine_ref[0]
    core = lax.rem(mine, cores)
    pieces = [pl.ds(begin, PIECE) for begin in range(0, rows, PIECE)]

    def weigh(output, which):
        residual = ((output - target_ref[...].astype(F32)) / tokens).astype(BF16)
        residual_state[...] = (residual.astype(F32) * count_ref[which]).astype(BF16)

    def descend(first, second, weights):
        root = second * lax.rsqrt(second)
        below = (100.0 * math.sqrt(0.05)) * root + 1e-06
        return 0.99 * weights - first * lax.rsqrt(below * below)

    def gradient_of(pair, which, slot):
        turned = jnp.concatenate(
            [low_turned_ref[slab, pair, which], high_turned_ref[slab, pair, which]], axis=1
        )
        gradient_state[slot] = jnp.dot(
            turned, residual_state[...], preferred_element_type=F32
        )

    @pl.when((step == 0) & (slab == 0))
    def _():
        weigh(jnp.concatenate([low_product_ref[...], high_product_ref[...]], axis=0), 0)
        output_state[...] = jnp.zeros_like(output_state)

    @pl.when((step == 1) & (slab == 0))
    def _():
        weigh(output_state[...], 1)

    @pl.when(step == 0)
    def _():
        total = jnp.zeros(output_state.shape, F32)
        for pair in range(pairs):
            for which in range(cores):
                slot = pair * cores + which
                gradient_of(pair, which, slot)
                for piece in pieces:
                    gradient = gradient_state[slot, piece]
                    first = 9.0 * first_ref[pair, which, piece] + gradient
                    second = 19.0 * second_ref[pair, which, piece] + gradient * gradient
                    weights = descend(first, second, start_ref[pair, which, piece].astype(F32))
                    first_state[slab, pair, which, piece] = first
                    second_state[slab, pair, which, piece] = second
                    weights_state[slab, pair, which, piece] = weights
                    rounded_state[slot, piece] = weights.astype(BF16)
                begin = (slab * pairs * cores + slot) * rows
                place = pl.ds(pl.multiple_of(begin, rows), rows)
                picked = jnp.concatenate([low_ref[:, place], high_ref[:, place]], axis=0)
                total += jnp.dot(picked, rounded_state[slot], preferred_element_type=F32)
        output_state[...] += total

    @pl.when(step == 1)
    def _():
        for pair in range(pairs):
            place = changed_place(mine, slab, pair, pairs)
            for slot, which, out_ref in ((0, 1 - core, send_ref), (1, core, keep_ref)):
                slot = pair * cores + slot
                gradient_of(pair, which, slot)
                for piece in pieces:
                    gradient = gradient_state[slot, piece]
                    first = 0.9 * first_state[slab, pair, which, piece] + gradient
                    second = 0.95 * second_state[slab, pair, which, piece] + gradient * gradient
                    weights = descend(first, second, weights_state[slab, pair, which, piece])
                    change = start_ref[pair, which, piece].astype(F32) - weights
                    out_ref[place, piece] = change * WIRE_SCALE


def inner(chunk, width, mine, banks, turned, start, first, second, products, target, count, tokens):
    slabs, pairs, cores, rows, _ = start.shape
    half, depth = banks[0].shape

    def held(step, slab):
        return jnp.where(step == 0, slab, slabs - 1)

    whole = pl.BlockSpec(memory_space=pltpu.VMEM)
    tile = (None, pairs, cores, rows, width)
    state = pl.BlockSpec(tile, lambda s, z, c: (held(s, z), 0, 0, 0, chunk))
    product = pl.BlockSpec((half, width), lambda s, z, c: (0, chunk))
    elements = depth * width
    return pl.pallas_call(
        functools.partial(inner_kernel, float(tokens)),
        grid_spec=pltpu.PrefetchScalarGridSpec(
            num_scalar_prefetch=1,
            grid=(2, slabs),
            in_specs=[whole] * 4
            + [
                pl.BlockSpec(tile, lambda s, z, c: (z, 0, 0, 0, chunk)),
                state,
                state,
                product,
                product,
                pl.BlockSpec((2 * half, width), lambda s, z, c: (0, chunk)),
                pl.BlockSpec(count.shape, lambda s, z, c: (0, 0, 0)),
            ],
            out_specs=[whole, whole],
            scratch_shapes=[
                pltpu.VMEM((slabs, pairs, cores, rows, width), F32),
                pltpu.VMEM((slabs, pairs, cores, rows, width), F32),
                pltpu.VMEM((slabs, pairs, cores, rows, width), F32),
                pltpu.VMEM((2 * half, width), F32),
                pltpu.VMEM((2 * half, width), BF16),
                pltpu.VMEM((pairs * cores, rows, width), F32),
                pltpu.VMEM((pairs * cores, rows, width), BF16),
            ],
        ),
        out_shape=[
            jax.ShapeDtypeStruct((slabs * pairs, rows, width), F32),
            jax.ShapeDtypeStruct((slabs * pairs, rows, width), F32),
        ],
        compiler_params=pltpu.CompilerParams(vmem_limit_bytes=22 * MIB),
        cost_estimate=pl.CostEstimate(
            flops=12 * half * elements,
            bytes_accessed=20 * elements,
            transcendentals=4 * elements,
        ),
        name="inner",
    )(mine, *banks, *turned, pinned(start), pinned(first), pinned(second), *products, target, count)


def assemble_kernel(chunk, offsets, place_ref, *refs):
    received = refs[: len(offsets)]
    out_ref, semaphore = refs[-2:]
    width = received[0].shape[-1]
    mine = place_ref[0]
    copies = []
    for ref, group in zip(received, offsets):
        for entry, offset in enumerate(group):
            copies.append(
                pltpu.make_async_copy(
                    ref.at[entry],
                    out_ref.at[lax.bitwise_xor(mine, offset), :, pl.ds(chunk * width, width)],
                    semaphore.at[len(copies)],
                )
            )
    for copy in copies:
        copy.start()
    for copy in copies:
        copy.wait()


def assemble(chunk, place, received, offsets, shape, before):
    vmem = pl.BlockSpec(memory_space=pltpu.VMEM)
    return pl.pallas_call(
        functools.partial(assemble_kernel, chunk, offsets),
        in_specs=[pl.BlockSpec(memory_space=pltpu.SMEM)]
        + [vmem] * len(received)
        + [pl.BlockSpec(memory_space=pl.ANY)] * len(before),
        out_specs=pl.BlockSpec(memory_space=pl.ANY),
        out_shape=jax.ShapeDtypeStruct(shape, BF16),
        input_output_aliases={1 + len(received): 0} if before else {},
        scratch_shapes=[pltpu.SemaphoreType.DMA((sum(map(len, offsets)),))],
        compiler_params=pltpu.CompilerParams(vmem_limit_bytes=12 * MIB),
        cost_estimate=pl.CostEstimate(
            flops=0, bytes_accessed=4 * shape[0] * shape[1] * received[0].shape[-1], transcendentals=0
        ),
        name="assemble",
    )(place, *received, *before)


def tied(first, second):
    return lax.optimization_barrier((first, second))


def per_device(sizes, global_weights, momentum, first_moment, second_moment, hidden_bank, target_bank, token_ids):
    reps, shards = sizes
    bits = reps.bit_length() - 1
    depth, columns = global_weights.shape
    rows = depth // reps
    store = hidden_bank.shape[1] * shards
    half = store // 2
    ids = token_ids[0]
    tokens = ids.shape[1]
    width = min(columns, LANES)
    chunks = columns // width
    mine = lax.axis_index("rep")

    def swapped(array, bit):
        pairs = [(index, index ^ (1 << bit)) for index in range(reps)]
        return lax.ppermute(array, "rep", pairs)

    own_bank = hidden_bank[0]
    target = target_bank[0]
    count = jnp.sum(
        ids[:, :, None] == jnp.arange(store, dtype=ids.dtype)[None, None, :], axis=1
    ).astype(F32)
    if shards == 2:
        block = depth // SLABS
        parts = []
        source = own_bank
        for d in range(SLABS):
            part, source = tied(source[:, d * block : (d + 1) * block], source)
            parts.append(lax.ppermute(part, "fsdp", [(0, 1), (1, 0)]))
        own_turned, own_product = forward(own_bank, global_weights)
        joined = ()
        for d, part in enumerate(parts):
            joined = arrive(d, part, global_weights, joined)
        banks = (own_bank, joined[0])
        turned = (own_turned, joined[1])
        products = (own_product, joined[2])
        swap = lax.axis_index("fsdp") == 1
        target = jnp.where(swap, jnp.roll(target, half, axis=0), target)
        count = jnp.where(swap, jnp.roll(count, half, axis=1), count)
    else:
        whole = lax.all_gather(own_bank, "fsdp", axis=0, tiled=True)
        banks = (whole[:half], whole[half:])
        turned, products = zip(*(forward(bank, global_weights) for bank in banks))
    count = count[:, :, None]

    cut = (SLABS, reps // (2 * SLABS), 2, rows, columns)
    turned = [array.reshape(cut[:4] + (half,)) for array in turned]
    start = global_weights.reshape(cut)
    first = first_moment.reshape(cut)
    second = second_moment.reshape(cut)
    place = mine.reshape(1).astype(jnp.int32)
    my_start = lax.dynamic_slice_in_dim(global_weights, mine * rows, rows, 0)
    shares = [
        tied(momentum[:, begin : begin + width], my_start[:, begin : begin + width])
        for begin in range(0, columns, width)
    ]

    def halved(terms):
        middle = terms[0].shape[0] // 2
        outgoing = sum(term[middle:].astype(F32) for term in terms).astype(WIRE)
        return outgoing, [term[:middle] for term in terms]

    new_momentum = []
    result = ()

    live = {}
    token = place
    for chunk in range(chunks):
        send, keep = inner(
            chunk, width, token, banks, turned, start, first, second, products, target, count, tokens
        )
        send = send.astype(WIRE)
        moving = {}
        for earlier in range(max(chunk - bits + 2, 0), chunk):
            outgoing, terms = halved(live[earlier])
            outgoing, send = tied(outgoing, send)
            moving[earlier] = (outgoing, terms)
        outgoing, terms = halved([keep, swapped(send, 0)])
        moving[chunk] = (outgoing, terms)
        if chunk + 1 < chunks:
            formed, token = tied([outgoing for outgoing, _ in moving.values()], token)
            moving = {
                which: (outgoing, terms)
                for (which, (_, terms)), outgoing in zip(moving.items(), formed)
            }
        for which, (outgoing, terms) in moving.items():
            live[which] = terms + [swapped(outgoing, chunk - which + 1)]

    for chunk in range(chunks):
        terms = live[chunk]
        for bit in range(min(chunks - chunk + 1, bits), bits):
            outgoing, terms = halved(terms)
            terms = terms + [swapped(outgoing, bit)]
        total = sum(term.astype(F32) for term in terms)[0]

        average = total * (1.0 / (WIRE_SCALE * reps))
        moved = 0.9 * shares[chunk][0] + average
        new_momentum.append(moved)
        fresh = (shares[chunk][1].astype(F32) - 0.7 * (average + 0.9 * moved)).astype(BF16)

        stack = fresh[None]
        offsets = [0]
        for bit in range(bits - 1, 1, -1):
            stack = jnp.concatenate([stack, swapped(stack, bit)])
            offsets = offsets + [offset ^ (1 << bit) for offset in offsets]
        across = swapped(stack, 1)
        if result:
            across, *result = tied(across, result[0])
        received = [stack, across, swapped(stack, 0), swapped(across, 0)]
        offsets = [[offset ^ low for offset in offsets] for low in (0, 2, 1, 3)]
        result = (
            assemble(chunk, place, received, offsets, (reps, rows, columns), result),
        )

    return result[0].reshape(depth, columns), jnp.concatenate(new_momentum, axis=1)


def solution(mesh):
    sizes = (mesh.shape["rep"], mesh.shape["fsdp"])
    return jax.shard_map(
        functools.partial(per_device, sizes),
        mesh=mesh,
        in_specs=(
            P(None, "fsdp"),
            P("rep", "fsdp"),
            P("rep", None, "fsdp"),
            P("rep", None, "fsdp"),
            P("rep", "fsdp", None),
            P("rep", None, "fsdp"),
            P("rep", None, None),
        ),
        out_specs=(P(None, "fsdp"), P("rep", "fsdp")),
        check_vma=False,
    )
```

```python
import functools
import math
import jax
import jax.numpy as jnp
from jax import lax
from jax.experimental import pallas as pl
from jax.experimental.pallas import tpu as pltpu
from jax.sharding import PartitionSpec as P

F32 = jnp.float32
BF16 = jnp.bfloat16
WIRE = jnp.float16
WIRE_SCALE = 64.0
LANES = 128
SLABS = 4
PIECE = 64
MIB = 1024 * 1024


def forward_kernel(part_ref, weights_ref, turned_ref, product_ref):
    @pl.when(pl.program_id(0) == 0)
    def _():
        product_ref[...] = jnp.zeros_like(product_ref)

    part = part_ref[...]
    turned_ref[...] = part.T
    product_ref[...] += jnp.dot(part, weights_ref[...], preferred_element_type=F32)


def forward(part, weights):
    rows, depth = part.shape
    columns = weights.shape[1]
    block = depth // SLABS
    return pl.pallas_call(
        forward_kernel,
        grid=(SLABS,),
        in_specs=[
            pl.BlockSpec((rows, block), lambda d: (0, d)),
            pl.BlockSpec((block, columns), lambda d: (d, 0)),
        ],
        out_specs=[
            pl.BlockSpec((block, rows), lambda d: (d, 0)),
            pl.BlockSpec((rows, columns), lambda d: (0, 0)),
        ],
        out_shape=[
            jax.ShapeDtypeStruct((depth, rows), BF16),
            jax.ShapeDtypeStruct((rows, columns), F32),
        ],
        compiler_params=pltpu.CompilerParams(vmem_limit_bytes=14 * MIB),
        cost_estimate=pl.CostEstimate(
            flops=2 * rows * depth * columns,
            bytes_accessed=2 * depth * columns + 4 * rows * depth,
            transcendentals=0,
        ),
        name="forward",
    )(part, pinned(weights))


def arrive_kernel(piece, part_ref, weights_ref, *refs):
    natural_ref, turned_ref, product_ref = refs[-3:]
    block = part_ref.shape[1]
    place = pl.ds(piece * block, block)
    part = part_ref[...]
    natural_ref[:, place] = part
    turned_ref[place, :] = part.T
    product = jnp.dot(part, weights_ref[...], preferred_element_type=F32)
    if len(refs) > 3:
        product = product + refs[2][...]
    product_ref[...] = product


def arrive(piece, part, weights, before):
    rows, block = part.shape
    depth, columns = weights.shape
    whole = pl.BlockSpec(memory_space=pltpu.VMEM)
    return pl.pallas_call(
        functools.partial(arrive_kernel, piece),
        grid=(1,),
        in_specs=[whole, pl.BlockSpec((block, columns), lambda d: (piece, 0))]
        + [whole] * len(before),
        out_specs=[whole] * 3,
        out_shape=[
            jax.ShapeDtypeStruct((rows, depth), BF16),
            jax.ShapeDtypeStruct((depth, rows), BF16),
            jax.ShapeDtypeStruct((rows, columns), F32),
        ],
        input_output_aliases={2: 0, 3: 1, 4: 2} if before else {},
        compiler_params=pltpu.CompilerParams(vmem_limit_bytes=10 * MIB),
        cost_estimate=pl.CostEstimate(
            flops=2 * rows * block * columns,
            bytes_accessed=2 * block * columns + 6 * rows * block,
            transcendentals=0,
        ),
        name="arrive",
    )(part, pinned(weights), *before)


def pinned(array):
    return pltpu.with_memory_space_constraint(array, pltpu.HBM)


def changed_place(mine, slab, pair, pairs):
    offset = lax.bitwise_xor(slab * pairs + pair, mine // 2)
    bits = (SLABS * pairs).bit_length() - 1
    place = jnp.int32(0)
    for bit in range(bits):
        place = place * 2 + lax.rem(lax.shift_right_logical(offset, bit), 2)
    return place


def inner_kernel(
    tokens,
    mine_ref,
    low_ref,
    high_ref,
    low_turned_ref,
    high_turned_ref,
    start_ref,
    first_ref,
    second_ref,
    low_product_ref,
    high_product_ref,
    target_ref,
    count_ref,
    send_ref,
    keep_ref,
    first_state,
    second_state,
    weights_state,
    output_state,
    residual_state,
    gradient_state,
    rounded_state,
):
    step = pl.program_id(0)
    slab = pl.program_id(1)
    pairs, cores, rows, _ = start_ref.shape
    mine = mine_ref[0]
    core = lax.rem(mine, cores)
    pieces = [pl.ds(begin, PIECE) for begin in range(0, rows, PIECE)]

    def weigh(output, which):
        residual = ((output - target_ref[...].astype(F32)) / tokens).astype(BF16)
        residual_state[...] = (residual.astype(F32) * count_ref[which]).astype(BF16)

    def descend(first, second, weights):
        root = second * lax.rsqrt(second)
        below = (100.0 * math.sqrt(0.05)) * root + 1e-06
        return 0.99 * weights - first * lax.rsqrt(below * below)

    def gradient_of(pair, which, slot):
        turned = jnp.concatenate(
            [low_turned_ref[slab, pair, which], high_turned_ref[slab, pair, which]], axis=1
        )
        gradient_state[slot] = jnp.dot(
            turned, residual_state[...], preferred_element_type=F32
        )

    @pl.when((step == 0) & (slab == 0))
    def _():
        weigh(jnp.concatenate([low_product_ref[...], high_product_ref[...]], axis=0), 0)
        output_state[...] = jnp.zeros_like(output_state)

    @pl.when((step == 1) & (slab == 0))
    def _():
        weigh(output_state[...], 1)

    @pl.when(step == 0)
    def _():
        total = jnp.zeros(output_state.shape, F32)
        for pair in range(pairs):
            for which in range(cores):
                slot = pair * cores + which
                gradient_of(pair, which, slot)
                for piece in pieces:
                    gradient = gradient_state[slot, piece]
                    first = 9.0 * first_ref[pair, which, piece] + gradient
                    second = 19.0 * second_ref[pair, which, piece] + gradient * gradient
                    weights = descend(first, second, start_ref[pair, which, piece].astype(F32))
                    first_state[slab, pair, which, piece] = first
                    second_state[slab, pair, which, piece] = second
                    weights_state[slab, pair, which, piece] = weights
                    rounded_state[slot, piece] = weights.astype(BF16)
                begin = (slab * pairs * cores + slot) * rows
                place = pl.ds(pl.multiple_of(begin, rows), rows)
                picked = jnp.concatenate([low_ref[:, place], high_ref[:, place]], axis=0)
                total += jnp.dot(picked, rounded_state[slot], preferred_element_type=F32)
        output_state[...] += total

    @pl.when(step == 1)
    def _():
        for pair in range(pairs):
            place = changed_place(mine, slab, pair, pairs)
            for slot, which, out_ref in ((0, 1 - core, send_ref), (1, core, keep_ref)):
                slot = pair * cores + slot
                gradient_of(pair, which, slot)
                for piece in pieces:
                    gradient = gradient_state[slot, piece]
                    first = 0.9 * first_state[slab, pair, which, piece] + gradient
                    second = 0.95 * second_state[slab, pair, which, piece] + gradient * gradient
                    weights = descend(first, second, weights_state[slab, pair, which, piece])
                    change = start_ref[pair, which, piece].astype(F32) - weights
                    out_ref[place, piece] = change * WIRE_SCALE


def inner(chunk, width, mine, banks, turned, start, first, second, products, target, count, tokens):
    slabs, pairs, cores, rows, _ = start.shape
    half, depth = banks[0].shape

    def held(step, slab):
        return jnp.where(step == 0, slab, slabs - 1)

    whole = pl.BlockSpec(memory_space=pltpu.VMEM)
    tile = (None, pairs, cores, rows, width)
    state = pl.BlockSpec(tile, lambda s, z, c: (held(s, z), 0, 0, 0, chunk))
    product = pl.BlockSpec((half, width), lambda s, z, c: (0, chunk))
    elements = depth * width
    return pl.pallas_call(
        functools.partial(inner_kernel, float(tokens)),
        grid_spec=pltpu.PrefetchScalarGridSpec(
            num_scalar_prefetch=1,
            grid=(2, slabs),
            in_specs=[whole] * 4
            + [
                pl.BlockSpec(tile, lambda s, z, c: (z, 0, 0, 0, chunk)),
                state,
                state,
                product,
                product,
                pl.BlockSpec((2 * half, width), lambda s, z, c: (0, chunk)),
                pl.BlockSpec(count.shape, lambda s, z, c: (0, 0, 0)),
            ],
            out_specs=[whole, whole],
            scratch_shapes=[
                pltpu.VMEM((slabs, pairs, cores, rows, width), F32),
                pltpu.VMEM((slabs, pairs, cores, rows, width), F32),
                pltpu.VMEM((slabs, pairs, cores, rows, width), F32),
                pltpu.VMEM((2 * half, width), F32),
                pltpu.VMEM((2 * half, width), BF16),
                pltpu.VMEM((pairs * cores, rows, width), F32),
                pltpu.VMEM((pairs * cores, rows, width), BF16),
            ],
        ),
        out_shape=[
            jax.ShapeDtypeStruct((slabs * pairs, rows, width), F32),
            jax.ShapeDtypeStruct((slabs * pairs, rows, width), F32),
        ],
        compiler_params=pltpu.CompilerParams(vmem_limit_bytes=22 * MIB),
        cost_estimate=pl.CostEstimate(
            flops=12 * half * elements,
            bytes_accessed=20 * elements,
            transcendentals=4 * elements,
        ),
        name="inner",
    )(mine, *banks, *turned, pinned(start), pinned(first), pinned(second), *products, target, count)


def assemble_kernel(chunk, offsets, place_ref, *refs):
    received = refs[: len(offsets)]
    out_ref, semaphore = refs[-2:]
    width = received[0].shape[-1]
    mine = place_ref[0]
    copies = []
    for ref, group in zip(received, offsets):
        for entry, offset in enumerate(group):
            copies.append(
                pltpu.make_async_copy(
                    ref.at[entry],
                    out_ref.at[lax.bitwise_xor(mine, offset), :, pl.ds(chunk * width, width)],
                    semaphore.at[len(copies)],
                )
            )
    for copy in copies:
        copy.start()
    for copy in copies:
        copy.wait()


def assemble(chunk, place, received, offsets, shape, before):
    vmem = pl.BlockSpec(memory_space=pltpu.VMEM)
    return pl.pallas_call(
        functools.partial(assemble_kernel, chunk, offsets),
        in_specs=[pl.BlockSpec(memory_space=pltpu.SMEM)]
        + [vmem] * len(received)
        + [pl.BlockSpec(memory_space=pl.ANY)] * len(before),
        out_specs=pl.BlockSpec(memory_space=pl.ANY),
        out_shape=jax.ShapeDtypeStruct(shape, BF16),
        input_output_aliases={1 + len(received): 0} if before else {},
        scratch_shapes=[pltpu.SemaphoreType.DMA((sum(map(len, offsets)),))],
        compiler_params=pltpu.CompilerParams(vmem_limit_bytes=12 * MIB),
        cost_estimate=pl.CostEstimate(
            flops=0, bytes_accessed=4 * shape[0] * shape[1] * received[0].shape[-1], transcendentals=0
        ),
        name="assemble",
    )(place, *received, *before)


def tied(first, second):
    return lax.optimization_barrier((first, second))


def per_device(sizes, global_weights, momentum, first_moment, second_moment, hidden_bank, target_bank, token_ids):
    reps, shards = sizes
    bits = reps.bit_length() - 1
    depth, columns = global_weights.shape
    rows = depth // reps
    store = hidden_bank.shape[1] * shards
    half = store // 2
    ids = token_ids[0]
    tokens = ids.shape[1]
    width = min(columns, LANES)
    chunks = columns // width
    mine = lax.axis_index("rep")

    def swapped(array, bit):
        pairs = [(index, index ^ (1 << bit)) for index in range(reps)]
        return lax.ppermute(array, "rep", pairs)

    own_bank = hidden_bank[0]
    target = target_bank[0]
    count = jnp.sum(
        ids[:, :, None] == jnp.arange(store, dtype=ids.dtype)[None, None, :], axis=1
    ).astype(F32)
    if shards == 2:
        block = depth // SLABS
        parts = []
        source = own_bank
        for d in range(SLABS):
            part, source = tied(source[:, d * block : (d + 1) * block], source)
            parts.append(lax.ppermute(part, "fsdp", [(0, 1), (1, 0)]))
        own_turned, own_product = forward(own_bank, global_weights)
        joined = ()
        for d, part in enumerate(parts):
            joined = arrive(d, part, global_weights, joined)
        banks = (own_bank, joined[0])
        turned = (own_turned, joined[1])
        products = (own_product, joined[2])
        swap = lax.axis_index("fsdp") == 1
        target = jnp.where(swap, jnp.roll(target, half, axis=0), target)
        count = jnp.where(swap, jnp.roll(count, half, axis=1), count)
    else:
        whole = lax.all_gather(own_bank, "fsdp", axis=0, tiled=True)
        banks = (whole[:half], whole[half:])
        turned, products = zip(*(forward(bank, global_weights) for bank in banks))
    count = count[:, :, None]

    cut = (SLABS, reps // (2 * SLABS), 2, rows, columns)
    turned = [array.reshape(cut[:4] + (half,)) for array in turned]
    start = global_weights.reshape(cut)
    first = first_moment.reshape(cut)
    second = second_moment.reshape(cut)
    place = mine.reshape(1).astype(jnp.int32)
    my_start = lax.dynamic_slice_in_dim(global_weights, mine * rows, rows, 0)
    shares = [
        tied(momentum[:, begin : begin + width], my_start[:, begin : begin + width])
        for begin in range(0, columns, width)
    ]

    def halved(terms):
        middle = terms[0].shape[0] // 2
        outgoing = sum(term[middle:].astype(F32) for term in terms).astype(WIRE)
        return outgoing, [term[:middle] for term in terms]

    new_momentum = []
    result = ()

    live = {}
    token = place
    for chunk in range(chunks):
        send, keep = inner(
            chunk, width, token, banks, turned, start, first, second, products, target, count, tokens
        )
        send = send.astype(WIRE)
        last = chunk + 1 == chunks
        moving = {}
        for earlier in range(max(chunk - bits + 2, 0), chunk):
            outgoing, terms = halved(live[earlier])
            outgoing, send = tied(outgoing, send)
            moving[earlier] = (outgoing, terms)
        moving[chunk] = halved([keep, swapped(send, 0)])
        if not last:
            formed, token = tied([outgoing for outgoing, _ in moving.values()], token)
            for (which, (_, terms)), outgoing in zip(moving.items(), formed):
                live[which] = terms + [swapped(outgoing, chunk - which + 1)]
            continue
        head, terms = moving.pop(chunk)
        live[chunk] = terms + [swapped(head, 1)]
        for which, (outgoing, terms) in moving.items():
            live[which] = terms + [swapped(outgoing, chunk - which + 1)]
        for which in range(chunk):
            live[which][-1], _ = tied(live[which][-1], head)

    for chunk in range(chunks):
        terms = live[chunk]
        for bit in range(min(chunks - chunk + 1, bits), bits):
            outgoing, terms = halved(terms)
            terms = terms + [swapped(outgoing, bit)]
        total = sum(term.astype(F32) for term in terms)[0]
        average = total * (1.0 / (WIRE_SCALE * reps))
        moved = 0.9 * shares[chunk][0] + average
        fresh = (shares[chunk][1].astype(F32) - 0.7 * (average + 0.9 * moved)).astype(BF16)
        new_momentum.append(moved)
        stack = fresh[None]
        offsets = [0]
        for bit in range(bits - 1, 1, -1):
            stack = jnp.concatenate([stack, swapped(stack, bit)])
            offsets = offsets + [offset ^ (1 << bit) for offset in offsets]
        across = swapped(stack, 1)
        offsets = [[offset ^ low for offset in offsets] for low in (0, 2, 1, 3)]
        if result:
            across, *result = tied(across, result[0])
        received = [stack, across, swapped(stack, 0), swapped(across, 0)]
        result = (
            assemble(chunk, place, received, offsets, (reps, rows, columns), result),
        )

    return result[0].reshape(depth, columns), jnp.concatenate(new_momentum, axis=1)


def solution(mesh):
    sizes = (mesh.shape["rep"], mesh.shape["fsdp"])
    return jax.shard_map(
        functools.partial(per_device, sizes),
        mesh=mesh,
        in_specs=(
            P(None, "fsdp"),
            P("rep", "fsdp"),
            P("rep", None, "fsdp"),
            P("rep", None, "fsdp"),
            P("rep", "fsdp", None),
            P("rep", None, "fsdp"),
            P("rep", None, None),
        ),
        out_specs=(P(None, "fsdp"), P("rep", "fsdp")),
        check_vma=False,
    )
```

```python
import functools
import math
import jax
import jax.numpy as jnp
from jax import lax
from jax.experimental import pallas as pl
from jax.experimental.pallas import tpu as pltpu
from jax.sharding import PartitionSpec as P

F32 = jnp.float32
BF16 = jnp.bfloat16
WIRE = jnp.float16
WIRE_SCALE = 64.0
LANES = 128
SLABS = 4
PIECE = 64
MIB = 1024 * 1024


def forward_kernel(part_ref, weights_ref, turned_ref, product_ref):
    @pl.when(pl.program_id(0) == 0)
    def _():
        product_ref[...] = jnp.zeros_like(product_ref)

    part = part_ref[...]
    turned_ref[...] = part.T
    product_ref[...] += jnp.dot(part, weights_ref[...], preferred_element_type=F32)


def forward(part, weights):
    rows, depth = part.shape
    columns = weights.shape[1]
    block = depth // SLABS
    return pl.pallas_call(
        forward_kernel,
        grid=(SLABS,),
        in_specs=[
            pl.BlockSpec((rows, block), lambda d: (0, d)),
            pl.BlockSpec((block, columns), lambda d: (d, 0)),
        ],
        out_specs=[
            pl.BlockSpec((block, rows), lambda d: (d, 0)),
            pl.BlockSpec((rows, columns), lambda d: (0, 0)),
        ],
        out_shape=[
            jax.ShapeDtypeStruct((depth, rows), BF16),
            jax.ShapeDtypeStruct((rows, columns), F32),
        ],
        compiler_params=pltpu.CompilerParams(vmem_limit_bytes=14 * MIB),
        cost_estimate=pl.CostEstimate(
            flops=2 * rows * depth * columns,
            bytes_accessed=2 * depth * columns + 4 * rows * depth,
            transcendentals=0,
        ),
        name="forward",
    )(part, pinned(weights))


def arrive_kernel(piece, part_ref, weights_ref, *refs):
    natural_ref, turned_ref, product_ref = refs[-3:]
    block = part_ref.shape[1]
    place = pl.ds(piece * block, block)
    part = part_ref[...]
    natural_ref[:, place] = part
    turned_ref[place, :] = part.T
    product = jnp.dot(part, weights_ref[...], preferred_element_type=F32)
    if len(refs) > 3:
        product = product + refs[2][...]
    product_ref[...] = product


def arrive(piece, part, weights, before):
    rows, block = part.shape
    depth, columns = weights.shape
    whole = pl.BlockSpec(memory_space=pltpu.VMEM)
    return pl.pallas_call(
        functools.partial(arrive_kernel, piece),
        grid=(1,),
        in_specs=[whole, pl.BlockSpec((block, columns), lambda d: (piece, 0))]
        + [whole] * len(before),
        out_specs=[whole] * 3,
        out_shape=[
            jax.ShapeDtypeStruct((rows, depth), BF16),
            jax.ShapeDtypeStruct((depth, rows), BF16),
            jax.ShapeDtypeStruct((rows, columns), F32),
        ],
        input_output_aliases={2: 0, 3: 1, 4: 2} if before else {},
        compiler_params=pltpu.CompilerParams(vmem_limit_bytes=10 * MIB),
        cost_estimate=pl.CostEstimate(
            flops=2 * rows * block * columns,
            bytes_accessed=2 * block * columns + 6 * rows * block,
            transcendentals=0,
        ),
        name="arrive",
    )(part, pinned(weights), *before)


def pinned(array):
    return pltpu.with_memory_space_constraint(array, pltpu.HBM)


def changed_place(mine, slab, pair, pairs):
    offset = lax.bitwise_xor(slab * pairs + pair, mine // 2)
    bits = (SLABS * pairs).bit_length() - 1
    place = jnp.int32(0)
    for bit in range(bits):
        place = place * 2 + lax.rem(lax.shift_right_logical(offset, bit), 2)
    return place


def inner_kernel(
    tokens,
    mine_ref,
    low_ref,
    high_ref,
    low_turned_ref,
    high_turned_ref,
    start_ref,
    first_ref,
    second_ref,
    low_product_ref,
    high_product_ref,
    target_ref,
    count_ref,
    send_ref,
    keep_ref,
    first_state,
    second_state,
    weights_state,
    output_state,
    residual_state,
    gradient_state,
    rounded_state,
):
    step = pl.program_id(0)
    slab = pl.program_id(1)
    pairs, cores, rows, _ = start_ref.shape
    mine = mine_ref[0]
    core = lax.rem(mine, cores)
    pieces = [pl.ds(begin, PIECE) for begin in range(0, rows, PIECE)]

    def weigh(output, which):
        residual = ((output - target_ref[...].astype(F32)) / tokens).astype(BF16)
        residual_state[...] = (residual.astype(F32) * count_ref[which]).astype(BF16)

    def descend(first, second, weights):
        root = second * lax.rsqrt(second)
        below = (100.0 * math.sqrt(0.05)) * root + 1e-06
        return 0.99 * weights - first * lax.rsqrt(below * below)

    def differentiate(pair, which, slot):
        turned = jnp.concatenate(
            [low_turned_ref[slab, pair, which], high_turned_ref[slab, pair, which]], axis=1
        )
        gradient_state[slot] = jnp.dot(
            turned, residual_state[...], preferred_element_type=F32
        )

    def project(slot):
        begin = (slab * pairs * cores + slot) * rows
        place = pl.ds(pl.multiple_of(begin, rows), rows)
        picked = jnp.concatenate([low_ref[:, place], high_ref[:, place]], axis=0)
        return jnp.dot(picked, rounded_state[slot], preferred_element_type=F32)

    @pl.when((step == 0) & (slab == 0))
    def _():
        weigh(jnp.concatenate([low_product_ref[...], high_product_ref[...]], axis=0), 0)
        output_state[...] = jnp.zeros_like(output_state)

    @pl.when((step == 1) & (slab == 0))
    def _():
        weigh(output_state[...], 1)

    slots = [(slot, *divmod(slot, cores)) for slot in range(pairs * cores)]

    @pl.when(step == 0)
    def _():
        total = jnp.zeros(output_state.shape, F32)
        differentiate(0, 0, 0)
        for slot, pair, which in slots:
            if slot + 1 < len(slots):
                ahead, *place = slots[slot + 1]
                differentiate(*place, ahead)
            for piece in pieces:
                gradient = gradient_state[slot, piece]
                first = 9.0 * first_ref[pair, which, piece] + gradient
                second = 19.0 * second_ref[pair, which, piece] + gradient * gradient
                weights = descend(first, second, start_ref[pair, which, piece].astype(F32))
                first_state[slab, pair, which, piece] = first
                second_state[slab, pair, which, piece] = second
                weights_state[slab, pair, which, piece] = weights
                rounded_state[slot, piece] = weights.astype(BF16)
            if slot:
                total += project(slot - 1)
        output_state[...] += total + project(len(slots) - 1)

    @pl.when(step == 1)
    def _():
        sides = ((1 - core, send_ref), (core, keep_ref))
        differentiate(0, sides[0][0], 0)
        for slot, pair, side in slots:
            if slot + 1 < len(slots):
                ahead, next_pair, next_side = slots[slot + 1]
                differentiate(next_pair, sides[next_side][0], ahead)
            which, out_ref = sides[side]
            place = changed_place(mine, slab, pair, pairs)
            for piece in pieces:
                gradient = gradient_state[slot, piece]
                first = 0.9 * first_state[slab, pair, which, piece] + gradient
                second = 0.95 * second_state[slab, pair, which, piece] + gradient * gradient
                weights = descend(first, second, weights_state[slab, pair, which, piece])
                change = start_ref[pair, which, piece].astype(F32) - weights
                out_ref[place, piece] = change * WIRE_SCALE


def inner(chunk, width, mine, banks, turned, start, first, second, products, target, count, tokens):
    slabs, pairs, cores, rows, _ = start.shape
    half, depth = banks[0].shape

    def held(step, slab):
        return jnp.where(step == 0, slab, slabs - 1)

    whole = pl.BlockSpec(memory_space=pltpu.VMEM)
    tile = (None, pairs, cores, rows, width)
    state = pl.BlockSpec(tile, lambda s, z, c: (held(s, z), 0, 0, 0, chunk))
    product = pl.BlockSpec((half, width), lambda s, z, c: (0, chunk))
    elements = depth * width
    return pl.pallas_call(
        functools.partial(inner_kernel, float(tokens)),
        grid_spec=pltpu.PrefetchScalarGridSpec(
            num_scalar_prefetch=1,
            grid=(2, slabs),
            in_specs=[whole] * 4
            + [
                pl.BlockSpec(tile, lambda s, z, c: (z, 0, 0, 0, chunk)),
                state,
                state,
                product,
                product,
                pl.BlockSpec((2 * half, width), lambda s, z, c: (0, chunk)),
                pl.BlockSpec(count.shape, lambda s, z, c: (0, 0, 0)),
            ],
            out_specs=[whole, whole],
            scratch_shapes=[
                pltpu.VMEM((slabs, pairs, cores, rows, width), F32),
                pltpu.VMEM((slabs, pairs, cores, rows, width), F32),
                pltpu.VMEM((slabs, pairs, cores, rows, width), F32),
                pltpu.VMEM((2 * half, width), F32),
                pltpu.VMEM((2 * half, width), BF16),
                pltpu.VMEM((pairs * cores, rows, width), F32),
                pltpu.VMEM((pairs * cores, rows, width), BF16),
            ],
        ),
        out_shape=[
            jax.ShapeDtypeStruct((slabs * pairs, rows, width), F32),
            jax.ShapeDtypeStruct((slabs * pairs, rows, width), F32),
        ],
        compiler_params=pltpu.CompilerParams(vmem_limit_bytes=22 * MIB),
        cost_estimate=pl.CostEstimate(
            flops=12 * half * elements,
            bytes_accessed=20 * elements,
            transcendentals=4 * elements,
        ),
        name="inner",
    )(mine, *banks, *turned, pinned(start), pinned(first), pinned(second), *products, target, count)


def assemble_kernel(chunk, offsets, place_ref, *refs):
    received = refs[: len(offsets)]
    out_ref, semaphore = refs[-2:]
    width = received[0].shape[-1]
    mine = place_ref[0]
    copies = []
    for ref, group in zip(received, offsets):
        for entry, offset in enumerate(group):
            copies.append(
                pltpu.make_async_copy(
                    ref.at[entry],
                    out_ref.at[lax.bitwise_xor(mine, offset), :, pl.ds(chunk * width, width)],
                    semaphore.at[len(copies)],
                )
            )
    for copy in copies:
        copy.start()
    for copy in copies:
        copy.wait()


def assemble(chunk, place, received, offsets, shape, before):
    vmem = pl.BlockSpec(memory_space=pltpu.VMEM)
    return pl.pallas_call(
        functools.partial(assemble_kernel, chunk, offsets),
        in_specs=[pl.BlockSpec(memory_space=pltpu.SMEM)]
        + [vmem] * len(received)
        + [pl.BlockSpec(memory_space=pl.ANY)] * len(before),
        out_specs=pl.BlockSpec(memory_space=pl.ANY),
        out_shape=jax.ShapeDtypeStruct(shape, BF16),
        input_output_aliases={1 + len(received): 0} if before else {},
        scratch_shapes=[pltpu.SemaphoreType.DMA((sum(map(len, offsets)),))],
        compiler_params=pltpu.CompilerParams(vmem_limit_bytes=12 * MIB),
        cost_estimate=pl.CostEstimate(
            flops=0, bytes_accessed=4 * shape[0] * shape[1] * received[0].shape[-1], transcendentals=0
        ),
        name="assemble",
    )(place, *received, *before)


def tied(first, second):
    return lax.optimization_barrier((first, second))


def per_device(sizes, global_weights, momentum, first_moment, second_moment, hidden_bank, target_bank, token_ids):
    reps, shards = sizes
    bits = reps.bit_length() - 1
    depth, columns = global_weights.shape
    rows = depth // reps
    store = hidden_bank.shape[1] * shards
    half = store // 2
    ids = token_ids[0]
    tokens = ids.shape[1]
    width = min(columns, LANES)
    chunks = columns // width
    mine = lax.axis_index("rep")

    def swapped(array, offset):
        pairs = [(index, index ^ offset) for index in range(reps)]
        return lax.ppermute(array, "rep", pairs)

    spans = [[0, 1 << bit] for bit in range(1, bits)]

    own_bank = hidden_bank[0]
    target = target_bank[0]
    count = jnp.sum(
        ids[:, :, None] == jnp.arange(store, dtype=ids.dtype)[None, None, :], axis=1
    ).astype(F32)
    if shards == 2:
        block = depth // SLABS
        parts = []
        source = own_bank
        for d in range(SLABS):
            part, source = tied(source[:, d * block : (d + 1) * block], source)
            parts.append(lax.ppermute(part, "fsdp", [(0, 1), (1, 0)]))
        own_turned, own_product = forward(own_bank, global_weights)
        joined = ()
        for d, part in enumerate(parts):
            joined = arrive(d, part, global_weights, joined)
        banks = (own_bank, joined[0])
        turned = (own_turned, joined[1])
        products = (own_product, joined[2])
        swap = lax.axis_index("fsdp") == 1
        target = jnp.where(swap, jnp.roll(target, half, axis=0), target)
        count = jnp.where(swap, jnp.roll(count, half, axis=1), count)
    else:
        whole = lax.all_gather(own_bank, "fsdp", axis=0, tiled=True)
        banks = (whole[:half], whole[half:])
        turned, products = zip(*(forward(bank, global_weights) for bank in banks))
    count = count[:, :, None]

    cut = (SLABS, reps // (2 * SLABS), 2, rows, columns)
    turned = [array.reshape(cut[:4] + (half,)) for array in turned]
    start = global_weights.reshape(cut)
    first = first_moment.reshape(cut)
    second = second_moment.reshape(cut)
    place = mine.reshape(1).astype(jnp.int32)
    my_start = lax.dynamic_slice_in_dim(global_weights, mine * rows, rows, 0)
    shares = [
        tied(momentum[:, begin : begin + width], my_start[:, begin : begin + width])
        for begin in range(0, columns, width)
    ]

    def parted(terms, span):
        size = terms[0].shape[0] // len(span)
        parts = [[term[begin : begin + size] for term in terms] for begin in range(0, size * len(span), size)]
        outgoing = [sum(term.astype(F32) for term in part).astype(WIRE) for part in parts[1:]]
        return outgoing, parts[0]

    def sent(outgoing, span):
        return [swapped(array, offset) for array, offset in zip(outgoing, span[1:])]

    new_momentum = []
    result = ()

    def chain(chunk, send, keep):
        send = yield send
        terms = [keep, swapped(send, 1)]
        for span in spans:
            outgoing, terms = parted(terms, span)
            outgoing = yield outgoing
            terms = terms + held_back(sent(outgoing, span))
        total = sum(term.astype(F32) for term in terms)[0]
        average = total * (1.0 / (WIRE_SCALE * reps))
        moved = 0.9 * shares[chunk][0] + average
        stack = (shares[chunk][1].astype(F32) - 0.7 * (average + 0.9 * moved)).astype(BF16)[None]
        offsets = [0]
        for span in spans[:0:-1]:
            stack = yield stack
            arrived = held_back(sent([stack] * (len(span) - 1), span))
            stack = jnp.concatenate([stack] + arrived)
            offsets = [offset ^ far for far in span for offset in offsets]
        stack = yield stack
        across = swapped(stack, 2)
        finished[chunk] = (moved, stack, across, offsets)

    finished = {}
    running = {}
    formed = {}
    gate = []

    def held_back(arrived):
        return tied(arrived, gate)[0] if gate else arrived

    def move_on(which, behind=()):
        gate[:] = [formed[other] for other in behind]
        try:
            formed[which] = running[which].send(formed[which])
        except StopIteration:
            del formed[which]

    token = place
    for chunk in range(chunks):
        send, keep = inner(
            chunk, width, token, banks, turned, start, first, second, products, target, count, tokens
        )
        send = send.astype(WIRE)
        for earlier in list(formed):
            move_on(earlier)
            formed[earlier], send = tied(formed[earlier], send)
        running[chunk] = chain(chunk, send, keep)
        formed[chunk] = running[chunk].send(next(running[chunk]))
        if chunk + 1 < chunks:
            formed, token = tied(formed, token)
    if chunks == 4:
        move_on(0, behind=[3])
        move_on(3, behind=[0])
        for which in (1, 2, 0):
            move_on(which, behind=[3])
    for which in range(chunks):
        while which in formed:
            move_on(which)

    for chunk in range(chunks):
        moved, stack, across, offsets = finished[chunk]
        new_momentum.append(moved)
        offsets = [[offset ^ low for offset in offsets] for low in (0, 2, 1, 3)]
        if result:
            across, *result = tied(across, result[0])
        received = [stack, across, swapped(stack, 1), swapped(across, 1)]
        result = (
            assemble(chunk, place, received, offsets, (reps, rows, columns), result),
        )

    return result[0].reshape(depth, columns), jnp.concatenate(new_momentum, axis=1)


def solution(mesh):
    sizes = (mesh.shape["rep"], mesh.shape["fsdp"])
    return jax.shard_map(
        functools.partial(per_device, sizes),
        mesh=mesh,
        in_specs=(
            P(None, "fsdp"),
            P("rep", "fsdp"),
            P("rep", None, "fsdp"),
            P("rep", None, "fsdp"),
            P("rep", "fsdp", None),
            P("rep", None, "fsdp"),
            P("rep", None, None),
        ),
        out_specs=(P(None, "fsdp"), P("rep", "fsdp")),
        check_vma=False,
    )
```

```python
import functools
import math
import jax
import jax.numpy as jnp
from jax import lax
from jax.experimental import pallas as pl
from jax.experimental.pallas import tpu as pltpu
from jax.sharding import PartitionSpec as P

F32 = jnp.float32
BF16 = jnp.bfloat16
WIRE = jnp.float16
WIRE_SCALE = 64.0
LANES = 128
SLABS = 4
PIECE = 64
MIB = 1024 * 1024


def forward_kernel(part_ref, weights_ref, turned_ref, product_ref):
    @pl.when(pl.program_id(0) == 0)
    def _():
        product_ref[...] = jnp.zeros_like(product_ref)

    part = part_ref[...]
    turned_ref[...] = part.T
    product_ref[...] += jnp.dot(part, weights_ref[...], preferred_element_type=F32)


def forward(part, weights):
    rows, depth = part.shape
    columns = weights.shape[1]
    block = depth // SLABS
    return pl.pallas_call(
        forward_kernel,
        grid=(SLABS,),
        in_specs=[
            pl.BlockSpec((rows, block), lambda d: (0, d)),
            pl.BlockSpec((block, columns), lambda d: (d, 0)),
        ],
        out_specs=[
            pl.BlockSpec((block, rows), lambda d: (d, 0)),
            pl.BlockSpec((rows, columns), lambda d: (0, 0)),
        ],
        out_shape=[
            jax.ShapeDtypeStruct((depth, rows), BF16),
            jax.ShapeDtypeStruct((rows, columns), F32),
        ],
        compiler_params=pltpu.CompilerParams(vmem_limit_bytes=14 * MIB),
        cost_estimate=pl.CostEstimate(
            flops=2 * rows * depth * columns,
            bytes_accessed=2 * depth * columns + 4 * rows * depth,
            transcendentals=0,
        ),
        name="forward",
    )(part, pinned(weights))


def arrive_kernel(piece, part_ref, weights_ref, *refs):
    natural_ref, turned_ref, product_ref = refs[-3:]
    block = part_ref.shape[1]
    place = pl.ds(piece * block, block)
    part = part_ref[...]
    natural_ref[:, place] = part
    turned_ref[place, :] = part.T
    product = jnp.dot(part, weights_ref[...], preferred_element_type=F32)
    if len(refs) > 3:
        product = product + refs[2][...]
    product_ref[...] = product


def arrive(piece, part, weights, before):
    rows, block = part.shape
    depth, columns = weights.shape
    whole = pl.BlockSpec(memory_space=pltpu.VMEM)
    return pl.pallas_call(
        functools.partial(arrive_kernel, piece),
        grid=(1,),
        in_specs=[whole, pl.BlockSpec((block, columns), lambda d: (piece, 0))]
        + [whole] * len(before),
        out_specs=[whole] * 3,
        out_shape=[
            jax.ShapeDtypeStruct((rows, depth), BF16),
            jax.ShapeDtypeStruct((depth, rows), BF16),
            jax.ShapeDtypeStruct((rows, columns), F32),
        ],
        input_output_aliases={2: 0, 3: 1, 4: 2} if before else {},
        compiler_params=pltpu.CompilerParams(vmem_limit_bytes=10 * MIB),
        cost_estimate=pl.CostEstimate(
            flops=2 * rows * block * columns,
            bytes_accessed=2 * block * columns + 6 * rows * block,
            transcendentals=0,
        ),
        name="arrive",
    )(part, pinned(weights), *before)


def pinned(array):
    return pltpu.with_memory_space_constraint(array, pltpu.HBM)


def changed_place(mine, slab, pair, pairs):
    offset = lax.bitwise_xor(slab * pairs + pair, mine // 2)
    bits = (SLABS * pairs).bit_length() - 1
    place = jnp.int32(0)
    for bit in range(bits):
        place = place * 2 + lax.rem(lax.shift_right_logical(offset, bit), 2)
    return place


def inner_kernel(
    tokens,
    mine_ref,
    low_ref,
    high_ref,
    low_turned_ref,
    high_turned_ref,
    start_ref,
    first_ref,
    second_ref,
    low_product_ref,
    high_product_ref,
    target_ref,
    count_ref,
    send_ref,
    keep_ref,
    first_state,
    second_state,
    weights_state,
    output_state,
    residual_state,
    gradient_state,
    rounded_state,
):
    step = pl.program_id(0)
    slab = pl.program_id(1)
    pairs, cores, rows, _ = start_ref.shape
    mine = mine_ref[0]
    core = lax.rem(mine, cores)
    pieces = [pl.ds(begin, PIECE) for begin in range(0, rows, PIECE)]

    def weigh(output, which):
        residual = ((output - target_ref[...].astype(F32)) / tokens).astype(BF16)
        residual_state[...] = (residual.astype(F32) * count_ref[which]).astype(BF16)

    def descend(first, second, weights):
        root = second * lax.rsqrt(second)
        below = (100.0 * math.sqrt(0.05)) * root + 1e-06
        return 0.99 * weights - first * lax.rsqrt(below * below)

    def differentiate(pair, which, slot):
        turned = jnp.concatenate(
            [low_turned_ref[slab, pair, which], high_turned_ref[slab, pair, which]], axis=1
        )
        gradient_state[slot] = jnp.dot(
            turned, residual_state[...], preferred_element_type=F32
        )

    def project(slot):
        begin = (slab * pairs * cores + slot) * rows
        place = pl.ds(pl.multiple_of(begin, rows), rows)
        picked = jnp.concatenate([low_ref[:, place], high_ref[:, place]], axis=0)
        return jnp.dot(picked, rounded_state[slot], preferred_element_type=F32)

    @pl.when((step == 0) & (slab == 0))
    def _():
        weigh(jnp.concatenate([low_product_ref[...], high_product_ref[...]], axis=0), 0)
        output_state[...] = jnp.zeros_like(output_state)

    @pl.when((step == 1) & (slab == 0))
    def _():
        weigh(output_state[...], 1)

    slots = [(slot, *divmod(slot, cores)) for slot in range(pairs * cores)]

    @pl.when(step == 0)
    def _():
        total = jnp.zeros(output_state.shape, F32)
        differentiate(0, 0, 0)
        for slot, pair, which in slots:
            if slot + 1 < len(slots):
                ahead, *place = slots[slot + 1]
                differentiate(*place, ahead)
            for piece in pieces:
                gradient = gradient_state[slot, piece]
                first = 9.0 * first_ref[pair, which, piece] + gradient
                second = 19.0 * second_ref[pair, which, piece] + gradient * gradient
                weights = descend(first, second, start_ref[pair, which, piece].astype(F32))
                first_state[slab, pair, which, piece] = first
                second_state[slab, pair, which, piece] = second
                weights_state[slab, pair, which, piece] = weights
                rounded_state[slot, piece] = weights.astype(BF16)
            if slot:
                total += project(slot - 1)
        output_state[...] += total + project(len(slots) - 1)

    @pl.when(step == 1)
    def _():
        sides = ((1 - core, send_ref), (core, keep_ref))
        differentiate(0, sides[0][0], 0)
        for slot, pair, side in slots:
            if slot + 1 < len(slots):
                ahead, next_pair, next_side = slots[slot + 1]
                differentiate(next_pair, sides[next_side][0], ahead)
            which, out_ref = sides[side]
            place = changed_place(mine, slab, pair, pairs)
            for piece in pieces:
                gradient = gradient_state[slot, piece]
                first = 0.9 * first_state[slab, pair, which, piece] + gradient
                second = 0.95 * second_state[slab, pair, which, piece] + gradient * gradient
                weights = descend(first, second, weights_state[slab, pair, which, piece])
                change = start_ref[pair, which, piece].astype(F32) - weights
                out_ref[place, piece] = change * WIRE_SCALE


def inner(chunk, width, mine, banks, turned, start, first, second, products, target, count, tokens):
    slabs, pairs, cores, rows, _ = start.shape
    half, depth = banks[0].shape

    def held(step, slab):
        return jnp.where(step == 0, slab, slabs - 1)

    whole = pl.BlockSpec(memory_space=pltpu.VMEM)
    tile = (None, pairs, cores, rows, width)
    state = pl.BlockSpec(tile, lambda s, z, c: (held(s, z), 0, 0, 0, chunk))
    product = pl.BlockSpec((half, width), lambda s, z, c: (0, chunk))
    elements = depth * width
    return pl.pallas_call(
        functools.partial(inner_kernel, float(tokens)),
        grid_spec=pltpu.PrefetchScalarGridSpec(
            num_scalar_prefetch=1,
            grid=(2, slabs),
            in_specs=[whole] * 4
            + [
                pl.BlockSpec(tile, lambda s, z, c: (z, 0, 0, 0, chunk)),
                state,
                state,
                product,
                product,
                pl.BlockSpec((2 * half, width), lambda s, z, c: (0, chunk)),
                pl.BlockSpec(count.shape, lambda s, z, c: (0, 0, 0)),
            ],
            out_specs=[whole, whole],
            scratch_shapes=[
                pltpu.VMEM((slabs, pairs, cores, rows, width), F32),
                pltpu.VMEM((slabs, pairs, cores, rows, width), F32),
                pltpu.VMEM((slabs, pairs, cores, rows, width), F32),
                pltpu.VMEM((2 * half, width), F32),
                pltpu.VMEM((2 * half, width), BF16),
                pltpu.VMEM((pairs * cores, rows, width), F32),
                pltpu.VMEM((pairs * cores, rows, width), BF16),
            ],
        ),
        out_shape=[
            jax.ShapeDtypeStruct((slabs * pairs, rows, width), F32),
            jax.ShapeDtypeStruct((slabs * pairs, rows, width), F32),
        ],
        compiler_params=pltpu.CompilerParams(vmem_limit_bytes=22 * MIB),
        cost_estimate=pl.CostEstimate(
            flops=12 * half * elements,
            bytes_accessed=20 * elements,
            transcendentals=4 * elements,
        ),
        name="inner",
    )(mine, *banks, *turned, pinned(start), pinned(first), pinned(second), *products, target, count)


def tied(first, second):
    return lax.optimization_barrier((first, second))


def per_device(sizes, global_weights, momentum, first_moment, second_moment, hidden_bank, target_bank, token_ids):
    reps, shards = sizes
    bits = reps.bit_length() - 1
    depth, columns = global_weights.shape
    rows = depth // reps
    store = hidden_bank.shape[1] * shards
    half = store // 2
    ids = token_ids[0]
    tokens = ids.shape[1]
    width = min(columns, LANES)
    chunks = columns // width
    mine = lax.axis_index("rep")

    def swapped(array, offset):
        pairs = [(index, index ^ offset) for index in range(reps)]
        return lax.ppermute(array, "rep", pairs)

    spans = [[0, 1 << bit] for bit in range(1, bits)]

    own_bank = hidden_bank[0]
    target = target_bank[0]
    count = jnp.sum(
        ids[:, :, None] == jnp.arange(store, dtype=ids.dtype)[None, None, :], axis=1
    ).astype(F32)
    if shards == 2:
        block = depth // SLABS
        parts = []
        source = own_bank
        for d in range(SLABS):
            part, source = tied(source[:, d * block : (d + 1) * block], source)
            parts.append(lax.ppermute(part, "fsdp", [(0, 1), (1, 0)]))
        own_turned, own_product = forward(own_bank, global_weights)
        joined = ()
        for d, part in enumerate(parts):
            joined = arrive(d, part, global_weights, joined)
        banks = (own_bank, joined[0])
        turned = (own_turned, joined[1])
        products = (own_product, joined[2])
        swap = lax.axis_index("fsdp") == 1
        target = jnp.where(swap, jnp.roll(target, half, axis=0), target)
        count = jnp.where(swap, jnp.roll(count, half, axis=1), count)
    else:
        whole = lax.all_gather(own_bank, "fsdp", axis=0, tiled=True)
        banks = (whole[:half], whole[half:])
        turned, products = zip(*(forward(bank, global_weights) for bank in banks))
    count = count[:, :, None]

    cut = (SLABS, reps // (2 * SLABS), 2, rows, columns)
    turned = [array.reshape(cut[:4] + (half,)) for array in turned]
    start = global_weights.reshape(cut)
    first = first_moment.reshape(cut)
    second = second_moment.reshape(cut)
    place = mine.reshape(1).astype(jnp.int32)
    my_start = lax.dynamic_slice_in_dim(global_weights, mine * rows, rows, 0)
    shares = [
        tied(momentum[:, begin : begin + width], my_start[:, begin : begin + width])
        for begin in range(0, columns, width)
    ]

    def parted(terms, span):
        size = terms[0].shape[0] // len(span)
        parts = [[term[begin : begin + size] for term in terms] for begin in range(0, size * len(span), size)]
        outgoing = [sum(term.astype(F32) for term in part).astype(WIRE) for part in parts[1:]]
        return outgoing, parts[0]

    def sent(outgoing, span):
        return [swapped(array, offset) for array, offset in zip(outgoing, span[1:])]

    result = ()

    def chain(chunk, keep, arrived):
        terms = [keep, arrived]
        for span in spans:
            outgoing, terms = parted(terms, span)
            outgoing = yield outgoing
            arrived = yield sent(outgoing, span)
            terms = terms + arrived
        total = sum(term.astype(F32) for term in terms)[0]
        average = total * (1.0 / (WIRE_SCALE * reps))
        moved = 0.9 * shares[chunk][0] + average
        fresh = (shares[chunk][1].astype(F32) - 0.7 * (average + 0.9 * moved)).astype(BF16)
        finished[chunk] = (moved, fresh)
        yield fresh

    finished = {}
    running = {}
    formed = {}

    def move_on(which, behind=()):
        which = [chunk for chunk in which if chunk not in finished]
        arrived = {chunk: running[chunk].send(formed[chunk]) for chunk in which}
        arrived, _ = tied(arrived, [formed[chunk] for chunk in behind])
        for chunk in which:
            formed[chunk] = running[chunk].send(arrived[chunk])

    token = place
    for chunk in range(chunks):
        send, keep = inner(
            chunk, width, token, banks, turned, start, first, second, products, target, count, tokens
        )
        send = send.astype(WIRE)
        if chunk:
            move_on(range(chunk))
            formed, send = tied(formed, send)
        running[chunk] = chain(chunk, keep, swapped(send, 1))
        formed[chunk] = next(running[chunk])
        if chunk + 1 < chunks:
            formed, token = tied(formed, token)

    head = chunks - 1
    move_on(range(head), behind=[head])
    while head not in finished:
        move_on(range(chunks))

    group = max(chunks // 2, 1)
    for begin in range(0, chunks, group):
        fresh = jnp.concatenate([finished[chunk][1] for chunk in range(begin, begin + group)], axis=1)
        gathered = lax.all_gather(fresh, "rep", axis=0, tiled=True)
        result = (join(begin // group, columns, gathered, result),)
    new_momentum = [finished[chunk][0] for chunk in range(chunks)]

    return result[0], jnp.concatenate(new_momentum, axis=1)


def join_kernel(part_ref, *refs):
    refs[-1][...] = part_ref[...]


def join(place, columns, part, before):
    depth, width = part.shape
    block = depth // 8
    return pl.pallas_call(
        join_kernel,
        grid=(depth // block,),
        in_specs=[pl.BlockSpec((block, width), lambda d: (d, 0))]
        + [pl.BlockSpec(memory_space=pl.ANY)] * len(before),
        out_specs=pl.BlockSpec((block, width), lambda d: (d, place)),
        out_shape=jax.ShapeDtypeStruct((depth, columns), BF16),
        input_output_aliases={1: 0} if before else {},
        compiler_params=pltpu.CompilerParams(vmem_limit_bytes=8 * MIB),
        cost_estimate=pl.CostEstimate(
            flops=0, bytes_accessed=4 * depth * width, transcendentals=0
        ),
        name="join",
    )(part, *before)


def solution(mesh):
    sizes = (mesh.shape["rep"], mesh.shape["fsdp"])
    return jax.shard_map(
        functools.partial(per_device, sizes),
        mesh=mesh,
        in_specs=(
            P(None, "fsdp"),
            P("rep", "fsdp"),
            P("rep", None, "fsdp"),
            P("rep", None, "fsdp"),
            P("rep", "fsdp", None),
            P("rep", None, "fsdp"),
            P("rep", None, None),
        ),
        out_specs=(P(None, "fsdp"), P("rep", "fsdp")),
        check_vma=False,
    )
```

```python
import functools
import math
import jax
import jax.numpy as jnp
from jax import lax
from jax.experimental import pallas as pl
from jax.experimental.pallas import tpu as pltpu
from jax.sharding import PartitionSpec as P

F32 = jnp.float32
BF16 = jnp.bfloat16
WIRE = jnp.float16
WIRE_SCALE = 64.0
LANES = 128
SLABS = 4
PIECE = 64
MIB = 1024 * 1024


def forward_kernel(part_ref, weights_ref, turned_ref, product_ref):
    @pl.when(pl.program_id(0) == 0)
    def _():
        product_ref[...] = jnp.zeros_like(product_ref)

    part = part_ref[...]
    turned_ref[...] = part.T
    product_ref[...] += jnp.dot(part, weights_ref[...], preferred_element_type=F32)


def forward(part, weights):
    rows, depth = part.shape
    columns = weights.shape[1]
    block = depth // SLABS
    return pl.pallas_call(
        forward_kernel,
        grid=(SLABS,),
        in_specs=[
            pl.BlockSpec((rows, block), lambda d: (0, d)),
            pl.BlockSpec((block, columns), lambda d: (d, 0)),
        ],
        out_specs=[
            pl.BlockSpec((block, rows), lambda d: (d, 0)),
            pl.BlockSpec((rows, columns), lambda d: (0, 0)),
        ],
        out_shape=[
            jax.ShapeDtypeStruct((depth, rows), BF16),
            jax.ShapeDtypeStruct((rows, columns), F32),
        ],
        compiler_params=pltpu.CompilerParams(vmem_limit_bytes=14 * MIB),
        cost_estimate=pl.CostEstimate(
            flops=2 * rows * depth * columns,
            bytes_accessed=2 * depth * columns + 4 * rows * depth,
            transcendentals=0,
        ),
        name="forward",
    )(part, pinned(weights))


def arrive_kernel(piece, part_ref, weights_ref, *refs):
    natural_ref, turned_ref, product_ref = refs[-3:]
    block = part_ref.shape[1]
    place = pl.ds(piece * block, block)
    part = part_ref[...]
    natural_ref[:, place] = part
    turned_ref[place, :] = part.T
    product = jnp.dot(part, weights_ref[...], preferred_element_type=F32)
    if len(refs) > 3:
        product = product + refs[2][...]
    product_ref[...] = product


def arrive(piece, part, weights, before):
    rows, block = part.shape
    depth, columns = weights.shape
    whole = pl.BlockSpec(memory_space=pltpu.VMEM)
    return pl.pallas_call(
        functools.partial(arrive_kernel, piece),
        grid=(1,),
        in_specs=[whole, pl.BlockSpec((block, columns), lambda d: (piece, 0))]
        + [whole] * len(before),
        out_specs=[whole] * 3,
        out_shape=[
            jax.ShapeDtypeStruct((rows, depth), BF16),
            jax.ShapeDtypeStruct((depth, rows), BF16),
            jax.ShapeDtypeStruct((rows, columns), F32),
        ],
        input_output_aliases={2: 0, 3: 1, 4: 2} if before else {},
        compiler_params=pltpu.CompilerParams(vmem_limit_bytes=10 * MIB),
        cost_estimate=pl.CostEstimate(
            flops=2 * rows * block * columns,
            bytes_accessed=2 * block * columns + 6 * rows * block,
            transcendentals=0,
        ),
        name="arrive",
    )(part, pinned(weights), *before)


def pinned(array):
    return pltpu.with_memory_space_constraint(array, pltpu.HBM)


def changed_place(mine, slab, pair, pairs):
    offset = lax.bitwise_xor(slab * pairs + pair, mine // 2)
    bits = (SLABS * pairs).bit_length() - 1
    place = jnp.int32(0)
    for bit in range(bits):
        place = place * 2 + lax.rem(lax.shift_right_logical(offset, bit), 2)
    return place


def fetch_kernel(chunk, first_ref, second_ref, first_out, second_out, semaphore):
    width = first_out.shape[-1]
    columns = pl.ds(chunk * width, width)
    copies = [
        pltpu.make_async_copy(source.at[..., columns], target, semaphore.at[index])
        for index, (source, target) in enumerate(((first_ref, first_out), (second_ref, second_out)))
    ]
    for copy in copies:
        copy.start()
    for copy in copies:
        copy.wait()


def fetch(chunk, width, first, second):
    out = jax.ShapeDtypeStruct(first.shape[:-1] + (width,), F32)
    return pl.pallas_call(
        functools.partial(fetch_kernel, chunk),
        in_specs=[pl.BlockSpec(memory_space=pl.ANY)] * 2,
        out_specs=[pl.BlockSpec(memory_space=pltpu.VMEM)] * 2,
        out_shape=[out, out],
        scratch_shapes=[pltpu.SemaphoreType.DMA((2,))],
        compiler_params=pltpu.CompilerParams(vmem_limit_bytes=MIB),
        name="fetch",
    )(pinned(first), pinned(second))


def inner_kernel(
    tokens,
    fetched,
    mine_ref,
    low_ref,
    high_ref,
    low_turned_ref,
    high_turned_ref,
    start_ref,
    first_ref,
    second_ref,
    low_product_ref,
    high_product_ref,
    target_ref,
    count_ref,
    send_ref,
    keep_ref,
    first_state,
    second_state,
    weights_state,
    output_state,
    residual_state,
    gradient_state,
    rounded_state,
):
    step = pl.program_id(0)
    slab = pl.program_id(1)
    if fetched:
        first_ref, second_ref = first_ref.at[slab], second_ref.at[slab]
    pairs, cores, rows, _ = start_ref.shape
    mine = mine_ref[0]
    core = lax.rem(mine, cores)
    pieces = [pl.ds(begin, PIECE) for begin in range(0, rows, PIECE)]

    def weigh(output, which):
        residual = ((output - target_ref[...].astype(F32)) / tokens).astype(BF16)
        residual_state[...] = (residual.astype(F32) * count_ref[which]).astype(BF16)

    def descend(first, second, weights):
        root = second * lax.rsqrt(second)
        below = (100.0 * math.sqrt(0.05)) * root + 1e-06
        return 0.99 * weights - first * pl.reciprocal(below, approx=True)

    def differentiate(pair, which, slot):
        turned = jnp.concatenate(
            [low_turned_ref[slab, pair, which], high_turned_ref[slab, pair, which]], axis=1
        )
        gradient_state[slot] = jnp.dot(
            turned, residual_state[...], preferred_element_type=F32
        )

    def project(slot):
        begin = (slab * pairs * cores + slot) * rows
        place = pl.ds(pl.multiple_of(begin, rows), rows)
        picked = jnp.concatenate([low_ref[:, place], high_ref[:, place]], axis=0)
        return jnp.dot(picked, rounded_state[slot], preferred_element_type=F32)

    @pl.when((step == 0) & (slab == 0))
    def _():
        weigh(jnp.concatenate([low_product_ref[...], high_product_ref[...]], axis=0), 0)
        output_state[...] = jnp.zeros_like(output_state)

    @pl.when((step == 1) & (slab == 0))
    def _():
        weigh(output_state[...], 1)

    slots = [(slot, *divmod(slot, cores)) for slot in range(pairs * cores)]

    @pl.when(step == 0)
    def _():
        total = jnp.zeros(output_state.shape, F32)
        differentiate(0, 0, 0)
        for slot, pair, which in slots:
            if slot + 1 < len(slots):
                ahead, *place = slots[slot + 1]
                differentiate(*place, ahead)
            for piece in pieces:
                gradient = gradient_state[slot, piece]
                first = 9.0 * first_ref[pair, which, piece] + gradient
                second = 19.0 * second_ref[pair, which, piece] + gradient * gradient
                weights = descend(first, second, start_ref[pair, which, piece].astype(F32))
                first_state[slab, pair, which, piece] = first
                second_state[slab, pair, which, piece] = second
                weights_state[slab, pair, which, piece] = weights
                rounded_state[slot, piece] = weights.astype(BF16)
            if slot:
                total += project(slot - 1)
        output_state[...] += total + project(len(slots) - 1)

    @pl.when(step == 1)
    def _():
        sides = ((1 - core, send_ref), (core, keep_ref))
        differentiate(0, sides[0][0], 0)
        for slot, pair, side in slots:
            if slot + 1 < len(slots):
                ahead, next_pair, next_side = slots[slot + 1]
                differentiate(next_pair, sides[next_side][0], ahead)
            which, out_ref = sides[side]
            place = changed_place(mine, slab, pair, pairs)
            for piece in pieces:
                gradient = gradient_state[slot, piece]
                first = 0.9 * first_state[slab, pair, which, piece] + gradient
                second = 0.95 * second_state[slab, pair, which, piece] + gradient * gradient
                weights = descend(first, second, weights_state[slab, pair, which, piece])
                change = start_ref[pair, which, piece].astype(F32) - weights
                out_ref[place, piece] = change * WIRE_SCALE


def inner(chunk, width, fetched, mine, banks, turned, start, first, second, products, target, count, tokens):
    slabs, pairs, cores, rows, _ = start.shape
    half, depth = banks[0].shape

    def held(step, slab):
        return jnp.where(step == 0, slab, slabs - 1)

    whole = pl.BlockSpec(memory_space=pltpu.VMEM)
    tile = (None, pairs, cores, rows, width)
    state = pl.BlockSpec(tile, lambda s, z, c: (held(s, z), 0, 0, 0, chunk))
    product = pl.BlockSpec((half, width), lambda s, z, c: (0, chunk))
    states = (first, second) if fetched else (pinned(first), pinned(second))
    elements = depth * width
    return pl.pallas_call(
        functools.partial(inner_kernel, float(tokens), fetched),
        grid_spec=pltpu.PrefetchScalarGridSpec(
            num_scalar_prefetch=1,
            grid=(2, slabs),
            in_specs=[whole] * 4
            + [
                pl.BlockSpec(tile, lambda s, z, c: (z, 0, 0, 0, chunk)),
                whole if fetched else state,
                whole if fetched else state,
                product,
                product,
                pl.BlockSpec((2 * half, width), lambda s, z, c: (0, chunk)),
                pl.BlockSpec(count.shape, lambda s, z, c: (0, 0, 0)),
            ],
            out_specs=[whole, whole],
            scratch_shapes=[
                pltpu.VMEM((slabs, pairs, cores, rows, width), F32),
                pltpu.VMEM((slabs, pairs, cores, rows, width), F32),
                pltpu.VMEM((slabs, pairs, cores, rows, width), F32),
                pltpu.VMEM((2 * half, width), F32),
                pltpu.VMEM((2 * half, width), BF16),
                pltpu.VMEM((pairs * cores, rows, width), F32),
                pltpu.VMEM((pairs * cores, rows, width), BF16),
            ],
        ),
        out_shape=[
            jax.ShapeDtypeStruct((slabs * pairs, rows, width), F32),
            jax.ShapeDtypeStruct((slabs * pairs, rows, width), F32),
        ],
        compiler_params=pltpu.CompilerParams(vmem_limit_bytes=22 * MIB),
        cost_estimate=pl.CostEstimate(
            flops=12 * half * elements,
            bytes_accessed=20 * elements,
            transcendentals=4 * elements,
        ),
        name="inner",
    )(mine, *banks, *turned, pinned(start), *states, *products, target, count)


def assemble_kernel(chunk, offsets, place_ref, *refs):
    received = refs[: len(offsets)]
    out_ref, semaphore = refs[-2:]
    width = received[0].shape[-1]
    mine = place_ref[0]
    copies = []
    for ref, group in zip(received, offsets):
        for entry, offset in enumerate(group):
            copies.append(
                pltpu.make_async_copy(
                    ref.at[entry],
                    out_ref.at[lax.bitwise_xor(mine, offset), :, pl.ds(chunk * width, width)],
                    semaphore.at[len(copies)],
                )
            )
    for copy in copies:
        copy.start()
    for copy in copies:
        copy.wait()


def assemble(chunk, place, received, offsets, shape, before):
    vmem = pl.BlockSpec(memory_space=pltpu.VMEM)
    return pl.pallas_call(
        functools.partial(assemble_kernel, chunk, offsets),
        in_specs=[pl.BlockSpec(memory_space=pltpu.SMEM)]
        + [vmem] * len(received)
        + [pl.BlockSpec(memory_space=pl.ANY)] * len(before),
        out_specs=pl.BlockSpec(memory_space=pl.ANY),
        out_shape=jax.ShapeDtypeStruct(shape, BF16),
        input_output_aliases={1 + len(received): 0} if before else {},
        scratch_shapes=[pltpu.SemaphoreType.DMA((sum(map(len, offsets)),))],
        compiler_params=pltpu.CompilerParams(vmem_limit_bytes=12 * MIB),
        cost_estimate=pl.CostEstimate(
            flops=0, bytes_accessed=4 * shape[0] * shape[1] * received[0].shape[-1], transcendentals=0
        ),
        name="assemble",
    )(place, *received, *before)


def tied(first, second):
    return lax.optimization_barrier((first, second))


def per_device(sizes, global_weights, momentum, first_moment, second_moment, hidden_bank, target_bank, token_ids):
    reps, shards = sizes
    bits = reps.bit_length() - 1
    depth, columns = global_weights.shape
    rows = depth // reps
    store = hidden_bank.shape[1] * shards
    half = store // 2
    ids = token_ids[0]
    tokens = ids.shape[1]
    width = min(columns, LANES)
    chunks = columns // width
    mine = lax.axis_index("rep")

    def swapped(array, offset):
        pairs = [(index, index ^ offset) for index in range(reps)]
        return lax.ppermute(array, "rep", pairs)

    spans = [[0, 1 << bit] for bit in range(1, bits)]

    cut = (SLABS, reps // (2 * SLABS), 2, rows, columns)
    start = global_weights.reshape(cut)
    first = first_moment.reshape(cut)
    second = second_moment.reshape(cut)
    early = fetch(0, width, first, second)

    own_bank = hidden_bank[0]
    target = target_bank[0]
    count = jnp.sum(
        ids[:, :, None] == jnp.arange(store, dtype=ids.dtype)[None, None, :], axis=1
    ).astype(F32)
    if shards == 2:
        block = depth // SLABS
        parts = []
        source = own_bank
        for d in range(SLABS):
            part, source = tied(source[:, d * block : (d + 1) * block], source)
            parts.append(lax.ppermute(part, "fsdp", [(0, 1), (1, 0)]))
        own_turned, own_product = forward(own_bank, global_weights)
        parts[0], early = tied(parts[0], early)
        joined = ()
        for d, part in enumerate(parts):
            joined = arrive(d, part, global_weights, joined)
        banks = (own_bank, joined[0])
        turned = (own_turned, joined[1])
        products = (own_product, joined[2])
        swap = lax.axis_index("fsdp") == 1
        target = jnp.where(swap, jnp.roll(target, half, axis=0), target)
        count = jnp.where(swap, jnp.roll(count, half, axis=1), count)
    else:
        whole = lax.all_gather(own_bank, "fsdp", axis=0, tiled=True)
        banks = (whole[:half], whole[half:])
        turned, products = zip(*(forward(bank, global_weights) for bank in banks))
    count = count[:, :, None]

    turned = [array.reshape(cut[:4] + (half,)) for array in turned]
    place = mine.reshape(1).astype(jnp.int32)
    my_start = lax.dynamic_slice_in_dim(global_weights, mine * rows, rows, 0)
    shares = [
        tied(momentum[:, begin : begin + width], my_start[:, begin : begin + width])
        for begin in range(0, columns, width)
    ]

    def parted(terms, span):
        size = terms[0].shape[0] // len(span)
        parts = [[term[begin : begin + size] for term in terms] for begin in range(0, size * len(span), size)]
        outgoing = [sum(term.astype(F32) for term in part).astype(WIRE) for part in parts[1:]]
        return outgoing, parts[0]

    def sent(outgoing, span):
        return [swapped(array, offset) for array, offset in zip(outgoing, span[1:])]

    result = ()

    def chain(chunk, keep, arrived):
        terms = [keep, arrived]
        for span in spans:
            outgoing, terms = parted(terms, span)
            outgoing = yield outgoing
            arrived = yield sent(outgoing, span)
            terms = terms + arrived
        total = sum(term.astype(F32) for term in terms)[0]
        average = total * (1.0 / (WIRE_SCALE * reps))
        moved = 0.9 * shares[chunk][0] + average
        fresh = (shares[chunk][1].astype(F32) - 0.7 * (average + 0.9 * moved)).astype(BF16)
        stack = yield fresh[None]
        offsets = [0]
        for span in spans[:0:-1]:
            arrived = yield sent([stack], span)
            offsets = [offset ^ far for far in span for offset in offsets]
            stack = yield jnp.concatenate([stack] + arrived)
        across, = yield sent([stack], spans[0])
        finished[chunk] = (moved, stack, across, offsets)
        yield ()

    finished = {}
    running = {}
    formed = {}

    def move_on(which, behind=()):
        which = [chunk for chunk in which if chunk not in finished]
        arrived = {chunk: running[chunk].send(formed[chunk]) for chunk in which}
        arrived, _ = tied(arrived, [formed[chunk] for chunk in behind])
        for chunk in which:
            formed[chunk] = running[chunk].send(arrived[chunk])

    token = place
    for chunk in range(chunks):
        states = early if chunk == 0 else (first, second)
        send, keep = inner(
            chunk, width, chunk == 0, token, banks, turned, start, *states, products, target, count, tokens
        )
        send = send.astype(WIRE)
        if chunk:
            move_on(range(chunk))
            formed, send = tied(formed, send)
        running[chunk] = chain(chunk, keep, swapped(send, 1))
        formed[chunk] = next(running[chunk])
        if chunk + 1 < chunks:
            formed, token = tied(formed, token)

    head = chunks - 1
    move_on(range(head), behind=[head])
    for chunk in range(chunks):
        while chunk not in finished:
            move_on([chunk])

    new_momentum = []
    for chunk in range(chunks):
        moved, stack, across, offsets = finished[chunk]
        new_momentum.append(moved)
        offsets = [[offset ^ low for offset in offsets] for low in (0, 2, 1, 3)]
        if result:
            across, *result = tied(across, result[0])
        received = [stack, across, swapped(stack, 1), swapped(across, 1)]
        result = (
            assemble(chunk, place, received, offsets, (reps, rows, columns), result),
        )

    return result[0].reshape(depth, columns), jnp.concatenate(new_momentum, axis=1)


def solution(mesh):
    sizes = (mesh.shape["rep"], mesh.shape["fsdp"])
    return jax.shard_map(
        functools.partial(per_device, sizes),
        mesh=mesh,
        in_specs=(
            P(None, "fsdp"),
            P("rep", "fsdp"),
            P("rep", None, "fsdp"),
            P("rep", None, "fsdp"),
            P("rep", "fsdp", None),
            P("rep", None, "fsdp"),
            P("rep", None, None),
        ),
        out_specs=(P(None, "fsdp"), P("rep", "fsdp")),
        check_vma=False,
    )
```

```python
import functools
import math
import jax
import jax.numpy as jnp
from jax import lax
from jax.experimental import pallas as pl
from jax.experimental.pallas import tpu as pltpu
from jax.sharding import PartitionSpec as P

F32 = jnp.float32
BF16 = jnp.bfloat16
WIRE = jnp.float16
WIRE_SCALE = 64.0
LANES = 128
SLABS = 4
PIECE = 32
MIB = 1024 * 1024


def forward_kernel(part_ref, weights_ref, turned_ref, product_ref):
    @pl.when(pl.program_id(0) == 0)
    def _():
        product_ref[...] = jnp.zeros_like(product_ref)

    part = part_ref[...]
    turned_ref[...] = part.T
    product_ref[...] += jnp.dot(part, weights_ref[...], preferred_element_type=F32)


def forward(part, weights):
    rows, depth = part.shape
    columns = weights.shape[1]
    block = depth // SLABS
    return pl.pallas_call(
        forward_kernel,
        grid=(SLABS,),
        in_specs=[
            pl.BlockSpec((rows, block), lambda d: (0, d)),
            pl.BlockSpec((block, columns), lambda d: (d, 0)),
        ],
        out_specs=[
            pl.BlockSpec((block, rows), lambda d: (d, 0)),
            pl.BlockSpec((rows, columns), lambda d: (0, 0)),
        ],
        out_shape=[
            jax.ShapeDtypeStruct((depth, rows), BF16),
            jax.ShapeDtypeStruct((rows, columns), F32),
        ],
        compiler_params=pltpu.CompilerParams(vmem_limit_bytes=14 * MIB),
        cost_estimate=pl.CostEstimate(
            flops=2 * rows * depth * columns,
            bytes_accessed=2 * depth * columns + 4 * rows * depth,
            transcendentals=0,
        ),
        name="forward",
    )(part, pinned(weights))


def arrive_kernel(piece, part_ref, weights_ref, *refs):
    natural_ref, turned_ref, product_ref = refs[-3:]
    block = part_ref.shape[1]
    place = pl.ds(piece * block, block)
    part = part_ref[...]
    natural_ref[:, place] = part
    turned_ref[place, :] = part.T
    product = jnp.dot(part, weights_ref[...], preferred_element_type=F32)
    if len(refs) > 3:
        product = product + refs[2][...]
    product_ref[...] = product


def arrive(piece, part, weights, before):
    rows, block = part.shape
    depth, columns = weights.shape
    whole = pl.BlockSpec(memory_space=pltpu.VMEM)
    return pl.pallas_call(
        functools.partial(arrive_kernel, piece),
        grid=(1,),
        in_specs=[whole, pl.BlockSpec((block, columns), lambda d: (piece, 0))]
        + [whole] * len(before),
        out_specs=[whole] * 3,
        out_shape=[
            jax.ShapeDtypeStruct((rows, depth), BF16),
            jax.ShapeDtypeStruct((depth, rows), BF16),
            jax.ShapeDtypeStruct((rows, columns), F32),
        ],
        input_output_aliases={2: 0, 3: 1, 4: 2} if before else {},
        compiler_params=pltpu.CompilerParams(vmem_limit_bytes=10 * MIB),
        cost_estimate=pl.CostEstimate(
            flops=2 * rows * block * columns,
            bytes_accessed=2 * block * columns + 6 * rows * block,
            transcendentals=0,
        ),
        name="arrive",
    )(part, pinned(weights), *before)


def pinned(array):
    return pltpu.with_memory_space_constraint(array, pltpu.HBM)


def changed_place(mine, slab, pair, pairs):
    offset = lax.bitwise_xor(slab * pairs + pair, mine // 2)
    bits = (SLABS * pairs).bit_length() - 1
    place = jnp.int32(0)
    for bit in range(bits):
        place = place * 2 + lax.rem(lax.shift_right_logical(offset, bit), 2)
    return place


def inner_kernel(
    tokens,
    mine_ref,
    low_ref,
    high_ref,
    low_turned_ref,
    high_turned_ref,
    start_ref,
    first_ref,
    second_ref,
    low_product_ref,
    high_product_ref,
    target_ref,
    count_ref,
    *rest,
):
    *change_refs, first_state, second_state, output_state, residual_state, gradient_state, rounded_state = rest
    send_refs, keep_refs = change_refs[::2], change_refs[1::2]
    step = pl.program_id(0)
    slab = pl.program_id(1)
    pairs, cores, rows, _ = start_ref.shape
    mine = mine_ref[0]
    core = lax.rem(mine, cores)
    pieces = [pl.ds(begin, PIECE) for begin in range(0, rows, PIECE)]
    slots = [(slot, *divmod(slot, cores)) for slot in range(pairs * cores)]
    held = gradient_state.shape[0]

    def weigh(output, which):
        residual = ((output - target_ref[...].astype(F32)) / tokens).astype(BF16)
        residual_state[...] = (residual.astype(F32) * count_ref[which]).astype(BF16)

    def descend(first, second, weights):
        root = second * lax.rsqrt(second)
        below = (100.0 * math.sqrt(0.05)) * root + 1e-06
        return 0.99 * weights - first * lax.rsqrt(below * below)

    def differentiate(pair, which, slot):
        turned = jnp.concatenate(
            [low_turned_ref[slab, pair, which], high_turned_ref[slab, pair, which]], axis=1
        )
        gradient_state[slot % held] = jnp.dot(
            turned, residual_state[...], preferred_element_type=F32
        )

    def project(slot):
        begin = (slab * pairs * cores + slot) * rows
        place = pl.ds(pl.multiple_of(begin, rows), rows)
        picked = jnp.concatenate([low_ref[:, place], high_ref[:, place]], axis=0)
        return jnp.dot(picked, rounded_state[slot % held], preferred_element_type=F32)

    @pl.when((step == 0) & (slab == 0))
    def _():
        weigh(jnp.concatenate([low_product_ref[...], high_product_ref[...]], axis=0), 0)
        output_state[...] = jnp.zeros_like(output_state)

    @pl.when((step == 1) & (slab == 0))
    def _():
        weigh(output_state[...], 1)

    @pl.when(step == 0)
    def _():
        differentiate(0, 0, 0)
        for slot, pair, which in slots:
            if slot + 1 < len(slots):
                ahead, *place = slots[slot + 1]
                differentiate(*place, ahead)
            for piece in pieces:
                gradient = gradient_state[slot % held, piece]
                first = 9.0 * first_ref[pair, which, piece] + gradient
                second = 19.0 * second_ref[pair, which, piece] + gradient * gradient
                weights = descend(first, second, start_ref[pair, which, piece].astype(F32))
                first_state[slab, pair, which, piece] = first
                second_state[slab, pair, which, piece] = second
                rounded_state[slot % held, piece] = weights.astype(BF16)
            output_state[...] += project(slot)

    @pl.when(step == 1)
    def _():
        sides = ((1 - core, send_refs), (core, keep_refs))
        differentiate(0, sides[0][0], 0)
        for slot, pair, side in slots:
            if slot + 1 < len(slots):
                ahead, next_pair, next_side = slots[slot + 1]
                differentiate(next_pair, sides[next_side][0], ahead)
            which, out_refs = sides[side]
            place = changed_place(mine, slab, pair, pairs)
            for piece in pieces:
                gradient = gradient_state[slot % held, piece]
                first = first_state[slab, pair, which, piece]
                second = second_state[slab, pair, which, piece]
                start = start_ref[pair, which, piece].astype(F32)
                weights = descend(first, second, start)
                first = 0.9 * first + gradient
                second = 0.95 * second + gradient * gradient
                change = (start - descend(first, second, weights)) * WIRE_SCALE
                for index, out_ref in enumerate(out_refs):
                    part = out_ref.shape[-1]
                    out_ref[place, piece] = change[:, index * part : (index + 1) * part]


def inner(call, width, part, mine, banks, turned, start, first, second, products, target, count, tokens):
    slabs, pairs, cores, rows, _ = start.shape
    half, depth = banks[0].shape

    def held(step, slab):
        return jnp.where(step == 0, slab, slabs - 1)

    whole = pl.BlockSpec(memory_space=pltpu.VMEM)
    tile = (None, pairs, cores, rows, width)
    state = pl.BlockSpec(tile, lambda s, z, c: (held(s, z), 0, 0, 0, call))
    product = pl.BlockSpec((half, width), lambda s, z, c: (0, call))
    change = jax.ShapeDtypeStruct((slabs * pairs, rows, part), F32)
    outputs = 2 * (width // part)
    elements = depth * width
    return pl.pallas_call(
        functools.partial(inner_kernel, float(tokens)),
        grid_spec=pltpu.PrefetchScalarGridSpec(
            num_scalar_prefetch=1,
            grid=(2, slabs),
            in_specs=[whole] * 4
            + [
                pl.BlockSpec(tile, lambda s, z, c: (z, 0, 0, 0, call)),
                state,
                state,
                product,
                product,
                pl.BlockSpec((2 * half, width), lambda s, z, c: (0, call)),
                pl.BlockSpec(count.shape, lambda s, z, c: (0, 0, 0)),
            ],
            out_specs=[whole] * outputs,
            scratch_shapes=[
                pltpu.VMEM((slabs, pairs, cores, rows, width), F32),
                pltpu.VMEM((slabs, pairs, cores, rows, width), F32),
                pltpu.VMEM((2 * half, width), F32),
                pltpu.VMEM((2 * half, width), BF16),
                pltpu.VMEM((2, rows, width), F32),
                pltpu.VMEM((2, rows, width), BF16),
            ],
        ),
        out_shape=[change] * outputs,
        compiler_params=pltpu.CompilerParams(vmem_limit_bytes=32 * MIB),
        cost_estimate=pl.CostEstimate(
            flops=12 * half * elements,
            bytes_accessed=20 * elements,
            transcendentals=6 * elements,
        ),
        name="inner",
    )(mine, *banks, *turned, pinned(start), pinned(first), pinned(second), *products, target, count)


def assemble_kernel(chunk, offsets, place_ref, *refs):
    received = refs[: len(offsets)]
    out_ref, semaphore = refs[-2:]
    width = received[0].shape[-1]
    mine = place_ref[0]
    copies = []
    for ref, group in zip(received, offsets):
        for entry, offset in enumerate(group):
            copies.append(
                pltpu.make_async_copy(
                    ref.at[entry],
                    out_ref.at[lax.bitwise_xor(mine, offset), :, pl.ds(chunk * width, width)],
                    semaphore.at[len(copies)],
                )
            )
    for copy in copies:
        copy.start()
    for copy in copies:
        copy.wait()


def assemble(chunk, place, received, offsets, shape, before):
    vmem = pl.BlockSpec(memory_space=pltpu.VMEM)
    return pl.pallas_call(
        functools.partial(assemble_kernel, chunk, offsets),
        in_specs=[pl.BlockSpec(memory_space=pltpu.SMEM)]
        + [vmem] * len(received)
        + [pl.BlockSpec(memory_space=pl.ANY)] * len(before),
        out_specs=pl.BlockSpec(memory_space=pl.ANY),
        out_shape=jax.ShapeDtypeStruct(shape, BF16),
        input_output_aliases={1 + len(received): 0} if before else {},
        scratch_shapes=[pltpu.SemaphoreType.DMA((sum(map(len, offsets)),))],
        compiler_params=pltpu.CompilerParams(vmem_limit_bytes=12 * MIB),
        cost_estimate=pl.CostEstimate(
            flops=0, bytes_accessed=4 * shape[0] * shape[1] * received[0].shape[-1], transcendentals=0
        ),
        name="assemble",
    )(place, *received, *before)


def tied(first, second):
    return lax.optimization_barrier((first, second))


def per_device(sizes, global_weights, momentum, first_moment, second_moment, hidden_bank, target_bank, token_ids):
    reps, shards = sizes
    bits = reps.bit_length() - 1
    depth, columns = global_weights.shape
    rows = depth // reps
    store = hidden_bank.shape[1] * shards
    half = store // 2
    ids = token_ids[0]
    tokens = ids.shape[1]
    width = min(columns, LANES)
    chunks = columns // width
    mine = lax.axis_index("rep")

    def swapped(array, offset):
        pairs = [(index, index ^ offset) for index in range(reps)]
        return lax.ppermute(array, "rep", pairs)

    spans = [[0, 1 << bit] for bit in range(1, bits)]

    cut = (SLABS, reps // (2 * SLABS), 2, rows, columns)
    start = global_weights.reshape(cut)
    first = first_moment.reshape(cut)
    second = second_moment.reshape(cut)

    own_bank = hidden_bank[0]
    target = target_bank[0]
    count = jnp.sum(
        ids[:, :, None] == jnp.arange(store, dtype=ids.dtype)[None, None, :], axis=1
    ).astype(F32)
    if shards == 2:
        block = depth // SLABS
        parts = []
        source = own_bank
        for d in range(SLABS):
            part, source = tied(source[:, d * block : (d + 1) * block], source)
            parts.append(lax.ppermute(part, "fsdp", [(0, 1), (1, 0)]))
        own_turned, own_product = forward(own_bank, global_weights)
        joined = ()
        for d, part in enumerate(parts):
            joined = arrive(d, part, global_weights, joined)
        banks = (own_bank, joined[0])
        turned = (own_turned, joined[1])
        products = (own_product, joined[2])
        swap = lax.axis_index("fsdp") == 1
        target = jnp.where(swap, jnp.roll(target, half, axis=0), target)
        count = jnp.where(swap, jnp.roll(count, half, axis=1), count)
    else:
        whole = lax.all_gather(own_bank, "fsdp", axis=0, tiled=True)
        banks = (whole[:half], whole[half:])
        turned, products = zip(*(forward(bank, global_weights) for bank in banks))
    count = count[:, :, None]

    turned = [array.reshape(cut[:4] + (half,)) for array in turned]
    place = mine.reshape(1).astype(jnp.int32)
    my_start = lax.dynamic_slice_in_dim(global_weights, mine * rows, rows, 0)
    shares = [
        tied(momentum[:, begin : begin + width], my_start[:, begin : begin + width])
        for begin in range(0, columns, width)
    ]

    def parted(terms, span):
        size = terms[0].shape[0] // len(span)
        parts = [[term[begin : begin + size] for term in terms] for begin in range(0, size * len(span), size)]
        outgoing = [sum(term.astype(F32) for term in part).astype(WIRE) for part in parts[1:]]
        return outgoing, parts[0]

    def sent(outgoing, span):
        return [swapped(array, offset) for array, offset in zip(outgoing, span[1:])]

    result = ()

    def chain(chunk, keep, arrived):
        terms = [keep, arrived]
        for span in spans:
            outgoing, terms = parted(terms, span)
            outgoing = yield outgoing
            arrived = yield sent(outgoing, span)
            terms = terms + arrived
        total = sum(term.astype(F32) for term in terms)[0]
        average = total * (1.0 / (WIRE_SCALE * reps))
        moved = 0.9 * shares[chunk][0] + average
        fresh = (shares[chunk][1].astype(F32) - 0.7 * (average + 0.9 * moved)).astype(BF16)
        stack = yield fresh[None]
        offsets = [0]
        for span in spans[:0:-1]:
            arrived = yield sent([stack], span)
            offsets = [offset ^ far for far in span for offset in offsets]
            stack = yield jnp.concatenate([stack] + arrived)
        across, = yield sent([stack], spans[0])
        finished[chunk] = (moved, stack, across, offsets)
        yield ()

    finished = {}
    running = {}
    formed = {}

    def move_on(which, behind=()):
        which = [chunk for chunk in which if chunk not in finished]
        arrived = {chunk: running[chunk].send(formed[chunk]) for chunk in which}
        arrived, _ = tied(arrived, [formed[chunk] for chunk in behind])
        for chunk in which:
            formed[chunk] = running[chunk].send(arrived[chunk])

    token = place
    wide = min(columns, 2 * LANES)
    for call in range(columns // wide):
        changes = inner(
            call, wide, width, token, banks, turned, start, first, second, products, target, count, tokens
        )
        fresh = range(call * (wide // width), (call + 1) * (wide // width))
        sends = [send.astype(WIRE) for send in changes[::2]]
        if call:
            move_on([0])
            sends, _ = tied(sends, formed[0])
        for chunk, send, keep in zip(fresh, sends, changes[1::2]):
            running[chunk] = chain(chunk, keep, swapped(send, 1))
            formed[chunk] = next(running[chunk])
        if fresh[-1] + 1 < chunks:
            formed, token = tied(formed, token)
    move_on(range(fresh[0]), behind=fresh)
    for chunk in range(chunks):
        while chunk not in finished:
            move_on([chunk])

    new_momentum = []
    for chunk in range(chunks):
        moved, stack, across, offsets = finished[chunk]
        new_momentum.append(moved)
        offsets = [[offset ^ low for offset in offsets] for low in (0, 2, 1, 3)]
        if result:
            across, *result = tied(across, result[0])
        received = [stack, across, swapped(stack, 1), swapped(across, 1)]
        result = (
            assemble(chunk, place, received, offsets, (reps, rows, columns), result),
        )

    return result[0].reshape(depth, columns), jnp.concatenate(new_momentum, axis=1)


def solution(mesh):
    sizes = (mesh.shape["rep"], mesh.shape["fsdp"])
    return jax.shard_map(
        functools.partial(per_device, sizes),
        mesh=mesh,
        in_specs=(
            P(None, "fsdp"),
            P("rep", "fsdp"),
            P("rep", None, "fsdp"),
            P("rep", None, "fsdp"),
            P("rep", "fsdp", None),
            P("rep", None, "fsdp"),
            P("rep", None, None),
        ),
        out_specs=(P(None, "fsdp"), P("rep", "fsdp")),
        check_vma=False,
    )
```

```python
import functools
import math
import jax
import jax.numpy as jnp
from jax import lax
from jax.experimental import pallas as pl
from jax.experimental.pallas import tpu as pltpu
from jax.sharding import PartitionSpec as P

F32 = jnp.float32
BF16 = jnp.bfloat16
WIRE = jnp.float16
WIRE_SCALE = 64.0
LANES = 128
SLABS = 4
PIECE = 8192
MIB = 1024 * 1024


def forward_kernel(part_ref, weights_ref, turned_ref, product_ref):
    @pl.when(pl.program_id(0) == 0)
    def _():
        product_ref[...] = jnp.zeros_like(product_ref)

    part = part_ref[...]
    turned_ref[...] = part.T
    product_ref[...] += jnp.dot(part, weights_ref[...], preferred_element_type=F32)


def forward(part, weights):
    rows, depth = part.shape
    columns = weights.shape[1]
    block = depth // SLABS
    return pl.pallas_call(
        forward_kernel,
        grid=(SLABS,),
        in_specs=[
            pl.BlockSpec((rows, block), lambda d: (0, d)),
            pl.BlockSpec((block, columns), lambda d: (d, 0)),
        ],
        out_specs=[
            pl.BlockSpec((block, rows), lambda d: (d, 0)),
            pl.BlockSpec((rows, columns), lambda d: (0, 0)),
        ],
        out_shape=[
            jax.ShapeDtypeStruct((depth, rows), BF16),
            jax.ShapeDtypeStruct((rows, columns), F32),
        ],
        compiler_params=pltpu.CompilerParams(vmem_limit_bytes=14 * MIB),
        cost_estimate=pl.CostEstimate(
            flops=2 * rows * depth * columns,
            bytes_accessed=2 * depth * columns + 4 * rows * depth,
            transcendentals=0,
        ),
        name="forward",
    )(part, pinned(weights))


def arrive_kernel(piece, part_ref, weights_ref, *refs):
    natural_ref, turned_ref, product_ref = refs[-3:]
    block = part_ref.shape[1]
    place = pl.ds(piece * block, block)
    part = part_ref[...]
    natural_ref[:, place] = part
    turned_ref[place, :] = part.T
    product = jnp.dot(part, weights_ref[...], preferred_element_type=F32)
    if len(refs) > 3:
        product = product + refs[2][...]
    product_ref[...] = product


def arrive(piece, part, weights, before):
    rows, block = part.shape
    depth, columns = weights.shape
    whole = pl.BlockSpec(memory_space=pltpu.VMEM)
    return pl.pallas_call(
        functools.partial(arrive_kernel, piece),
        grid=(1,),
        in_specs=[whole, pl.BlockSpec((block, columns), lambda d: (piece, 0))]
        + [whole] * len(before),
        out_specs=[whole] * 3,
        out_shape=[
            jax.ShapeDtypeStruct((rows, depth), BF16),
            jax.ShapeDtypeStruct((depth, rows), BF16),
            jax.ShapeDtypeStruct((rows, columns), F32),
        ],
        input_output_aliases={2: 0, 3: 1, 4: 2} if before else {},
        compiler_params=pltpu.CompilerParams(vmem_limit_bytes=10 * MIB),
        cost_estimate=pl.CostEstimate(
            flops=2 * rows * block * columns,
            bytes_accessed=2 * block * columns + 6 * rows * block,
            transcendentals=0,
        ),
        name="arrive",
    )(part, pinned(weights), *before)


def pinned(array):
    return pltpu.with_memory_space_constraint(array, pltpu.HBM)


def changed_place(mine, slab, pair, pairs):
    offset = lax.bitwise_xor(slab * pairs + pair, mine // 2)
    bits = (SLABS * pairs).bit_length() - 1
    place = jnp.int32(0)
    for bit in range(bits):
        place = place * 2 + lax.rem(lax.shift_right_logical(offset, bit), 2)
    return place


def inner_kernel(
    tokens,
    mine_ref,
    low_ref,
    high_ref,
    low_turned_ref,
    high_turned_ref,
    start_ref,
    first_ref,
    second_ref,
    low_product_ref,
    high_product_ref,
    target_ref,
    count_ref,
    *rest,
):
    *change_refs, first_state, second_state, output_state, residual_state, gradient_state, rounded_state = rest
    send_refs, keep_refs = change_refs[::2], change_refs[1::2]
    step = pl.program_id(0)
    slab = pl.program_id(1)
    pairs, cores, rows, _ = start_ref.shape
    mine = mine_ref[0]
    core = lax.rem(mine, cores)
    height = PIECE // start_ref.shape[-1]
    pieces = [pl.ds(begin, height) for begin in range(0, rows, height)]
    slots = [(slot, *divmod(slot, cores)) for slot in range(pairs * cores)]
    held = gradient_state.shape[0]

    def weigh(output, which):
        residual = ((output - target_ref[...].astype(F32)) / tokens).astype(BF16)
        residual_state[...] = (residual.astype(F32) * count_ref[which]).astype(BF16)

    def descend(first, second, weights):
        root = second * lax.rsqrt(second)
        below = (100.0 * math.sqrt(0.05)) * root + 1e-06
        return 0.99 * weights - first * lax.rsqrt(below * below)

    def differentiate(pair, which, slot):
        turned = jnp.concatenate(
            [low_turned_ref[slab, pair, which], high_turned_ref[slab, pair, which]], axis=1
        )
        gradient_state[slot % held] = jnp.dot(
            turned, residual_state[...], preferred_element_type=F32
        )

    def project(slot):
        begin = (slab * pairs * cores + slot) * rows
        place = pl.ds(pl.multiple_of(begin, rows), rows)
        picked = jnp.concatenate([low_ref[:, place], high_ref[:, place]], axis=0)
        return jnp.dot(picked, rounded_state[slot % held], preferred_element_type=F32)

    @pl.when((step == 0) & (slab == 0))
    def _():
        weigh(jnp.concatenate([low_product_ref[...], high_product_ref[...]], axis=0), 0)
        output_state[...] = jnp.zeros_like(output_state)

    @pl.when((step == 1) & (slab == 0))
    def _():
        weigh(output_state[...], 1)

    @pl.when(step == 0)
    def _():
        differentiate(0, 0, 0)
        for slot, pair, which in slots:
            if slot + 1 < len(slots):
                ahead, *place = slots[slot + 1]
                differentiate(*place, ahead)
            for piece in pieces:
                gradient = gradient_state[slot % held, piece]
                first = 9.0 * first_ref[pair, which, piece] + gradient
                second = 19.0 * second_ref[pair, which, piece] + gradient * gradient
                weights = descend(first, second, start_ref[pair, which, piece].astype(F32))
                first_state[slab, pair, which, piece] = first
                second_state[slab, pair, which, piece] = second
                rounded_state[slot % held, piece] = weights.astype(BF16)
            output_state[...] += project(slot)

    @pl.when(step == 1)
    def _():
        sides = ((1 - core, send_refs), (core, keep_refs))
        differentiate(0, sides[0][0], 0)
        for slot, pair, side in slots:
            if slot + 1 < len(slots):
                ahead, next_pair, next_side = slots[slot + 1]
                differentiate(next_pair, sides[next_side][0], ahead)
            which, out_refs = sides[side]
            place = changed_place(mine, slab, pair, pairs)
            for piece in pieces:
                gradient = gradient_state[slot % held, piece]
                first = first_state[slab, pair, which, piece]
                second = second_state[slab, pair, which, piece]
                start = start_ref[pair, which, piece].astype(F32)
                weights = descend(first, second, start)
                first = 0.9 * first + gradient
                second = 0.95 * second + gradient * gradient
                change = (start - descend(first, second, weights)) * WIRE_SCALE
                for index, out_ref in enumerate(out_refs):
                    part = out_ref.shape[-1]
                    out_ref[place, piece] = change[:, index * part : (index + 1) * part]


def inner(call, width, part, mine, banks, turned, start, first, second, products, target, count, tokens):
    slabs, pairs, cores, rows, _ = start.shape
    half, depth = banks[0].shape

    def held(step, slab):
        return jnp.where(step == 0, slab, slabs - 1)

    whole = pl.BlockSpec(memory_space=pltpu.VMEM)
    tile = (None, pairs, cores, rows, width)
    state = pl.BlockSpec(tile, lambda s, z, c: (held(s, z), 0, 0, 0, call))
    product = pl.BlockSpec((half, width), lambda s, z, c: (0, call))
    change = jax.ShapeDtypeStruct((slabs * pairs, rows, part), F32)
    outputs = 2 * (width // part)
    elements = depth * width
    return pl.pallas_call(
        functools.partial(inner_kernel, float(tokens)),
        grid_spec=pltpu.PrefetchScalarGridSpec(
            num_scalar_prefetch=1,
            grid=(2, slabs),
            in_specs=[whole] * 4
            + [
                pl.BlockSpec(tile, lambda s, z, c: (z, 0, 0, 0, call)),
                state,
                state,
                product,
                product,
                pl.BlockSpec((2 * half, width), lambda s, z, c: (0, call)),
                pl.BlockSpec(count.shape, lambda s, z, c: (0, 0, 0)),
            ],
            out_specs=[whole] * outputs,
            scratch_shapes=[
                pltpu.VMEM((slabs, pairs, cores, rows, width), F32),
                pltpu.VMEM((slabs, pairs, cores, rows, width), F32),
                pltpu.VMEM((2 * half, width), F32),
                pltpu.VMEM((2 * half, width), BF16),
                pltpu.VMEM((2, rows, width), F32),
                pltpu.VMEM((2, rows, width), BF16),
            ],
        ),
        out_shape=[change] * outputs,
        compiler_params=pltpu.CompilerParams(vmem_limit_bytes=32 * MIB),
        cost_estimate=pl.CostEstimate(
            flops=12 * half * elements,
            bytes_accessed=20 * elements,
            transcendentals=6 * elements,
        ),
        name="inner",
    )(mine, *banks, *turned, pinned(start), pinned(first), pinned(second), *products, target, count)


def assemble_kernel(begin, offsets, place_ref, *refs):
    received = refs[: len(offsets)]
    out_ref, semaphore = refs[-2:]
    width = received[0].shape[-1]
    mine = place_ref[0]
    copies = []
    for ref, group in zip(received, offsets):
        for entry, offset in enumerate(group):
            copies.append(
                pltpu.make_async_copy(
                    ref.at[entry],
                    out_ref.at[lax.bitwise_xor(mine, offset), :, pl.ds(begin, width)],
                    semaphore.at[len(copies)],
                )
            )
    for copy in copies:
        copy.start()
    for copy in copies:
        copy.wait()


def assemble(begin, place, received, offsets, shape, before):
    vmem = pl.BlockSpec(memory_space=pltpu.VMEM)
    return pl.pallas_call(
        functools.partial(assemble_kernel, begin, offsets),
        in_specs=[pl.BlockSpec(memory_space=pltpu.SMEM)]
        + [vmem] * len(received)
        + [pl.BlockSpec(memory_space=pl.ANY)] * len(before),
        out_specs=pl.BlockSpec(memory_space=pl.ANY),
        out_shape=jax.ShapeDtypeStruct(shape, BF16),
        input_output_aliases={1 + len(received): 0} if before else {},
        scratch_shapes=[pltpu.SemaphoreType.DMA((sum(map(len, offsets)),))],
        compiler_params=pltpu.CompilerParams(vmem_limit_bytes=12 * MIB),
        cost_estimate=pl.CostEstimate(
            flops=0, bytes_accessed=4 * shape[0] * shape[1] * received[0].shape[-1], transcendentals=0
        ),
        name="assemble",
    )(place, *received, *before)


def tied(first, second):
    return lax.optimization_barrier((first, second))


def per_device(sizes, global_weights, momentum, first_moment, second_moment, hidden_bank, target_bank, token_ids):
    reps, shards = sizes
    bits = reps.bit_length() - 1
    depth, columns = global_weights.shape
    rows = depth // reps
    store = hidden_bank.shape[1] * shards
    half = store // 2
    ids = token_ids[0]
    tokens = ids.shape[1]
    width = min(columns, LANES)
    chunks = columns // width
    mine = lax.axis_index("rep")

    def swapped(array, offset):
        pairs = [(index, index ^ offset) for index in range(reps)]
        return lax.ppermute(array, "rep", pairs)

    spans = [[0, 1 << bit] for bit in range(1, bits)]

    cut = (SLABS, reps // (2 * SLABS), 2, rows, columns)
    start = global_weights.reshape(cut)
    first = first_moment.reshape(cut)
    second = second_moment.reshape(cut)

    own_bank = hidden_bank[0]
    target = target_bank[0]
    count = jnp.sum(
        ids[:, :, None] == jnp.arange(store, dtype=ids.dtype)[None, None, :], axis=1
    ).astype(F32)
    if shards == 2:
        block = depth // SLABS
        parts = []
        source = own_bank
        for d in range(SLABS):
            part, source = tied(source[:, d * block : (d + 1) * block], source)
            parts.append(lax.ppermute(part, "fsdp", [(0, 1), (1, 0)]))
        own_turned, own_product = forward(own_bank, global_weights)
        joined = ()
        for d, part in enumerate(parts):
            joined = arrive(d, part, global_weights, joined)
        banks = (own_bank, joined[0])
        turned = (own_turned, joined[1])
        products = (own_product, joined[2])
        swap = lax.axis_index("fsdp") == 1
        target = jnp.where(swap, jnp.roll(target, half, axis=0), target)
        count = jnp.where(swap, jnp.roll(count, half, axis=1), count)
    else:
        whole = lax.all_gather(own_bank, "fsdp", axis=0, tiled=True)
        banks = (whole[:half], whole[half:])
        turned, products = zip(*(forward(bank, global_weights) for bank in banks))
    count = count[:, :, None]

    turned = [array.reshape(cut[:4] + (half,)) for array in turned]
    place = mine.reshape(1).astype(jnp.int32)
    if chunks == 4:
        calls = [(2 * width, width), (0, 2 * width), (3 * width, width)]
    else:
        calls = [(begin, width) for begin in range(0, columns, width)]
    begins = [begin + part for begin, wide in calls for part in range(0, wide, width)]

    def start_rows(owner):
        return lax.dynamic_slice_in_dim(global_weights, owner * rows, rows, 0)

    pair_start = jnp.stack([start_rows(mine), start_rows(mine ^ spans[-1][1])])
    shares = [
        tied(momentum[:, begin : begin + width], pair_start[:, :, begin : begin + width])
        for begin in begins
    ]

    def parted(terms, span):
        size = terms[0].shape[0] // len(span)
        parts = [[term[begin : begin + size] for term in terms] for begin in range(0, size * len(span), size)]
        outgoing = [sum(term.astype(F32) for term in part).astype(WIRE) for part in parts[1:]]
        return outgoing, parts[0]

    def sent(outgoing, span):
        return [swapped(array, offset) for array, offset in zip(outgoing, span[1:])]

    result = ()

    def chain(chunk, keep, arrived):
        terms = [keep, arrived]
        for span in spans[:-1]:
            outgoing, terms = parted(terms, span)
            outgoing = yield outgoing
            arrived = yield sent(outgoing, span)
            terms = terms + arrived
        scale = WIRE_SCALE * reps
        momentum_share, starts = shares[chunk]
        total = sum(term.astype(F32) for term in terms)
        pushed = (0.81 / 1.9 * scale) * momentum_share
        rounded = jnp.stack([total[0] + pushed, total[1]]).astype(WIRE)
        rounded = lax.optimization_barrier((yield rounded))
        arrived, = yield sent([rounded], spans[-1])
        moved = 0.9 * momentum_share + (total[0] + arrived[1].astype(F32)) * (1.0 / scale)
        both = rounded.astype(F32) + arrived[::-1].astype(F32)
        stack = (starts.astype(F32) - (1.33 / scale) * both).astype(BF16)
        offsets = list(spans[-1])
        stack = yield stack
        for span in spans[-2:0:-1]:
            arrived = yield sent([stack], span)
            offsets = [offset ^ far for far in span for offset in offsets]
            stack = yield jnp.concatenate([stack] + arrived)
        across, = yield sent([stack], spans[0])
        finished[chunk] = (moved, stack, across, offsets)
        yield ()

    finished = {}
    running = {}
    formed = {}

    def move_on(which, behind=()):
        which = [chunk for chunk in which if chunk not in finished]
        arrived = {chunk: running[chunk].send(formed[chunk]) for chunk in which}
        arrived, _ = tied(arrived, [formed[chunk] for chunk in behind])
        for chunk in which:
            formed[chunk] = running[chunk].send(arrived[chunk])

    token = place
    fresh = range(0)
    for begin, wide in calls:
        changes = inner(
            begin // wide, wide, width, token, banks, turned, start, first, second, products, target, count, tokens
        )
        sends = [send.astype(WIRE) for send in changes[::2]]
        if fresh:
            ready = range(fresh[0] + 1)
            move_on(ready)
            sends, _ = tied(sends, [formed[chunk] for chunk in ready])
        fresh = range(fresh.stop, fresh.stop + wide // width)
        for chunk, send, keep in zip(fresh, sends, changes[1::2]):
            running[chunk] = chain(chunk, keep, swapped(send, 1))
            formed[chunk] = next(running[chunk])
        if fresh.stop < chunks:
            formed, token = tied(formed, token)
    move_on(range(fresh[0]), behind=fresh)
    for chunk in range(chunks):
        while chunk not in finished:
            move_on([chunk])

    for chunk in range(chunks):
        _, stack, across, offsets = finished[chunk]
        offsets = [[offset ^ low for offset in offsets] for low in (0, 2, 1, 3)]
        if result:
            across, *result = tied(across, result[0])
        received = [stack, across, swapped(stack, 1), swapped(across, 1)]
        result = (
            assemble(begins[chunk], place, received, offsets, (reps, rows, columns), result),
        )
    new_momentum = [finished[chunk][0] for chunk in sorted(range(chunks), key=begins.__getitem__)]

    return result[0].reshape(depth, columns), jnp.concatenate(new_momentum, axis=1)


def solution(mesh):
    sizes = (mesh.shape["rep"], mesh.shape["fsdp"])
    return jax.shard_map(
        functools.partial(per_device, sizes),
        mesh=mesh,
        in_specs=(
            P(None, "fsdp"),
            P("rep", "fsdp"),
            P("rep", None, "fsdp"),
            P("rep", None, "fsdp"),
            P("rep", "fsdp", None),
            P("rep", None, "fsdp"),
            P("rep", None, None),
        ),
        out_specs=(P(None, "fsdp"), P("rep", "fsdp")),
        check_vma=False,
    )
```

```python
import functools
import math
import jax
import jax.numpy as jnp
from jax import lax
from jax.experimental import pallas as pl
from jax.experimental.pallas import tpu as pltpu
from jax.sharding import PartitionSpec as P

F32 = jnp.float32
BF16 = jnp.bfloat16
WIRE = jnp.float16
WIRE_SCALE = 64.0
LANES = 128
SLABS = 4
PIECE = 4096
MIB = 1024 * 1024


def forward_kernel(part_ref, weights_ref, turned_ref, product_ref):
    @pl.when(pl.program_id(0) == 0)
    def _():
        product_ref[...] = jnp.zeros_like(product_ref)

    part = part_ref[...]
    turned_ref[...] = part.T
    product_ref[...] += jnp.dot(part, weights_ref[...], preferred_element_type=F32)


def forward(part, weights):
    rows, depth = part.shape
    columns = weights.shape[1]
    block = depth // SLABS
    return pl.pallas_call(
        forward_kernel,
        grid=(SLABS,),
        in_specs=[
            pl.BlockSpec((rows, block), lambda d: (0, d)),
            pl.BlockSpec((block, columns), lambda d: (d, 0)),
        ],
        out_specs=[
            pl.BlockSpec((block, rows), lambda d: (d, 0)),
            pl.BlockSpec((rows, columns), lambda d: (0, 0)),
        ],
        out_shape=[
            jax.ShapeDtypeStruct((depth, rows), BF16),
            jax.ShapeDtypeStruct((rows, columns), F32),
        ],
        compiler_params=pltpu.CompilerParams(vmem_limit_bytes=14 * MIB),
        cost_estimate=pl.CostEstimate(
            flops=2 * rows * depth * columns,
            bytes_accessed=2 * depth * columns + 4 * rows * depth,
            transcendentals=0,
        ),
        name="forward",
    )(part, pinned(weights))


def arrive_kernel(piece, part_ref, weights_ref, *refs):
    natural_ref, turned_ref, product_ref = refs[-3:]
    block = part_ref.shape[1]
    place = pl.ds(piece * block, block)
    part = part_ref[...]
    natural_ref[:, place] = part
    turned_ref[place, :] = part.T
    product = jnp.dot(part, weights_ref[...], preferred_element_type=F32)
    if len(refs) > 3:
        product = product + refs[2][...]
    product_ref[...] = product


def arrive(piece, part, weights, before):
    rows, block = part.shape
    depth, columns = weights.shape
    whole = pl.BlockSpec(memory_space=pltpu.VMEM)
    return pl.pallas_call(
        functools.partial(arrive_kernel, piece),
        grid=(1,),
        in_specs=[whole, pl.BlockSpec((block, columns), lambda d: (piece, 0))]
        + [whole] * len(before),
        out_specs=[whole] * 3,
        out_shape=[
            jax.ShapeDtypeStruct((rows, depth), BF16),
            jax.ShapeDtypeStruct((depth, rows), BF16),
            jax.ShapeDtypeStruct((rows, columns), F32),
        ],
        input_output_aliases={2: 0, 3: 1, 4: 2} if before else {},
        compiler_params=pltpu.CompilerParams(vmem_limit_bytes=10 * MIB),
        cost_estimate=pl.CostEstimate(
            flops=2 * rows * block * columns,
            bytes_accessed=2 * block * columns + 6 * rows * block,
            transcendentals=0,
        ),
        name="arrive",
    )(part, pinned(weights), *before)


def pinned(array):
    return pltpu.with_memory_space_constraint(array, pltpu.HBM)


def changed_place(mine, slab, pair, pairs):
    offset = lax.bitwise_xor(slab * pairs + pair, mine // 2)
    bits = (SLABS * pairs).bit_length() - 1
    place = jnp.int32(0)
    for bit in range(bits):
        place = place * 2 + lax.rem(lax.shift_right_logical(offset, bit), 2)
    return place


def inner_kernel(
    tokens,
    mine_ref,
    low_ref,
    high_ref,
    low_turned_ref,
    high_turned_ref,
    start_ref,
    first_ref,
    second_ref,
    low_product_ref,
    high_product_ref,
    target_ref,
    count_ref,
    *rest,
):
    *change_refs, first_state, second_state, output_state, residual_state, gradient_state, rounded_state = rest
    send_refs, keep_refs = change_refs[::2], change_refs[1::2]
    step = pl.program_id(0)
    slab = pl.program_id(1)
    pairs, cores, rows, _ = start_ref.shape
    mine = mine_ref[0]
    core = lax.rem(mine, cores)
    height = PIECE // start_ref.shape[-1]
    pieces = [pl.ds(begin, height) for begin in range(0, rows, height)]
    slots = [(slot, *divmod(slot, cores)) for slot in range(pairs * cores)]
    held = gradient_state.shape[0]

    def weigh(output, which):
        residual = ((output - target_ref[...].astype(F32)) / tokens).astype(BF16)
        residual_state[...] = (residual.astype(F32) * count_ref[which]).astype(BF16)

    def descend(first, second, weights):
        root = second * lax.rsqrt(second)
        below = (100.0 * math.sqrt(0.05)) * root + 1e-06
        return 0.99 * weights - first * lax.rsqrt(below * below)

    def differentiate(pair, which, slot):
        turned = jnp.concatenate(
            [low_turned_ref[slab, pair, which], high_turned_ref[slab, pair, which]], axis=1
        )
        gradient_state[slot % held] = jnp.dot(
            turned, residual_state[...], preferred_element_type=F32
        )

    def project(slot):
        begin = (slab * pairs * cores + slot) * rows
        place = pl.ds(pl.multiple_of(begin, rows), rows)
        picked = jnp.concatenate([low_ref[:, place], high_ref[:, place]], axis=0)
        return jnp.dot(picked, rounded_state[slot % held], preferred_element_type=F32)

    @pl.when((step == 0) & (slab == 0))
    def _():
        weigh(jnp.concatenate([low_product_ref[...], high_product_ref[...]], axis=0), 0)
        output_state[...] = jnp.zeros_like(output_state)

    @pl.when((step == 1) & (slab == 0))
    def _():
        weigh(output_state[...], 1)

    @pl.when(step == 0)
    def _():
        differentiate(0, 0, 0)
        for slot, pair, which in slots:
            if slot + 1 < len(slots):
                ahead, *place = slots[slot + 1]
                differentiate(*place, ahead)
            for piece in pieces:
                gradient = gradient_state[slot % held, piece]
                first = 9.0 * first_ref[pair, which, piece] + gradient
                second = 19.0 * second_ref[pair, which, piece] + gradient * gradient
                weights = descend(first, second, start_ref[pair, which, piece].astype(F32))
                first_state[slab, pair, which, piece] = first
                second_state[slab, pair, which, piece] = second
                rounded_state[slot % held, piece] = weights.astype(BF16)
            output_state[...] += project(slot)

    @pl.when(step == 1)
    def _():
        sides = ((1 - core, send_refs), (core, keep_refs))
        differentiate(0, sides[0][0], 0)
        for slot, pair, side in slots:
            if slot + 1 < len(slots):
                ahead, next_pair, next_side = slots[slot + 1]
                differentiate(next_pair, sides[next_side][0], ahead)
            which, out_refs = sides[side]
            place = changed_place(mine, slab, pair, pairs)
            for piece in pieces:
                gradient = gradient_state[slot % held, piece]
                first = first_state[slab, pair, which, piece]
                second = second_state[slab, pair, which, piece]
                start = start_ref[pair, which, piece].astype(F32)
                weights = descend(first, second, start)
                first = 0.9 * first + gradient
                second = 0.95 * second + gradient * gradient
                change = (start - descend(first, second, weights)) * WIRE_SCALE
                for index, out_ref in enumerate(out_refs):
                    part = out_ref.shape[-1]
                    out_ref[place, piece] = change[:, index * part : (index + 1) * part]


def inner(call, width, part, mine, banks, turned, start, first, second, products, target, count, tokens):
    slabs, pairs, cores, rows, _ = start.shape
    half, depth = banks[0].shape

    def held(step, slab):
        return jnp.where(step == 0, slab, slabs - 1)

    whole = pl.BlockSpec(memory_space=pltpu.VMEM)
    tile = (None, pairs, cores, rows, width)
    state = pl.BlockSpec(tile, lambda s, z, c: (held(s, z), 0, 0, 0, call))
    product = pl.BlockSpec((half, width), lambda s, z, c: (0, call))
    change = jax.ShapeDtypeStruct((slabs * pairs, rows, part), F32)
    outputs = 2 * (width // part)
    elements = depth * width
    return pl.pallas_call(
        functools.partial(inner_kernel, float(tokens)),
        grid_spec=pltpu.PrefetchScalarGridSpec(
            num_scalar_prefetch=1,
            grid=(2, slabs),
            in_specs=[whole] * 4
            + [
                pl.BlockSpec(tile, lambda s, z, c: (z, 0, 0, 0, call)),
                state,
                state,
                product,
                product,
                pl.BlockSpec((2 * half, width), lambda s, z, c: (0, call)),
                pl.BlockSpec(count.shape, lambda s, z, c: (0, 0, 0)),
            ],
            out_specs=[whole] * outputs,
            scratch_shapes=[
                pltpu.VMEM((slabs, pairs, cores, rows, width), F32),
                pltpu.VMEM((slabs, pairs, cores, rows, width), F32),
                pltpu.VMEM((2 * half, width), F32),
                pltpu.VMEM((2 * half, width), BF16),
                pltpu.VMEM((2, rows, width), F32),
                pltpu.VMEM((2, rows, width), BF16),
            ],
        ),
        out_shape=[change] * outputs,
        compiler_params=pltpu.CompilerParams(vmem_limit_bytes=32 * MIB),
        cost_estimate=pl.CostEstimate(
            flops=12 * half * elements,
            bytes_accessed=20 * elements,
            transcendentals=6 * elements,
        ),
        name="inner",
    )(mine, *banks, *turned, pinned(start), pinned(first), pinned(second), *products, target, count)


def assemble_kernel(begin, offsets, place_ref, *refs):
    received = refs[: len(offsets)]
    out_ref, semaphore = refs[-2:]
    width = received[0].shape[-1]
    mine = place_ref[0]
    copies = []
    for ref, group in zip(received, offsets):
        for entry, offset in enumerate(group):
            copies.append(
                pltpu.make_async_copy(
                    ref.at[entry],
                    out_ref.at[lax.bitwise_xor(mine, offset), :, pl.ds(begin, width)],
                    semaphore.at[len(copies)],
                )
            )
    for copy in copies:
        copy.start()
    for copy in copies:
        copy.wait()


def assemble(begin, place, received, offsets, shape, before):
    vmem = pl.BlockSpec(memory_space=pltpu.VMEM)
    return pl.pallas_call(
        functools.partial(assemble_kernel, begin, offsets),
        in_specs=[pl.BlockSpec(memory_space=pltpu.SMEM)]
        + [vmem] * len(received)
        + [pl.BlockSpec(memory_space=pl.ANY)] * len(before),
        out_specs=pl.BlockSpec(memory_space=pl.ANY),
        out_shape=jax.ShapeDtypeStruct(shape, BF16),
        input_output_aliases={1 + len(received): 0} if before else {},
        scratch_shapes=[pltpu.SemaphoreType.DMA((sum(map(len, offsets)),))],
        compiler_params=pltpu.CompilerParams(vmem_limit_bytes=12 * MIB),
        cost_estimate=pl.CostEstimate(
            flops=0, bytes_accessed=4 * shape[0] * shape[1] * received[0].shape[-1], transcendentals=0
        ),
        name="assemble",
    )(place, *received, *before)


def tied(first, second):
    return lax.optimization_barrier((first, second))


def per_device(sizes, global_weights, momentum, first_moment, second_moment, hidden_bank, target_bank, token_ids):
    reps, shards = sizes
    bits = reps.bit_length() - 1
    depth, columns = global_weights.shape
    rows = depth // reps
    store = hidden_bank.shape[1] * shards
    half = store // 2
    ids = token_ids[0]
    tokens = ids.shape[1]
    width = min(columns, LANES)
    chunks = columns // width
    mine = lax.axis_index("rep")

    def swapped(array, offset):
        pairs = [(index, index ^ offset) for index in range(reps)]
        return lax.ppermute(array, "rep", pairs)

    spans = [[0, 1 << bit] for bit in range(1, bits)]

    cut = (SLABS, reps // (2 * SLABS), 2, rows, columns)
    start = global_weights.reshape(cut)
    first = first_moment.reshape(cut)
    second = second_moment.reshape(cut)

    own_bank = hidden_bank[0]
    target = target_bank[0]
    count = jnp.sum(
        ids[:, :, None] == jnp.arange(store, dtype=ids.dtype)[None, None, :], axis=1
    ).astype(F32)
    if shards == 2:
        block = depth // SLABS
        parts = []
        source = own_bank
        for d in range(SLABS):
            part, source = tied(source[:, d * block : (d + 1) * block], source)
            parts.append(lax.ppermute(part, "fsdp", [(0, 1), (1, 0)]))
        own_turned, own_product = forward(own_bank, global_weights)
        joined = ()
        for d, part in enumerate(parts):
            joined = arrive(d, part, global_weights, joined)
        banks = (own_bank, joined[0])
        turned = (own_turned, joined[1])
        products = (own_product, joined[2])
        swap = lax.axis_index("fsdp") == 1
        target = jnp.where(swap, jnp.roll(target, half, axis=0), target)
        count = jnp.where(swap, jnp.roll(count, half, axis=1), count)
    else:
        whole = lax.all_gather(own_bank, "fsdp", axis=0, tiled=True)
        banks = (whole[:half], whole[half:])
        turned, products = zip(*(forward(bank, global_weights) for bank in banks))
    count = count[:, :, None]

    turned = [array.reshape(cut[:4] + (half,)) for array in turned]
    place = mine.reshape(1).astype(jnp.int32)
    if chunks == 4:
        calls = [(0, 2 * width), (2 * width, width), (3 * width, width)]
    else:
        calls = [(begin, width) for begin in range(0, columns, width)]
    begins = [begin + part for begin, wide in calls for part in range(0, wide, width)]

    def start_rows(owner):
        return lax.dynamic_slice_in_dim(global_weights, owner * rows, rows, 0)

    pair_start = jnp.stack([start_rows(mine), start_rows(mine ^ spans[-1][1])])
    shares = [
        tied(momentum[:, begin : begin + width], pair_start[:, :, begin : begin + width])
        for begin in begins
    ]

    def parted(terms, span):
        size = terms[0].shape[0] // len(span)
        parts = [[term[begin : begin + size] for term in terms] for begin in range(0, size * len(span), size)]
        outgoing = [sum(term.astype(F32) for term in part).astype(WIRE) for part in parts[1:]]
        return outgoing, parts[0]

    def sent(outgoing, span):
        return [swapped(array, offset) for array, offset in zip(outgoing, span[1:])]

    result = ()

    def chain(chunk, keep, arrived):
        terms = [keep, arrived]
        for span in spans[:-1]:
            outgoing, terms = parted(terms, span)
            outgoing = yield outgoing
            arrived = yield sent(outgoing, span)
            terms = terms + arrived
        scale = WIRE_SCALE * reps
        momentum_share, starts = shares[chunk]
        total = sum(term.astype(F32) for term in terms)
        pushed = (0.81 / 1.9 * scale) * momentum_share
        rounded = jnp.stack([total[0] + pushed, total[1]]).astype(WIRE)
        rounded = lax.optimization_barrier((yield rounded))
        arrived, = yield sent([rounded], spans[-1])
        moved = 0.9 * momentum_share + (total[0] + arrived[1].astype(F32)) * (1.0 / scale)
        both = rounded.astype(F32) + arrived[::-1].astype(F32)
        stack = (starts.astype(F32) - (1.33 / scale) * both).astype(BF16)
        offsets = list(spans[-1])
        stack = yield stack
        for span in spans[-2:0:-1]:
            arrived = yield sent([stack], span)
            offsets = [offset ^ far for far in span for offset in offsets]
            stack = yield jnp.concatenate([stack] + arrived)
        across, = yield sent([stack], spans[0])
        finished[chunk] = (moved, stack, across, offsets)
        yield ()

    finished = {}
    running = {}
    formed = {}

    def move_on(which, behind=()):
        which = [chunk for chunk in which if chunk not in finished]
        arrived = {chunk: running[chunk].send(formed[chunk]) for chunk in which}
        arrived, _ = tied(arrived, [formed[chunk] for chunk in behind])
        for chunk in which:
            formed[chunk] = running[chunk].send(arrived[chunk])

    token = place
    fresh = range(0)
    for begin, wide in calls:
        changes = inner(
            begin // wide, wide, width, token, banks, turned, start, first, second, products, target, count, tokens
        )
        sends = [send.astype(WIRE) for send in changes[::2]]
        if fresh:
            ready = range(fresh[0] + 1)
            move_on(ready)
            sends, _ = tied(sends, [formed[chunk] for chunk in ready])
        fresh = range(fresh.stop, fresh.stop + wide // width)
        for chunk, send, keep in zip(fresh, sends, changes[1::2]):
            running[chunk] = chain(chunk, keep, swapped(send, 1))
            formed[chunk] = next(running[chunk])
        if fresh.stop < chunks:
            formed, token = tied(formed, token)
    move_on(range(fresh[0]), behind=fresh)
    move_on(fresh, behind=range(fresh[0]))
    move_on(range(fresh[0])[:1], behind=fresh)
    for chunk in range(chunks):
        while chunk not in finished:
            move_on([chunk])

    for chunk in range(chunks):
        _, stack, across, offsets = finished[chunk]
        offsets = [[offset ^ low for offset in offsets] for low in (0, 2, 1, 3)]
        if result and chunk + 1 < chunks:
            across, *result = tied(across, result[0])
        received = [stack, across, swapped(stack, 1), swapped(across, 1)]
        result = (
            assemble(begins[chunk], place, received, offsets, (reps, rows, columns), result),
        )
    new_momentum = [finished[chunk][0] for chunk in sorted(range(chunks), key=begins.__getitem__)]

    return result[0].reshape(depth, columns), jnp.concatenate(new_momentum, axis=1)


def solution(mesh):
    sizes = (mesh.shape["rep"], mesh.shape["fsdp"])
    return jax.shard_map(
        functools.partial(per_device, sizes),
        mesh=mesh,
        in_specs=(
            P(None, "fsdp"),
            P("rep", "fsdp"),
            P("rep", None, "fsdp"),
            P("rep", None, "fsdp"),
            P("rep", "fsdp", None),
            P("rep", None, "fsdp"),
            P("rep", None, None),
        ),
        out_specs=(P(None, "fsdp"), P("rep", "fsdp")),
        check_vma=False,
    )
```

```python
import functools
import math
import jax
import jax.numpy as jnp
from jax import lax
from jax.experimental import pallas as pl
from jax.experimental.pallas import tpu as pltpu
from jax.sharding import PartitionSpec as P

F32 = jnp.float32
BF16 = jnp.bfloat16
WIRE = jnp.float16
WIRE_SCALE = 64.0
LANES = 128
SLABS = 4
PIECE = 8192
MIB = 1024 * 1024


def forward_kernel(part_ref, weights_ref, turned_ref, product_ref):
    @pl.when(pl.program_id(0) == 0)
    def _():
        product_ref[...] = jnp.zeros_like(product_ref)

    part = part_ref[...]
    turned_ref[...] = part.T
    product_ref[...] += jnp.dot(part, weights_ref[...], preferred_element_type=F32)


def forward(part, weights):
    rows, depth = part.shape
    columns = weights.shape[1]
    block = depth // SLABS
    return pl.pallas_call(
        forward_kernel,
        grid=(SLABS,),
        in_specs=[
            pl.BlockSpec((rows, block), lambda d: (0, d)),
            pl.BlockSpec((block, columns), lambda d: (d, 0)),
        ],
        out_specs=[
            pl.BlockSpec((block, rows), lambda d: (d, 0)),
            pl.BlockSpec((rows, columns), lambda d: (0, 0)),
        ],
        out_shape=[
            jax.ShapeDtypeStruct((depth, rows), BF16),
            jax.ShapeDtypeStruct((rows, columns), F32),
        ],
        compiler_params=pltpu.CompilerParams(vmem_limit_bytes=14 * MIB),
        cost_estimate=pl.CostEstimate(
            flops=2 * rows * depth * columns,
            bytes_accessed=2 * depth * columns + 4 * rows * depth,
            transcendentals=0,
        ),
        name="forward",
    )(part, pinned(weights))


def arrive_kernel(piece, part_ref, weights_ref, *refs):
    natural_ref, turned_ref, product_ref = refs[-3:]
    block = part_ref.shape[1]
    place = pl.ds(piece * block, block)
    part = part_ref[...]
    natural_ref[:, place] = part
    turned_ref[place, :] = part.T
    product = jnp.dot(part, weights_ref[...], preferred_element_type=F32)
    if len(refs) > 3:
        product = product + refs[2][...]
    product_ref[...] = product


def arrive(piece, part, weights, before):
    rows, block = part.shape
    depth, columns = weights.shape
    whole = pl.BlockSpec(memory_space=pltpu.VMEM)
    return pl.pallas_call(
        functools.partial(arrive_kernel, piece),
        grid=(1,),
        in_specs=[whole, pl.BlockSpec((block, columns), lambda d: (piece, 0))]
        + [whole] * len(before),
        out_specs=[whole] * 3,
        out_shape=[
            jax.ShapeDtypeStruct((rows, depth), BF16),
            jax.ShapeDtypeStruct((depth, rows), BF16),
            jax.ShapeDtypeStruct((rows, columns), F32),
        ],
        input_output_aliases={2: 0, 3: 1, 4: 2} if before else {},
        compiler_params=pltpu.CompilerParams(vmem_limit_bytes=10 * MIB),
        cost_estimate=pl.CostEstimate(
            flops=2 * rows * block * columns,
            bytes_accessed=2 * block * columns + 6 * rows * block,
            transcendentals=0,
        ),
        name="arrive",
    )(part, pinned(weights), *before)


def pinned(array):
    return pltpu.with_memory_space_constraint(array, pltpu.HBM)


def changed_place(mine, slab, pair, pairs):
    offset = lax.bitwise_xor(slab * pairs + pair, mine // 2)
    bits = (SLABS * pairs).bit_length() - 1
    place = jnp.int32(0)
    for bit in range(bits):
        place = place * 2 + lax.rem(lax.shift_right_logical(offset, bit), 2)
    return place


def inner_kernel(
    tokens,
    kept,
    mine_ref,
    low_ref,
    high_ref,
    low_turned_ref,
    high_turned_ref,
    start_ref,
    first_ref,
    second_ref,
    low_product_ref,
    high_product_ref,
    target_ref,
    count_ref,
    *rest,
):
    *rest, first_state, second_state, output_state, residual_state, gradient_state, rounded_state = rest
    change_refs, weights_state = (rest[:-1], rest[-1]) if kept else (rest, None)
    send_refs, keep_refs = change_refs[::2], change_refs[1::2]
    step = pl.program_id(0)
    slab = pl.program_id(1)
    pairs, cores, rows, _ = start_ref.shape
    mine = mine_ref[0]
    core = lax.rem(mine, cores)
    height = PIECE // start_ref.shape[-1]
    pieces = [pl.ds(begin, height) for begin in range(0, rows, height)]
    slots = [(slot, *divmod(slot, cores)) for slot in range(pairs * cores)]
    held = gradient_state.shape[0]

    def weigh(output, which):
        residual = ((output - target_ref[...].astype(F32)) / tokens).astype(BF16)
        residual_state[...] = (residual.astype(F32) * count_ref[which]).astype(BF16)

    def descend(first, second, weights):
        root = second * lax.rsqrt(second)
        below = (100.0 * math.sqrt(0.05)) * root + 1e-06
        return 0.99 * weights - first * lax.rsqrt(below * below)

    def differentiate(pair, which, slot):
        turned = jnp.concatenate(
            [low_turned_ref[slab, pair, which], high_turned_ref[slab, pair, which]], axis=1
        )
        gradient_state[slot % held] = jnp.dot(
            turned, residual_state[...], preferred_element_type=F32
        )

    def project(slot):
        begin = (slab * pairs * cores + slot) * rows
        place = pl.ds(pl.multiple_of(begin, rows), rows)
        picked = jnp.concatenate([low_ref[:, place], high_ref[:, place]], axis=0)
        return jnp.dot(picked, rounded_state[slot % held], preferred_element_type=F32)

    @pl.when((step == 0) & (slab == 0))
    def _():
        weigh(jnp.concatenate([low_product_ref[...], high_product_ref[...]], axis=0), 0)
        output_state[...] = jnp.zeros_like(output_state)

    @pl.when((step == 1) & (slab == 0))
    def _():
        weigh(output_state[...], 1)

    @pl.when(step == 0)
    def _():
        differentiate(0, 0, 0)
        for slot, pair, which in slots:
            if slot + 1 < len(slots):
                ahead, *place = slots[slot + 1]
                differentiate(*place, ahead)
            for piece in pieces:
                gradient = gradient_state[slot % held, piece]
                first = 9.0 * first_ref[pair, which, piece] + gradient
                second = 19.0 * second_ref[pair, which, piece] + gradient * gradient
                weights = descend(first, second, start_ref[pair, which, piece].astype(F32))
                first_state[slab, pair, which, piece] = first
                second_state[slab, pair, which, piece] = second
                if kept:
                    weights_state[slab, pair, which, piece] = weights
                rounded_state[slot % held, piece] = weights.astype(BF16)
            output_state[...] += project(slot)

    @pl.when(step == 1)
    def _():
        sides = ((1 - core, send_refs), (core, keep_refs))
        differentiate(0, sides[0][0], 0)
        for slot, pair, side in slots:
            if slot + 1 < len(slots):
                ahead, next_pair, next_side = slots[slot + 1]
                differentiate(next_pair, sides[next_side][0], ahead)
            which, out_refs = sides[side]
            place = changed_place(mine, slab, pair, pairs)
            for piece in pieces:
                gradient = gradient_state[slot % held, piece]
                first = first_state[slab, pair, which, piece]
                second = second_state[slab, pair, which, piece]
                start = start_ref[pair, which, piece].astype(F32)
                if kept:
                    weights = weights_state[slab, pair, which, piece]
                else:
                    weights = descend(first, second, start)
                first = 0.9 * first + gradient
                second = 0.95 * second + gradient * gradient
                change = (start - descend(first, second, weights)) * WIRE_SCALE
                for index, out_ref in enumerate(out_refs):
                    part = out_ref.shape[-1]
                    out_ref[place, piece] = change[:, index * part : (index + 1) * part]


def inner(call, width, part, mine, banks, turned, start, first, second, products, target, count, tokens):
    slabs, pairs, cores, rows, _ = start.shape
    half, depth = banks[0].shape

    def held(step, slab):
        return jnp.where(step == 0, slab, slabs - 1)

    whole = pl.BlockSpec(memory_space=pltpu.VMEM)
    tile = (None, pairs, cores, rows, width)
    state = pl.BlockSpec(tile, lambda s, z, c: (held(s, z), 0, 0, 0, call))
    product = pl.BlockSpec((half, width), lambda s, z, c: (0, call))
    change = jax.ShapeDtypeStruct((slabs * pairs, rows, part), F32)
    outputs = 2 * (width // part)
    kept = width == part
    elements = depth * width
    return pl.pallas_call(
        functools.partial(inner_kernel, float(tokens), kept),
        grid_spec=pltpu.PrefetchScalarGridSpec(
            num_scalar_prefetch=1,
            grid=(2, slabs),
            in_specs=[whole] * 4
            + [
                pl.BlockSpec(tile, lambda s, z, c: (z, 0, 0, 0, call)),
                state,
                state,
                product,
                product,
                pl.BlockSpec((2 * half, width), lambda s, z, c: (0, call)),
                pl.BlockSpec(count.shape, lambda s, z, c: (0, 0, 0)),
            ],
            out_specs=[whole] * outputs,
            scratch_shapes=[pltpu.VMEM((slabs, pairs, cores, rows, width), F32)] * (2 + kept)
            + [
                pltpu.VMEM((2 * half, width), F32),
                pltpu.VMEM((2 * half, width), BF16),
                pltpu.VMEM((2, rows, width), F32),
                pltpu.VMEM((2, rows, width), BF16),
            ],
        ),
        out_shape=[change] * outputs,
        compiler_params=pltpu.CompilerParams(vmem_limit_bytes=32 * MIB),
        cost_estimate=pl.CostEstimate(
            flops=12 * half * elements,
            bytes_accessed=20 * elements,
            transcendentals=6 * elements,
        ),
        name="inner",
    )(mine, *banks, *turned, pinned(start), pinned(first), pinned(second), *products, target, count)


def assemble_kernel(begin, offsets, place_ref, *refs):
    received = refs[: len(offsets)]
    out_ref, semaphore = refs[-2:]
    width = received[0].shape[-1]
    mine = place_ref[0]
    copies = []
    for ref, group in zip(received, offsets):
        for entry, offset in enumerate(group):
            copies.append(
                pltpu.make_async_copy(
                    ref.at[entry],
                    out_ref.at[lax.bitwise_xor(mine, offset), :, pl.ds(begin, width)],
                    semaphore.at[len(copies)],
                )
            )
    for copy in copies:
        copy.start()
    for copy in copies:
        copy.wait()


def assemble(begin, place, received, offsets, shape, before):
    vmem = pl.BlockSpec(memory_space=pltpu.VMEM)
    return pl.pallas_call(
        functools.partial(assemble_kernel, begin, offsets),
        in_specs=[pl.BlockSpec(memory_space=pltpu.SMEM)]
        + [vmem] * len(received)
        + [pl.BlockSpec(memory_space=pl.ANY)] * len(before),
        out_specs=pl.BlockSpec(memory_space=pl.ANY),
        out_shape=jax.ShapeDtypeStruct(shape, BF16),
        input_output_aliases={1 + len(received): 0} if before else {},
        scratch_shapes=[pltpu.SemaphoreType.DMA((sum(map(len, offsets)),))],
        compiler_params=pltpu.CompilerParams(vmem_limit_bytes=12 * MIB),
        cost_estimate=pl.CostEstimate(
            flops=0, bytes_accessed=4 * shape[0] * shape[1] * received[0].shape[-1], transcendentals=0
        ),
        name="assemble",
    )(place, *received, *before)


def tied(first, second):
    return lax.optimization_barrier((first, second))


def per_device(sizes, global_weights, momentum, first_moment, second_moment, hidden_bank, target_bank, token_ids):
    reps, shards = sizes
    bits = reps.bit_length() - 1
    depth, columns = global_weights.shape
    rows = depth // reps
    store = hidden_bank.shape[1] * shards
    half = store // 2
    ids = token_ids[0]
    tokens = ids.shape[1]
    width = min(columns, LANES)
    chunks = columns // width
    mine = lax.axis_index("rep")

    def swapped(array, offset):
        pairs = [(index, index ^ offset) for index in range(reps)]
        return lax.ppermute(array, "rep", pairs)

    spans = [[0, 1 << bit] for bit in range(1, bits)]

    cut = (SLABS, reps // (2 * SLABS), 2, rows, columns)
    start = global_weights.reshape(cut)
    first = first_moment.reshape(cut)
    second = second_moment.reshape(cut)

    own_bank = hidden_bank[0]
    target = target_bank[0]
    count = jnp.sum(
        ids[:, :, None] == jnp.arange(store, dtype=ids.dtype)[None, None, :], axis=1
    ).astype(F32)
    if shards == 2:
        block = depth // SLABS
        parts = []
        source = own_bank
        for d in range(SLABS):
            part, source = tied(source[:, d * block : (d + 1) * block], source)
            parts.append(lax.ppermute(part, "fsdp", [(0, 1), (1, 0)]))
        own_turned, own_product = forward(own_bank, global_weights)
        joined = ()
        for d, part in enumerate(parts):
            joined = arrive(d, part, global_weights, joined)
        banks = (own_bank, joined[0])
        turned = (own_turned, joined[1])
        products = (own_product, joined[2])
        swap = lax.axis_index("fsdp") == 1
        target = jnp.where(swap, jnp.roll(target, half, axis=0), target)
        count = jnp.where(swap, jnp.roll(count, half, axis=1), count)
    else:
        whole = lax.all_gather(own_bank, "fsdp", axis=0, tiled=True)
        banks = (whole[:half], whole[half:])
        turned, products = zip(*(forward(bank, global_weights) for bank in banks))
    count = count[:, :, None]

    turned = [array.reshape(cut[:4] + (half,)) for array in turned]
    place = mine.reshape(1).astype(jnp.int32)
    if chunks == 4:
        calls = [(2 * width, width), (0, 2 * width), (3 * width, width)]
    else:
        calls = [(begin, width) for begin in range(0, columns, width)]
    begins = [begin + part for begin, wide in calls for part in range(0, wide, width)]

    def start_rows(owner):
        return lax.dynamic_slice_in_dim(global_weights, owner * rows, rows, 0)

    pair_start = jnp.stack([start_rows(mine), start_rows(mine ^ spans[-1][1])])
    shares = [
        tied(momentum[:, begin : begin + width], pair_start[:, :, begin : begin + width])
        for begin in begins
    ]

    def parted(terms, span):
        size = terms[0].shape[0] // len(span)
        parts = [[term[begin : begin + size] for term in terms] for begin in range(0, size * len(span), size)]
        outgoing = [sum(term.astype(F32) for term in part).astype(WIRE) for part in parts[1:]]
        return outgoing, parts[0]

    def sent(outgoing, span):
        return [swapped(array, offset) for array, offset in zip(outgoing, span[1:])]

    result = ()

    def chain(chunk, keep, arrived):
        terms = [keep, arrived]
        for span in spans[:-1]:
            outgoing, terms = parted(terms, span)
            outgoing = yield outgoing
            arrived = yield sent(outgoing, span)
            terms = terms + arrived
        scale = WIRE_SCALE * reps
        momentum_share, starts = shares[chunk]
        total = sum(term.astype(F32) for term in terms)
        pushed = (0.81 / 1.9 * scale) * momentum_share
        rounded = jnp.stack([total[0] + pushed, total[1]]).astype(WIRE)
        rounded = lax.optimization_barrier((yield rounded))
        arrived, = yield sent([rounded], spans[-1])
        moved = 0.9 * momentum_share + (total[0] + arrived[1].astype(F32)) * (1.0 / scale)
        both = rounded.astype(F32) + arrived[::-1].astype(F32)
        stack = (starts.astype(F32) - (1.33 / scale) * both).astype(BF16)
        offsets = list(spans[-1])
        stack = yield stack
        for span in spans[-2:0:-1]:
            arrived = yield sent([stack], span)
            offsets = [offset ^ far for far in span for offset in offsets]
            stack = yield jnp.concatenate([stack] + arrived)
        across, = yield sent([stack], spans[0])
        finished[chunk] = (moved, stack, across, offsets)
        yield ()

    finished = {}
    running = {}
    formed = {}

    def move_on(which, behind=()):
        which = [chunk for chunk in which if chunk not in finished]
        arrived = {chunk: running[chunk].send(formed[chunk]) for chunk in which}
        arrived, _ = tied(arrived, [formed[chunk] for chunk in behind])
        for chunk in which:
            formed[chunk] = running[chunk].send(arrived[chunk])

    token = place
    fresh = range(0)
    for begin, wide in calls:
        changes = inner(
            begin // wide, wide, width, token, banks, turned, start, first, second, products, target, count, tokens
        )
        sends = [send.astype(WIRE) for send in changes[::2]]
        if fresh:
            ready = range(fresh[0] + 1)
            move_on(ready)
            sends, _ = tied(sends, [formed[chunk] for chunk in ready])
        fresh = range(fresh.stop, fresh.stop + wide // width)
        for chunk, send, keep in zip(fresh, sends, changes[1::2]):
            running[chunk] = chain(chunk, keep, swapped(send, 1))
            formed[chunk] = next(running[chunk])
        if fresh.stop < chunks:
            formed, token = tied(formed, token)
    others = range(fresh[0])
    move_on(others, behind=fresh)
    move_on(fresh, behind=others)
    move_on(others, behind=fresh)
    for chunk in range(chunks):
        while chunk not in finished:
            move_on([chunk])

    for chunk in range(chunks):
        _, stack, across, offsets = finished[chunk]
        offsets = [[offset ^ low for offset in offsets] for low in (0, 2, 1, 3)]
        if result and chunk + 1 < chunks:
            across, *result = tied(across, result[0])
        received = [stack, across, swapped(stack, 1), swapped(across, 1)]
        result = (
            assemble(begins[chunk], place, received, offsets, (reps, rows, columns), result),
        )
    new_momentum = [finished[chunk][0] for chunk in sorted(range(chunks), key=begins.__getitem__)]

    return result[0].reshape(depth, columns), jnp.concatenate(new_momentum, axis=1)


def solution(mesh):
    sizes = (mesh.shape["rep"], mesh.shape["fsdp"])
    return jax.shard_map(
        functools.partial(per_device, sizes),
        mesh=mesh,
        in_specs=(
            P(None, "fsdp"),
            P("rep", "fsdp"),
            P("rep", None, "fsdp"),
            P("rep", None, "fsdp"),
            P("rep", "fsdp", None),
            P("rep", None, "fsdp"),
            P("rep", None, None),
        ),
        out_specs=(P(None, "fsdp"), P("rep", "fsdp")),
        check_vma=False,
    )
```

```python
import functools
import math
import jax
import jax.numpy as jnp
from jax import lax
from jax.experimental import pallas as pl
from jax.experimental.pallas import tpu as pltpu
from jax.sharding import PartitionSpec as P

F32 = jnp.float32
BF16 = jnp.bfloat16
WIRE = jnp.float16
WIRE_SCALE = 64.0
LANES = 128
SLABS = 4
PIECE = 8192
MIB = 1024 * 1024


def forward_kernel(part_ref, weights_ref, turned_ref, product_ref):
    @pl.when(pl.program_id(0) == 0)
    def _():
        product_ref[...] = jnp.zeros_like(product_ref)

    part = part_ref[...]
    turned_ref[...] = part.T
    product_ref[...] += jnp.dot(part, weights_ref[...], preferred_element_type=F32)


def forward(part, weights):
    rows, depth = part.shape
    columns = weights.shape[1]
    block = depth // SLABS
    return pl.pallas_call(
        forward_kernel,
        grid=(SLABS,),
        in_specs=[
            pl.BlockSpec((rows, block), lambda d: (0, d)),
            pl.BlockSpec((block, columns), lambda d: (d, 0)),
        ],
        out_specs=[
            pl.BlockSpec((block, rows), lambda d: (d, 0)),
            pl.BlockSpec((rows, columns), lambda d: (0, 0)),
        ],
        out_shape=[
            jax.ShapeDtypeStruct((depth, rows), BF16),
            jax.ShapeDtypeStruct((rows, columns), F32),
        ],
        compiler_params=pltpu.CompilerParams(vmem_limit_bytes=14 * MIB),
        cost_estimate=pl.CostEstimate(
            flops=2 * rows * depth * columns,
            bytes_accessed=2 * depth * columns + 4 * rows * depth,
            transcendentals=0,
        ),
        name="forward",
    )(part, pinned(weights))


def arrive_kernel(piece, part_ref, weights_ref, *refs):
    natural_ref, turned_ref, product_ref = refs[-3:]
    block = part_ref.shape[1]
    place = pl.ds(piece * block, block)
    part = part_ref[...]
    natural_ref[:, place] = part
    turned_ref[place, :] = part.T
    product = jnp.dot(part, weights_ref[...], preferred_element_type=F32)
    if len(refs) > 3:
        product = product + refs[2][...]
    product_ref[...] = product


def arrive(piece, part, weights, before):
    rows, block = part.shape
    depth, columns = weights.shape
    whole = pl.BlockSpec(memory_space=pltpu.VMEM)
    return pl.pallas_call(
        functools.partial(arrive_kernel, piece),
        grid=(1,),
        in_specs=[whole, pl.BlockSpec((block, columns), lambda d: (piece, 0))]
        + [whole] * len(before),
        out_specs=[whole] * 3,
        out_shape=[
            jax.ShapeDtypeStruct((rows, depth), BF16),
            jax.ShapeDtypeStruct((depth, rows), BF16),
            jax.ShapeDtypeStruct((rows, columns), F32),
        ],
        input_output_aliases={2: 0, 3: 1, 4: 2} if before else {},
        compiler_params=pltpu.CompilerParams(vmem_limit_bytes=10 * MIB),
        cost_estimate=pl.CostEstimate(
            flops=2 * rows * block * columns,
            bytes_accessed=2 * block * columns + 6 * rows * block,
            transcendentals=0,
        ),
        name="arrive",
    )(part, pinned(weights), *before)


def pinned(array):
    return pltpu.with_memory_space_constraint(array, pltpu.HBM)


def changed_place(mine, slab, pair, pairs):
    offset = lax.bitwise_xor(slab * pairs + pair, mine // 2)
    bits = (SLABS * pairs).bit_length() - 1
    place = jnp.int32(0)
    for bit in range(bits):
        place = place * 2 + lax.rem(lax.shift_right_logical(offset, bit), 2)
    return place


def inner_kernel(
    tokens,
    kept,
    mine_ref,
    low_ref,
    high_ref,
    low_turned_ref,
    high_turned_ref,
    start_ref,
    first_ref,
    second_ref,
    low_product_ref,
    high_product_ref,
    target_ref,
    count_ref,
    *rest,
):
    *rest, first_state, second_state, output_state, residual_state, gradient_state, rounded_state = rest
    change_refs, weights_state = (rest[:-1], rest[-1]) if kept else (rest, None)
    send_refs, keep_refs = change_refs[::2], change_refs[1::2]
    step = pl.program_id(0)
    slab = pl.program_id(1)
    pairs, cores, rows, _ = start_ref.shape
    mine = mine_ref[0]
    core = lax.rem(mine, cores)
    height = PIECE // start_ref.shape[-1]
    pieces = [pl.ds(begin, height) for begin in range(0, rows, height)]
    slots = [(slot, *divmod(slot, cores)) for slot in range(pairs * cores)]
    held = gradient_state.shape[0]

    def weigh(output, which):
        residual = ((output - target_ref[...].astype(F32)) / tokens).astype(BF16)
        residual_state[...] = (residual.astype(F32) * count_ref[which]).astype(BF16)

    def descend(first, second, weights):
        root = second * lax.rsqrt(second)
        below = (100.0 * math.sqrt(0.05)) * root + 1e-06
        return 0.99 * weights - first * lax.rsqrt(below * below)

    def differentiate(pair, which, slot):
        turned = jnp.concatenate(
            [low_turned_ref[slab, pair, which], high_turned_ref[slab, pair, which]], axis=1
        )
        gradient_state[slot % held] = jnp.dot(
            turned, residual_state[...], preferred_element_type=F32
        )

    def project(slot):
        begin = (slab * pairs * cores + slot) * rows
        place = pl.ds(pl.multiple_of(begin, rows), rows)
        picked = jnp.concatenate([low_ref[:, place], high_ref[:, place]], axis=0)
        return jnp.dot(picked, rounded_state[slot % held], preferred_element_type=F32)

    @pl.when((step == 0) & (slab == 0))
    def _():
        weigh(jnp.concatenate([low_product_ref[...], high_product_ref[...]], axis=0), 0)
        output_state[...] = jnp.zeros_like(output_state)

    @pl.when((step == 1) & (slab == 0))
    def _():
        weigh(output_state[...], 1)

    @pl.when(step == 0)
    def _():
        differentiate(0, 0, 0)
        for slot, pair, which in slots:
            if slot + 1 < len(slots):
                ahead, *place = slots[slot + 1]
                differentiate(*place, ahead)
            for piece in pieces:
                gradient = gradient_state[slot % held, piece]
                first = 9.0 * first_ref[pair, which, piece] + gradient
                second = 19.0 * second_ref[pair, which, piece] + gradient * gradient
                weights = descend(first, second, start_ref[pair, which, piece].astype(F32))
                first_state[slab, pair, which, piece] = first
                second_state[slab, pair, which, piece] = second
                if kept:
                    weights_state[slab, pair, which, piece] = weights
                rounded_state[slot % held, piece] = weights.astype(BF16)
            output_state[...] += project(slot)

    @pl.when(step == 1)
    def _():
        sides = ((1 - core, send_refs), (core, keep_refs))
        differentiate(0, sides[0][0], 0)
        for slot, pair, side in slots:
            if slot + 1 < len(slots):
                ahead, next_pair, next_side = slots[slot + 1]
                differentiate(next_pair, sides[next_side][0], ahead)
            which, out_refs = sides[side]
            place = changed_place(mine, slab, pair, pairs)
            for piece in pieces:
                gradient = gradient_state[slot % held, piece]
                first = first_state[slab, pair, which, piece]
                second = second_state[slab, pair, which, piece]
                start = start_ref[pair, which, piece].astype(F32)
                if kept:
                    weights = weights_state[slab, pair, which, piece]
                else:
                    weights = descend(first, second, start)
                first = 0.9 * first + gradient
                second = 0.95 * second + gradient * gradient
                change = (start - descend(first, second, weights)) * WIRE_SCALE
                for index, out_ref in enumerate(out_refs):
                    part = out_ref.shape[-1]
                    out_ref[place, piece] = change[:, index * part : (index + 1) * part]


def inner(call, width, part, mine, banks, turned, start, first, second, products, target, count, tokens):
    slabs, pairs, cores, rows, _ = start.shape
    half, depth = banks[0].shape

    def held(step, slab):
        return jnp.where(step == 0, slab, slabs - 1)

    whole = pl.BlockSpec(memory_space=pltpu.VMEM)
    tile = (None, pairs, cores, rows, width)
    state = pl.BlockSpec(tile, lambda s, z, c: (held(s, z), 0, 0, 0, call))
    product = pl.BlockSpec((half, width), lambda s, z, c: (0, call))
    change = jax.ShapeDtypeStruct((slabs * pairs, rows, part), F32)
    outputs = 2 * (width // part)
    kept = width == part
    elements = depth * width
    return pl.pallas_call(
        functools.partial(inner_kernel, float(tokens), kept),
        grid_spec=pltpu.PrefetchScalarGridSpec(
            num_scalar_prefetch=1,
            grid=(2, slabs),
            in_specs=[whole] * 4
            + [
                pl.BlockSpec(tile, lambda s, z, c: (z, 0, 0, 0, call)),
                state,
                state,
                product,
                product,
                pl.BlockSpec((2 * half, width), lambda s, z, c: (0, call)),
                pl.BlockSpec(count.shape, lambda s, z, c: (0, 0, 0)),
            ],
            out_specs=[whole] * outputs,
            scratch_shapes=[pltpu.VMEM((slabs, pairs, cores, rows, width), F32)] * (2 + kept)
            + [
                pltpu.VMEM((2 * half, width), F32),
                pltpu.VMEM((2 * half, width), BF16),
                pltpu.VMEM((2, rows, width), F32),
                pltpu.VMEM((2, rows, width), BF16),
            ],
        ),
        out_shape=[change] * outputs,
        compiler_params=pltpu.CompilerParams(vmem_limit_bytes=32 * MIB),
        cost_estimate=pl.CostEstimate(
            flops=12 * half * elements,
            bytes_accessed=20 * elements,
            transcendentals=6 * elements,
        ),
        name="inner",
    )(mine, *banks, *turned, pinned(start), pinned(first), pinned(second), *products, target, count)


def assemble_kernel(begin, offsets, place_ref, *refs):
    received = refs[: len(offsets)]
    out_ref, semaphore = refs[-2:]
    width = received[0].shape[-1]
    mine = place_ref[0]
    copies = []
    for ref, group in zip(received, offsets):
        for entry, offset in enumerate(group):
            copies.append(
                pltpu.make_async_copy(
                    ref.at[entry],
                    out_ref.at[lax.bitwise_xor(mine, offset), :, pl.ds(begin, width)],
                    semaphore.at[len(copies)],
                )
            )
    for copy in copies:
        copy.start()
    for copy in copies:
        copy.wait()


def assemble(begin, place, received, offsets, shape, before):
    vmem = pl.BlockSpec(memory_space=pltpu.VMEM)
    return pl.pallas_call(
        functools.partial(assemble_kernel, begin, offsets),
        in_specs=[pl.BlockSpec(memory_space=pltpu.SMEM)]
        + [vmem] * len(received)
        + [pl.BlockSpec(memory_space=pl.ANY)] * len(before),
        out_specs=pl.BlockSpec(memory_space=pl.ANY),
        out_shape=jax.ShapeDtypeStruct(shape, BF16),
        input_output_aliases={1 + len(received): 0} if before else {},
        scratch_shapes=[pltpu.SemaphoreType.DMA((sum(map(len, offsets)),))],
        compiler_params=pltpu.CompilerParams(vmem_limit_bytes=12 * MIB),
        cost_estimate=pl.CostEstimate(
            flops=0, bytes_accessed=4 * shape[0] * shape[1] * received[0].shape[-1], transcendentals=0
        ),
        name="assemble",
    )(place, *received, *before)


def tied(first, second):
    return lax.optimization_barrier((first, second))


def per_device(sizes, global_weights, momentum, first_moment, second_moment, hidden_bank, target_bank, token_ids):
    reps, shards = sizes
    bits = reps.bit_length() - 1
    depth, columns = global_weights.shape
    rows = depth // reps
    store = hidden_bank.shape[1] * shards
    half = store // 2
    ids = token_ids[0]
    tokens = ids.shape[1]
    width = min(columns, LANES)
    chunks = columns // width
    mine = lax.axis_index("rep")

    def swapped(array, offset):
        pairs = [(index, index ^ offset) for index in range(reps)]
        return lax.ppermute(array, "rep", pairs)

    spans = [[0, 1 << bit] for bit in range(1, bits)]

    cut = (SLABS, reps // (2 * SLABS), 2, rows, columns)
    start = global_weights.reshape(cut)
    first = first_moment.reshape(cut)
    second = second_moment.reshape(cut)

    own_bank = hidden_bank[0]
    target = target_bank[0]
    count = jnp.sum(
        ids[:, :, None] == jnp.arange(store, dtype=ids.dtype)[None, None, :], axis=1
    ).astype(F32)
    if shards == 2:
        block = depth // SLABS
        parts = []
        source = own_bank
        for d in range(SLABS):
            part, source = tied(source[:, d * block : (d + 1) * block], source)
            parts.append(lax.ppermute(part, "fsdp", [(0, 1), (1, 0)]))
        own_turned, own_product = forward(own_bank, global_weights)
        joined = ()
        for d, part in enumerate(parts):
            joined = arrive(d, part, global_weights, joined)
        banks = (own_bank, joined[0])
        turned = (own_turned, joined[1])
        products = (own_product, joined[2])
        swap = lax.axis_index("fsdp") == 1
        target = jnp.where(swap, jnp.roll(target, half, axis=0), target)
        count = jnp.where(swap, jnp.roll(count, half, axis=1), count)
    else:
        whole = lax.all_gather(own_bank, "fsdp", axis=0, tiled=True)
        banks = (whole[:half], whole[half:])
        turned, products = zip(*(forward(bank, global_weights) for bank in banks))
    count = count[:, :, None]

    turned = [array.reshape(cut[:4] + (half,)) for array in turned]
    place = mine.reshape(1).astype(jnp.int32)
    if chunks == 4:
        calls = [(2 * width, width), (0, 2 * width), (3 * width, width)]
    else:
        calls = [(begin, width) for begin in range(0, columns, width)]
    begins = [begin + part for begin, wide in calls for part in range(0, wide, width)]

    def start_rows(owner):
        return lax.dynamic_slice_in_dim(global_weights, owner * rows, rows, 0)

    pair_start = jnp.stack([start_rows(mine), start_rows(mine ^ spans[-1][1])])
    shares = [
        tied(momentum[:, begin : begin + width], pair_start[:, :, begin : begin + width])
        for begin in begins
    ]

    def parted(terms, span):
        size = terms[0].shape[0] // len(span)
        parts = [[term[begin : begin + size] for term in terms] for begin in range(0, size * len(span), size)]
        outgoing = [sum(term.astype(F32) for term in part).astype(WIRE) for part in parts[1:]]
        return outgoing, parts[0]

    def sent(outgoing, span):
        return [swapped(array, offset) for array, offset in zip(outgoing, span[1:])]

    result = ()

    def chain(chunk, keep, arrived):
        terms = [keep, arrived]
        for span in spans[:-1]:
            outgoing, terms = parted(terms, span)
            outgoing = yield outgoing
            arrived = yield sent(outgoing, span)
            terms = terms + arrived
        scale = WIRE_SCALE * reps
        momentum_share, starts = shares[chunk]
        total = sum(term.astype(F32) for term in terms)
        pushed = (0.81 / 1.9 * scale) * momentum_share
        rounded = jnp.stack([total[0] + pushed, total[1]]).astype(WIRE)
        rounded = lax.optimization_barrier((yield rounded))
        arrived, = yield sent([rounded], spans[-1])
        moved = 0.9 * momentum_share + (total[0] + arrived[1].astype(F32)) * (1.0 / scale)
        both = rounded.astype(F32) + arrived[::-1].astype(F32)
        stack = (starts.astype(F32) - (1.33 / scale) * both).astype(BF16)
        offsets = list(spans[-1])
        stack = yield stack
        back = spans[-2::-1] if chunk + 1 < chunks or chunks == 1 else spans[:-1]
        for span in back[:-1]:
            arrived = yield sent([stack], span)
            offsets = [offset ^ far for far in span for offset in offsets]
            stack = yield jnp.concatenate([stack] + arrived)
        across, = yield sent([stack], back[-1])
        ends = [0, back[-1][1], 1, back[-1][1] ^ 1]
        finished[chunk] = (moved, stack, across, [[offset ^ end for offset in offsets] for end in ends])
        yield ()

    finished = {}
    running = {}
    formed = {}

    def move_on(which, behind=()):
        which = [chunk for chunk in which if chunk not in finished]
        arrived = {chunk: running[chunk].send(formed[chunk]) for chunk in which}
        arrived, _ = tied(arrived, [formed[chunk] for chunk in behind])
        for chunk in which:
            formed[chunk] = running[chunk].send(arrived[chunk])

    token = place
    fresh = range(0)
    for begin, wide in calls:
        changes = inner(
            begin // wide, wide, width, token, banks, turned, start, first, second, products, target, count, tokens
        )
        sends = [send.astype(WIRE) for send in changes[::2]]
        if fresh:
            move_on(range(fresh[0] + 1))
            sends, _ = tied(sends, [formed[chunk] for chunk in range(fresh.stop)])
        fresh = range(fresh.stop, fresh.stop + wide // width)
        for chunk, send, keep in zip(fresh, sends, changes[1::2]):
            running[chunk] = chain(chunk, keep, swapped(send, 1))
            formed[chunk] = next(running[chunk])
        if fresh.stop < chunks:
            early = {chunk: formed[chunk] for chunk in range(fresh[0] + 1)}
            early, token = tied(early, token)
            formed.update(early)
    if chunks == 4:
        move_on([0], behind=[3])
        move_on([1, 2], behind=[0])
        move_on([3], behind=[1, 2])
        move_on([0], behind=[3])
        move_on([1, 2], behind=[0])
    for chunk in range(chunks):
        while chunk not in finished:
            move_on([chunk])

    for chunk in range(chunks):
        _, stack, across, offsets = finished[chunk]
        if result and chunk + 1 < chunks:
            across, *result = tied(across, result[0])
        received = [stack, across, swapped(stack, 1), swapped(across, 1)]
        result = (
            assemble(begins[chunk], place, received, offsets, (reps, rows, columns), result),
        )
    new_momentum = [finished[chunk][0] for chunk in sorted(range(chunks), key=begins.__getitem__)]

    return result[0].reshape(depth, columns), jnp.concatenate(new_momentum, axis=1)


def solution(mesh):
    sizes = (mesh.shape["rep"], mesh.shape["fsdp"])
    return jax.shard_map(
        functools.partial(per_device, sizes),
        mesh=mesh,
        in_specs=(
            P(None, "fsdp"),
            P("rep", "fsdp"),
            P("rep", None, "fsdp"),
            P("rep", None, "fsdp"),
            P("rep", "fsdp", None),
            P("rep", None, "fsdp"),
            P("rep", None, None),
        ),
        out_specs=(P(None, "fsdp"), P("rep", "fsdp")),
        check_vma=False,
    )
```

```python
import functools
import math
import jax
import jax.numpy as jnp
from jax import lax
from jax.experimental import pallas as pl
from jax.experimental.pallas import tpu as pltpu
from jax.sharding import PartitionSpec as P

F32 = jnp.float32
BF16 = jnp.bfloat16
WIRE = jnp.float16
WIRE_SCALE = 64.0
LANES = 128
SLABS = 4
PIECE = 8192
MIB = 1024 * 1024


def forward_kernel(part_ref, weights_ref, turned_ref, product_ref):
    @pl.when(pl.program_id(0) == 0)
    def _():
        product_ref[...] = jnp.zeros_like(product_ref)

    part = part_ref[...]
    turned_ref[...] = part.T
    product_ref[...] += jnp.dot(part, weights_ref[...], preferred_element_type=F32)


def forward(part, weights):
    rows, depth = part.shape
    columns = weights.shape[1]
    block = depth // SLABS
    return pl.pallas_call(
        forward_kernel,
        grid=(SLABS,),
        in_specs=[
            pl.BlockSpec((rows, block), lambda d: (0, d)),
            pl.BlockSpec((block, columns), lambda d: (d, 0)),
        ],
        out_specs=[
            pl.BlockSpec((block, rows), lambda d: (d, 0)),
            pl.BlockSpec((rows, columns), lambda d: (0, 0)),
        ],
        out_shape=[
            jax.ShapeDtypeStruct((depth, rows), BF16),
            jax.ShapeDtypeStruct((rows, columns), F32),
        ],
        compiler_params=pltpu.CompilerParams(vmem_limit_bytes=14 * MIB),
        cost_estimate=pl.CostEstimate(
            flops=2 * rows * depth * columns,
            bytes_accessed=2 * depth * columns + 4 * rows * depth,
            transcendentals=0,
        ),
        name="forward",
    )(part, pinned(weights))


def arrive_kernel(piece, part_ref, weights_ref, *refs):
    natural_ref, turned_ref, product_ref = refs[-3:]
    block = part_ref.shape[1]
    place = pl.ds(piece * block, block)
    part = part_ref[...]
    natural_ref[:, place] = part
    turned_ref[place, :] = part.T
    product = jnp.dot(part, weights_ref[...], preferred_element_type=F32)
    if len(refs) > 3:
        product = product + refs[2][...]
    product_ref[...] = product


def arrive(piece, part, weights, before):
    rows, block = part.shape
    depth, columns = weights.shape
    whole = pl.BlockSpec(memory_space=pltpu.VMEM)
    return pl.pallas_call(
        functools.partial(arrive_kernel, piece),
        grid=(1,),
        in_specs=[whole, pl.BlockSpec((block, columns), lambda d: (piece, 0))]
        + [whole] * len(before),
        out_specs=[whole] * 3,
        out_shape=[
            jax.ShapeDtypeStruct((rows, depth), BF16),
            jax.ShapeDtypeStruct((depth, rows), BF16),
            jax.ShapeDtypeStruct((rows, columns), F32),
        ],
        input_output_aliases={2: 0, 3: 1, 4: 2} if before else {},
        compiler_params=pltpu.CompilerParams(vmem_limit_bytes=10 * MIB),
        cost_estimate=pl.CostEstimate(
            flops=2 * rows * block * columns,
            bytes_accessed=2 * block * columns + 6 * rows * block,
            transcendentals=0,
        ),
        name="arrive",
    )(part, pinned(weights), *before)


def pinned(array):
    return pltpu.with_memory_space_constraint(array, pltpu.HBM)


def changed_place(mine, slab, pair, pairs):
    offset = lax.bitwise_xor(slab * pairs + pair, mine // 2)
    bits = (SLABS * pairs).bit_length() - 1
    place = jnp.int32(0)
    for bit in range(bits):
        place = place * 2 + lax.rem(lax.shift_right_logical(offset, bit), 2)
    return place


def inner_kernel(
    tokens,
    kept,
    mine_ref,
    low_ref,
    high_ref,
    low_turned_ref,
    high_turned_ref,
    start_ref,
    first_ref,
    second_ref,
    low_product_ref,
    high_product_ref,
    target_ref,
    count_ref,
    *rest,
):
    *rest, first_state, second_state, output_state, residual_state, gradient_state, rounded_state = rest
    change_refs, weights_state = (rest[:-1], rest[-1]) if kept else (rest, None)
    send_refs, keep_refs = change_refs[::2], change_refs[1::2]
    step = pl.program_id(0)
    slab = pl.program_id(1)
    pairs, cores, rows, _ = start_ref.shape
    mine = mine_ref[0]
    core = lax.rem(mine, cores)
    height = PIECE // start_ref.shape[-1]
    pieces = [pl.ds(begin, height) for begin in range(0, rows, height)]
    slots = [(slot, *divmod(slot, cores)) for slot in range(pairs * cores)]
    held = gradient_state.shape[0]

    def weigh(output, which):
        residual = ((output - target_ref[...].astype(F32)) / tokens).astype(BF16)
        residual_state[...] = (residual.astype(F32) * count_ref[which]).astype(BF16)

    def descend(first, second, weights):
        root = second * lax.rsqrt(second)
        below = (100.0 * math.sqrt(0.05)) * root + 1e-06
        return 0.99 * weights - first * lax.rsqrt(below * below)

    def differentiate(pair, which, slot):
        turned = jnp.concatenate(
            [low_turned_ref[slab, pair, which], high_turned_ref[slab, pair, which]], axis=1
        )
        gradient_state[slot % held] = jnp.dot(
            turned, residual_state[...], preferred_element_type=F32
        )

    def project(slot):
        begin = (slab * pairs * cores + slot) * rows
        place = pl.ds(pl.multiple_of(begin, rows), rows)
        picked = jnp.concatenate([low_ref[:, place], high_ref[:, place]], axis=0)
        return jnp.dot(picked, rounded_state[slot % held], preferred_element_type=F32)

    @pl.when((step == 0) & (slab == 0))
    def _():
        weigh(jnp.concatenate([low_product_ref[...], high_product_ref[...]], axis=0), 0)
        output_state[...] = jnp.zeros_like(output_state)

    @pl.when((step == 1) & (slab == 0))
    def _():
        weigh(output_state[...], 1)

    @pl.when(step == 0)
    def _():
        differentiate(0, 0, 0)
        for slot, pair, which in slots:
            if slot + 1 < len(slots):
                ahead, *place = slots[slot + 1]
                differentiate(*place, ahead)
            for piece in pieces:
                gradient = gradient_state[slot % held, piece]
                first = 9.0 * first_ref[pair, which, piece] + gradient
                second = 19.0 * second_ref[pair, which, piece] + gradient * gradient
                weights = descend(first, second, start_ref[pair, which, piece].astype(F32))
                first_state[slab, pair, which, piece] = first
                second_state[slab, pair, which, piece] = second
                if kept:
                    weights_state[slab, pair, which, piece] = weights
                rounded_state[slot % held, piece] = weights.astype(BF16)
            output_state[...] += project(slot)

    @pl.when(step == 1)
    def _():
        sides = ((1 - core, send_refs), (core, keep_refs))
        differentiate(0, sides[0][0], 0)
        for slot, pair, side in slots:
            if slot + 1 < len(slots):
                ahead, next_pair, next_side = slots[slot + 1]
                differentiate(next_pair, sides[next_side][0], ahead)
            which, out_refs = sides[side]
            place = changed_place(mine, slab, pair, pairs)
            for piece in pieces:
                gradient = gradient_state[slot % held, piece]
                first = first_state[slab, pair, which, piece]
                second = second_state[slab, pair, which, piece]
                start = start_ref[pair, which, piece].astype(F32)
                if kept:
                    weights = weights_state[slab, pair, which, piece]
                else:
                    weights = descend(first, second, start)
                first = 0.9 * first + gradient
                second = 0.95 * second + gradient * gradient
                change = (start - descend(first, second, weights)) * WIRE_SCALE
                for index, out_ref in enumerate(out_refs):
                    part = out_ref.shape[-1]
                    out_ref[place, piece] = change[:, index * part : (index + 1) * part]


def inner(call, width, part, mine, banks, turned, start, first, second, products, target, count, tokens):
    slabs, pairs, cores, rows, _ = start.shape
    half, depth = banks[0].shape

    def held(step, slab):
        return jnp.where(step == 0, slab, slabs - 1)

    whole = pl.BlockSpec(memory_space=pltpu.VMEM)
    tile = (None, pairs, cores, rows, width)
    state = pl.BlockSpec(tile, lambda s, z, c: (held(s, z), 0, 0, 0, call))
    product = pl.BlockSpec((half, width), lambda s, z, c: (0, call))
    change = jax.ShapeDtypeStruct((slabs * pairs, rows, part), F32)
    outputs = 2 * (width // part)
    kept = width == part
    elements = depth * width
    return pl.pallas_call(
        functools.partial(inner_kernel, float(tokens), kept),
        grid_spec=pltpu.PrefetchScalarGridSpec(
            num_scalar_prefetch=1,
            grid=(2, slabs),
            in_specs=[whole] * 4
            + [
                pl.BlockSpec(tile, lambda s, z, c: (z, 0, 0, 0, call)),
                state,
                state,
                product,
                product,
                pl.BlockSpec((2 * half, width), lambda s, z, c: (0, call)),
                pl.BlockSpec(count.shape, lambda s, z, c: (0, 0, 0)),
            ],
            out_specs=[whole] * outputs,
            scratch_shapes=[pltpu.VMEM((slabs, pairs, cores, rows, width), F32)] * (2 + kept)
            + [
                pltpu.VMEM((2 * half, width), F32),
                pltpu.VMEM((2 * half, width), BF16),
                pltpu.VMEM((2, rows, width), F32),
                pltpu.VMEM((2, rows, width), BF16),
            ],
        ),
        out_shape=[change] * outputs,
        compiler_params=pltpu.CompilerParams(vmem_limit_bytes=32 * MIB),
        cost_estimate=pl.CostEstimate(
            flops=12 * half * elements,
            bytes_accessed=20 * elements,
            transcendentals=6 * elements,
        ),
        name="inner",
    )(mine, *banks, *turned, pinned(start), pinned(first), pinned(second), *products, target, count)


def assemble_kernel(begins, offsets, place_ref, *refs):
    out_ref, semaphore = refs[-2:]
    width = refs[0].shape[-1]
    mine = place_ref[0]
    copies = []
    for ref, begin, group in zip(refs, begins, offsets):
        for entry, offset in enumerate(group):
            copies.append(
                pltpu.make_async_copy(
                    ref.at[entry],
                    out_ref.at[lax.bitwise_xor(mine, offset), :, pl.ds(begin, width)],
                    semaphore.at[len(copies)],
                )
            )
    for copy in copies:
        copy.start()
    for copy in copies:
        copy.wait()


def assemble(place, blocks, shape, before):
    begins, received, offsets = zip(*blocks)
    vmem = pl.BlockSpec(memory_space=pltpu.VMEM)
    return pl.pallas_call(
        functools.partial(assemble_kernel, begins, offsets),
        in_specs=[pl.BlockSpec(memory_space=pltpu.SMEM)]
        + [vmem] * len(received)
        + [pl.BlockSpec(memory_space=pl.ANY)] * len(before),
        out_specs=pl.BlockSpec(memory_space=pl.ANY),
        out_shape=jax.ShapeDtypeStruct(shape, BF16),
        input_output_aliases={1 + len(received): 0} if before else {},
        scratch_shapes=[pltpu.SemaphoreType.DMA((sum(map(len, offsets)),))],
        compiler_params=pltpu.CompilerParams(vmem_limit_bytes=12 * MIB),
        cost_estimate=pl.CostEstimate(
            flops=0, bytes_accessed=4 * sum(array.size for array in received), transcendentals=0
        ),
        name="assemble",
    )(place, *received, *before)


def tied(first, second):
    return lax.optimization_barrier((first, second))


def per_device(sizes, global_weights, momentum, first_moment, second_moment, hidden_bank, target_bank, token_ids):
    reps, shards = sizes
    bits = reps.bit_length() - 1
    depth, columns = global_weights.shape
    rows = depth // reps
    store = hidden_bank.shape[1] * shards
    half = store // 2
    ids = token_ids[0]
    tokens = ids.shape[1]
    width = min(columns, LANES)
    chunks = columns // width
    mine = lax.axis_index("rep")

    def swapped(array, offset):
        pairs = [(index, index ^ offset) for index in range(reps)]
        return lax.ppermute(array, "rep", pairs)

    spans = [[0, 1 << bit] for bit in range(1, bits)]

    cut = (SLABS, reps // (2 * SLABS), 2, rows, columns)
    start = global_weights.reshape(cut)
    first = first_moment.reshape(cut)
    second = second_moment.reshape(cut)

    own_bank = hidden_bank[0]
    target = target_bank[0]
    count = jnp.sum(
        ids[:, :, None] == jnp.arange(store, dtype=ids.dtype)[None, None, :], axis=1
    ).astype(F32)
    if shards == 2:
        block = depth // SLABS
        parts = []
        source = own_bank
        for d in range(SLABS):
            part, source = tied(source[:, d * block : (d + 1) * block], source)
            parts.append(lax.ppermute(part, "fsdp", [(0, 1), (1, 0)]))
        own_turned, own_product = forward(own_bank, global_weights)
        joined = ()
        for d, part in enumerate(parts):
            joined = arrive(d, part, global_weights, joined)
        banks = (own_bank, joined[0])
        turned = (own_turned, joined[1])
        products = (own_product, joined[2])
        swap = lax.axis_index("fsdp") == 1
        target = jnp.where(swap, jnp.roll(target, half, axis=0), target)
        count = jnp.where(swap, jnp.roll(count, half, axis=1), count)
    else:
        whole = lax.all_gather(own_bank, "fsdp", axis=0, tiled=True)
        banks = (whole[:half], whole[half:])
        turned, products = zip(*(forward(bank, global_weights) for bank in banks))
    count = count[:, :, None]

    turned = [array.reshape(cut[:4] + (half,)) for array in turned]
    place = mine.reshape(1).astype(jnp.int32)
    if chunks == 4:
        calls = [(2 * width, width), (0, 2 * width), (3 * width, width)]
    else:
        calls = [(begin, width) for begin in range(0, columns, width)]
    begins = [begin + part for begin, wide in calls for part in range(0, wide, width)]

    def start_rows(owner):
        return lax.dynamic_slice_in_dim(global_weights, owner * rows, rows, 0)

    pair_start = jnp.stack([start_rows(mine), start_rows(mine ^ spans[-1][1])])
    shares = [
        tied(momentum[:, begin : begin + width], pair_start[:, :, begin : begin + width])
        for begin in begins
    ]

    def parted(terms, span):
        size = terms[0].shape[0] // len(span)
        parts = [[term[begin : begin + size] for term in terms] for begin in range(0, size * len(span), size)]
        outgoing = [sum(term.astype(F32) for term in part).astype(WIRE) for part in parts[1:]]
        return outgoing, parts[0]

    def sent(outgoing, span):
        return [swapped(array, offset) for array, offset in zip(outgoing, span[1:])]

    result = ()

    def chain(chunk, keep, arrived):
        terms = [keep, arrived]
        for span in spans[:-1]:
            outgoing, terms = parted(terms, span)
            outgoing = yield outgoing
            arrived = yield sent(outgoing, span)
            terms = terms + arrived
        scale = WIRE_SCALE * reps
        momentum_share, starts = shares[chunk]
        total = sum(term.astype(F32) for term in terms)
        pushed = (0.81 / 1.9 * scale) * momentum_share
        rounded = jnp.stack([total[0] + pushed, total[1]]).astype(WIRE)
        rounded = lax.optimization_barrier((yield rounded))
        arrived, = yield sent([rounded], spans[-1])
        moved = 0.9 * momentum_share + (total[0] + arrived[1].astype(F32)) * (1.0 / scale)
        both = rounded.astype(F32) + arrived[::-1].astype(F32)
        stack = (starts.astype(F32) - (1.33 / scale) * both).astype(BF16)
        offsets = list(spans[-1])
        stack = yield stack
        back = spans[-2::-1] if chunk + 1 < chunks or chunks == 1 else spans[:-1]
        for span in back[:-1]:
            arrived = yield sent([stack], span)
            offsets = [offset ^ far for far in span for offset in offsets]
            stack = yield jnp.concatenate([stack] + arrived)
        across, = yield sent([stack], back[-1])
        ends = [0, back[-1][1], 1, back[-1][1] ^ 1]
        finished[chunk] = (moved, stack, across, [[offset ^ end for offset in offsets] for end in ends])
        yield ()

    finished = {}
    running = {}
    formed = {}

    def move_on(which, behind=()):
        which = [chunk for chunk in which if chunk not in finished]
        arrived = {chunk: running[chunk].send(formed[chunk]) for chunk in which}
        arrived, _ = tied(arrived, [formed[chunk] for chunk in behind])
        for chunk in which:
            formed[chunk] = running[chunk].send(arrived[chunk])

    token = place
    fresh = range(0)
    later = {}
    for begin, wide in calls:
        changes = inner(
            begin // wide, wide, width, token, banks, turned, start, first, second, products, target, count, tokens
        )
        sends = [send.astype(WIRE) for send in changes[::2]]
        if fresh:
            move_on(range(fresh[0] + 1))
            for chunk in fresh[1:]:
                keep, arrived = later.pop(chunk)
                arrived, _ = tied(arrived, [formed[other] for other in range(fresh[0] + 1)])
                running[chunk] = chain(chunk, keep, arrived)
                formed[chunk] = next(running[chunk])
            sends, _ = tied(sends, [formed[chunk] for chunk in range(fresh.stop)])
        fresh = range(fresh.stop, fresh.stop + wide // width)
        for chunk, send, keep in zip(fresh, sends, changes[1::2]):
            later[chunk] = (keep, swapped(send, 1))
        running[fresh[0]] = chain(fresh[0], *later.pop(fresh[0]))
        formed[fresh[0]] = next(running[fresh[0]])
        if fresh.stop < chunks:
            formed, token = tied(formed, token)
    if chunks == 4:
        before = 3
        for which in (1, 0, 2, 3, 0, 1, 2):
            move_on([which], behind=[before])
            before = which
    for chunk in range(chunks):
        while chunk not in finished:
            move_on([chunk])

    blocks = []
    for chunk in range(chunks):
        _, stack, across, offsets = finished[chunk]
        if chunk == 1 and result:
            across, *result = tied(across, result[0])
        received = [stack, across, swapped(stack, 1), swapped(across, 1)]
        blocks += [(begins[chunk], array, group) for array, group in zip(received, offsets)]
        if chunk + 2 != chunks:
            result = (assemble(place, blocks, (reps, rows, columns), result),)
            blocks = []

    new_momentum = [finished[chunk][0] for chunk in sorted(range(chunks), key=begins.__getitem__)]

    return result[0].reshape(depth, columns), jnp.concatenate(new_momentum, axis=1)


def solution(mesh):
    sizes = (mesh.shape["rep"], mesh.shape["fsdp"])
    return jax.shard_map(
        functools.partial(per_device, sizes),
        mesh=mesh,
        in_specs=(
            P(None, "fsdp"),
            P("rep", "fsdp"),
            P("rep", None, "fsdp"),
            P("rep", None, "fsdp"),
            P("rep", "fsdp", None),
            P("rep", None, "fsdp"),
            P("rep", None, None),
        ),
        out_specs=(P(None, "fsdp"), P("rep", "fsdp")),
        check_vma=False,
    )
```

```python
import functools
import math
import jax
import jax.numpy as jnp
from jax import lax
from jax.experimental import pallas as pl
from jax.experimental.pallas import tpu as pltpu
from jax.sharding import PartitionSpec as P

F32 = jnp.float32
BF16 = jnp.bfloat16
WIRE = jnp.float16
WIRE_SCALE = 64.0
LANES = 128
SLABS = 4
PIECE = 8192
MIB = 1024 * 1024


def forward_kernel(part_ref, weights_ref, turned_ref, product_ref):
    depth = part_ref.shape[1]
    block = depth // SLABS
    product = jnp.zeros(product_ref.shape, F32)
    for begin in range(0, depth, block):
        place = pl.ds(begin, block)
        part = part_ref[:, place]
        product += jnp.dot(part, weights_ref[place, :], preferred_element_type=F32)
        turned_ref[place, :] = part.T
    product_ref[...] = product


def forward(part, weights):
    rows, depth = part.shape
    columns = weights.shape[1]
    vmem = pl.BlockSpec(memory_space=pltpu.VMEM)
    return pl.pallas_call(
        forward_kernel,
        in_specs=[vmem, vmem],
        out_specs=[vmem, vmem],
        out_shape=[
            jax.ShapeDtypeStruct((depth, rows), BF16),
            jax.ShapeDtypeStruct((rows, columns), F32),
        ],
        compiler_params=pltpu.CompilerParams(vmem_limit_bytes=8 * MIB),
        cost_estimate=pl.CostEstimate(
            flops=2 * rows * depth * columns,
            bytes_accessed=2 * depth * columns + 4 * rows * depth,
            transcendentals=0,
        ),
        name="forward",
    )(part, weights)


def pinned(array):
    return pltpu.with_memory_space_constraint(array, pltpu.HBM)


def changed_place(mine, slab, pair, pairs):
    offset = lax.bitwise_xor(slab * pairs + pair, mine // 2)
    bits = (SLABS * pairs).bit_length() - 1
    place = jnp.int32(0)
    for bit in range(bits):
        place = place * 2 + lax.rem(lax.shift_right_logical(offset, bit), 2)
    return place


def inner_kernel(
    tokens,
    kept,
    mine_ref,
    low_ref,
    high_ref,
    low_turned_ref,
    high_turned_ref,
    start_ref,
    first_ref,
    second_ref,
    low_product_ref,
    high_product_ref,
    target_ref,
    count_ref,
    *rest,
):
    *rest, first_state, second_state, output_state, residual_state, gradient_state, rounded_state = rest
    change_refs, weights_state = (rest[:-1], rest[-1]) if kept else (rest, None)
    send_refs, keep_refs = change_refs[::2], change_refs[1::2]
    step = pl.program_id(0)
    slab = pl.program_id(1)
    pairs, cores, rows, _ = start_ref.shape
    mine = mine_ref[0]
    core = lax.rem(mine, cores)
    height = PIECE // start_ref.shape[-1]
    pieces = [pl.ds(begin, height) for begin in range(0, rows, height)]
    slots = [(slot, *divmod(slot, cores)) for slot in range(pairs * cores)]
    held = gradient_state.shape[0]

    def weigh(output, which):
        residual = ((output - target_ref[...].astype(F32)) / tokens).astype(BF16)
        residual_state[...] = (residual.astype(F32) * count_ref[which]).astype(BF16)

    def descend(first, second, weights):
        root = second * lax.rsqrt(second)
        below = (100.0 * math.sqrt(0.05)) * root + 1e-06
        return 0.99 * weights - first * lax.rsqrt(below * below)

    def differentiate(pair, which, slot):
        turned = jnp.concatenate(
            [low_turned_ref[slab, pair, which], high_turned_ref[slab, pair, which]], axis=1
        )
        gradient_state[slot % held] = jnp.dot(
            turned, residual_state[...], preferred_element_type=F32
        )

    def project(slot):
        begin = (slab * pairs * cores + slot) * rows
        place = pl.ds(pl.multiple_of(begin, rows), rows)
        picked = jnp.concatenate([low_ref[:, place], high_ref[:, place]], axis=0)
        return jnp.dot(picked, rounded_state[slot % held], preferred_element_type=F32)

    @pl.when((step == 0) & (slab == 0))
    def _():
        weigh(jnp.concatenate([low_product_ref[...], high_product_ref[...]], axis=0), 0)
        output_state[...] = jnp.zeros_like(output_state)

    @pl.when((step == 1) & (slab == 0))
    def _():
        weigh(output_state[...], 1)

    @pl.when(step == 0)
    def _():
        differentiate(0, 0, 0)
        for slot, pair, which in slots:
            if slot + 1 < len(slots):
                ahead, *place = slots[slot + 1]
                differentiate(*place, ahead)
            for piece in pieces:
                gradient = gradient_state[slot % held, piece]
                first = 9.0 * first_ref[pair, which, piece] + gradient
                second = 19.0 * second_ref[pair, which, piece] + gradient * gradient
                weights = descend(first, second, start_ref[pair, which, piece].astype(F32))
                first_state[slab, pair, which, piece] = first
                second_state[slab, pair, which, piece] = second
                if kept:
                    weights_state[slab, pair, which, piece] = weights
                rounded_state[slot % held, piece] = weights.astype(BF16)
            output_state[...] += project(slot)

    @pl.when(step == 1)
    def _():
        sides = ((1 - core, send_refs), (core, keep_refs))
        differentiate(0, sides[0][0], 0)
        for slot, pair, side in slots:
            if slot + 1 < len(slots):
                ahead, next_pair, next_side = slots[slot + 1]
                differentiate(next_pair, sides[next_side][0], ahead)
            which, out_refs = sides[side]
            place = changed_place(mine, slab, pair, pairs)
            for piece in pieces:
                gradient = gradient_state[slot % held, piece]
                first = first_state[slab, pair, which, piece]
                second = second_state[slab, pair, which, piece]
                start = start_ref[pair, which, piece].astype(F32)
                if kept:
                    weights = weights_state[slab, pair, which, piece]
                else:
                    weights = descend(first, second, start)
                first = 0.9 * first + gradient
                second = 0.95 * second + gradient * gradient
                change = (start - descend(first, second, weights)) * WIRE_SCALE
                for index, out_ref in enumerate(out_refs):
                    part = out_ref.shape[-1]
                    out_ref[place, piece] = change[:, index * part : (index + 1) * part]


def inner(call, width, part, mine, banks, turned, start, first, second, products, target, count, tokens):
    slabs, pairs, cores, rows, _ = start.shape
    half, depth = banks[0].shape

    def held(step, slab):
        return jnp.where(step == 0, slab, slabs - 1)

    whole = pl.BlockSpec(memory_space=pltpu.VMEM)
    tile = (None, pairs, cores, rows, width)
    state = pl.BlockSpec(tile, lambda s, z, c: (held(s, z), 0, 0, 0, call))
    product = pl.BlockSpec((half, width), lambda s, z, c: (0, call))
    change = jax.ShapeDtypeStruct((slabs * pairs, rows, part), F32)
    outputs = 2 * (width // part)
    kept = width == part
    elements = depth * width
    return pl.pallas_call(
        functools.partial(inner_kernel, float(tokens), kept),
        grid_spec=pltpu.PrefetchScalarGridSpec(
            num_scalar_prefetch=1,
            grid=(2, slabs),
            in_specs=[whole] * 4
            + [
                pl.BlockSpec(tile, lambda s, z, c: (z, 0, 0, 0, call)),
                state,
                state,
                product,
                product,
                pl.BlockSpec((2 * half, width), lambda s, z, c: (0, call)),
                pl.BlockSpec(count.shape, lambda s, z, c: (0, 0, 0)),
            ],
            out_specs=[whole] * outputs,
            scratch_shapes=[pltpu.VMEM((slabs, pairs, cores, rows, width), F32)] * (2 + kept)
            + [
                pltpu.VMEM((2 * half, width), F32),
                pltpu.VMEM((2 * half, width), BF16),
                pltpu.VMEM((2, rows, width), F32),
                pltpu.VMEM((2, rows, width), BF16),
            ],
        ),
        out_shape=[change] * outputs,
        compiler_params=pltpu.CompilerParams(vmem_limit_bytes=32 * MIB),
        cost_estimate=pl.CostEstimate(
            flops=12 * half * elements,
            bytes_accessed=20 * elements,
            transcendentals=6 * elements,
        ),
        name="inner",
    )(mine, *banks, *turned, pinned(start), pinned(first), pinned(second), *products, target, count)


def assemble_kernel(begins, offsets, place_ref, *refs):
    out_ref, semaphore = refs[-2:]
    width = refs[0].shape[-1]
    mine = place_ref[0]
    copies = []
    for ref, begin, group in zip(refs, begins, offsets):
        for entry, offset in enumerate(group):
            copies.append(
                pltpu.make_async_copy(
                    ref.at[entry],
                    out_ref.at[lax.bitwise_xor(mine, offset), :, pl.ds(begin, width)],
                    semaphore.at[len(copies)],
                )
            )
    for copy in copies:
        copy.start()
    for copy in copies:
        copy.wait()


def assemble(place, blocks, shape, before):
    begins, received, offsets = zip(*blocks)
    vmem = pl.BlockSpec(memory_space=pltpu.VMEM)
    return pl.pallas_call(
        functools.partial(assemble_kernel, begins, offsets),
        in_specs=[pl.BlockSpec(memory_space=pltpu.SMEM)]
        + [vmem] * len(received)
        + [pl.BlockSpec(memory_space=pl.ANY)] * len(before),
        out_specs=pl.BlockSpec(memory_space=pl.ANY),
        out_shape=jax.ShapeDtypeStruct(shape, BF16),
        input_output_aliases={1 + len(received): 0} if before else {},
        scratch_shapes=[pltpu.SemaphoreType.DMA((sum(map(len, offsets)),))],
        compiler_params=pltpu.CompilerParams(vmem_limit_bytes=12 * MIB),
        cost_estimate=pl.CostEstimate(
            flops=0, bytes_accessed=4 * sum(array.size for array in received), transcendentals=0
        ),
        name="assemble",
    )(place, *received, *before)


def tied(first, second):
    return lax.optimization_barrier((first, second))


def per_device(sizes, global_weights, momentum, first_moment, second_moment, hidden_bank, target_bank, token_ids):
    reps, shards = sizes
    bits = reps.bit_length() - 1
    depth, columns = global_weights.shape
    rows = depth // reps
    store = hidden_bank.shape[1] * shards
    half = store // 2
    ids = token_ids[0]
    tokens = ids.shape[1]
    width = min(columns, LANES)
    chunks = columns // width
    mine = lax.axis_index("rep")

    def swapped(array, offset):
        pairs = [(index, index ^ offset) for index in range(reps)]
        return lax.ppermute(array, "rep", pairs)

    spans = [[0, 1 << bit] for bit in range(1, bits)]

    cut = (SLABS, reps // (2 * SLABS), 2, rows, columns)
    start = global_weights.reshape(cut)
    first = first_moment.reshape(cut)
    second = second_moment.reshape(cut)

    own_bank = hidden_bank[0]
    target = target_bank[0]
    count = jnp.sum(
        ids[:, :, None] == jnp.arange(store, dtype=ids.dtype)[None, None, :], axis=1
    ).astype(F32)
    if shards == 2:
        banks = (own_bank, lax.ppermute(own_bank, "fsdp", [(0, 1), (1, 0)]))
        swap = lax.axis_index("fsdp") == 1
        target = jnp.where(swap, jnp.roll(target, half, axis=0), target)
        count = jnp.where(swap, jnp.roll(count, half, axis=1), count)
    else:
        whole = lax.all_gather(own_bank, "fsdp", axis=0, tiled=True)
        banks = (whole[:half], whole[half:])
    count = count[:, :, None]

    place = mine.reshape(1).astype(jnp.int32)
    if chunks == 4:
        calls = [(2 * width, width), (0, 2 * width), (3 * width, width)]
    else:
        calls = [(begin, width) for begin in range(0, columns, width)]
    begins = [begin + part for begin, wide in calls for part in range(0, wide, width)]

    def start_rows(owner):
        return lax.dynamic_slice_in_dim(global_weights, owner * rows, rows, 0)

    pair_start = jnp.stack([start_rows(mine), start_rows(mine ^ spans[-1][1])])
    shares = [
        tied(momentum[:, begin : begin + width], pair_start[:, :, begin : begin + width])
        for begin in begins
    ]

    own = forward(banks[0], global_weights)
    received, (shares, own) = tied(banks[1], (shares, own))
    turned, products = zip(own, forward(received, global_weights))
    banks = (banks[0], received)
    turned = [array.reshape(cut[:4] + (half,)) for array in turned]

    def parted(terms, span):
        size = terms[0].shape[0] // len(span)
        parts = [[term[begin : begin + size] for term in terms] for begin in range(0, size * len(span), size)]
        outgoing = [sum(term.astype(F32) for term in part).astype(WIRE) for part in parts[1:]]
        return outgoing, parts[0]

    def sent(outgoing, span):
        return [swapped(array, offset) for array, offset in zip(outgoing, span[1:])]

    result = ()

    def chain(chunk, keep, arrived):
        terms = [keep, arrived]
        for span in spans[:-1]:
            outgoing, terms = parted(terms, span)
            outgoing = yield outgoing
            arrived = yield sent(outgoing, span)
            terms = terms + arrived
        scale = WIRE_SCALE * reps
        momentum_share, starts = shares[chunk]
        total = sum(term.astype(F32) for term in terms)
        pushed = (0.81 / 1.9 * scale) * momentum_share
        rounded = jnp.stack([total[0] + pushed, total[1]]).astype(WIRE)
        rounded = lax.optimization_barrier((yield rounded))
        arrived, = yield sent([rounded], spans[-1])
        moved = 0.9 * momentum_share + (total[0] + arrived[1].astype(F32)) * (1.0 / scale)
        both = rounded.astype(F32) + arrived[::-1].astype(F32)
        stack = (starts.astype(F32) - (1.33 / scale) * both).astype(BF16)
        offsets = list(spans[-1])
        stack = yield stack
        back = spans[-2::-1] if chunk + 1 < chunks or chunks == 1 else spans[:-1]
        for span in back[:-1]:
            arrived = yield sent([stack], span)
            offsets = [offset ^ far for far in span for offset in offsets]
            stack = yield jnp.concatenate([stack] + arrived)
        across, = yield sent([stack], back[-1])
        ends = [0, back[-1][1], 1, back[-1][1] ^ 1]
        finished[chunk] = (moved, stack, across, [[offset ^ end for offset in offsets] for end in ends])
        yield ()

    finished = {}
    running = {}
    formed = {}

    def move_on(which, behind=()):
        which = [chunk for chunk in which if chunk not in finished]
        arrived = {chunk: running[chunk].send(formed[chunk]) for chunk in which}
        arrived, _ = tied(arrived, [formed[chunk] for chunk in behind])
        for chunk in which:
            formed[chunk] = running[chunk].send(arrived[chunk])

    token = place
    fresh = range(0)
    later = {}
    for begin, wide in calls:
        changes = inner(
            begin // wide, wide, width, token, banks, turned, start, first, second, products, target, count, tokens
        )
        sends = [send.astype(WIRE) for send in changes[::2]]
        if fresh:
            move_on(range(fresh[0] + 1))
            for chunk in fresh[1:]:
                keep, arrived = later.pop(chunk)
                arrived, _ = tied(arrived, [formed[other] for other in range(fresh[0] + 1)])
                running[chunk] = chain(chunk, keep, arrived)
                formed[chunk] = next(running[chunk])
            sends, _ = tied(sends, [formed[chunk] for chunk in range(fresh.stop)])
        fresh = range(fresh.stop, fresh.stop + wide // width)
        for chunk, send, keep in zip(fresh, sends, changes[1::2]):
            later[chunk] = (keep, swapped(send, 1))
        running[fresh[0]] = chain(fresh[0], *later.pop(fresh[0]))
        formed[fresh[0]] = next(running[fresh[0]])
        if fresh.stop < chunks:
            formed, token = tied(formed, token)
    if chunks == 4:
        before = 3
        for which in (1, 0, 2, 3, 0, 1, 2):
            move_on([which], behind=[before])
            before = which
    for chunk in range(chunks):
        while chunk not in finished:
            move_on([chunk])

    blocks = []
    for chunk in range(chunks):
        _, stack, across, offsets = finished[chunk]
        if chunk == 1 and result:
            across, *result = tied(across, result[0])
        received = [stack, across, swapped(stack, 1), swapped(across, 1)]
        blocks += [(begins[chunk], array, group) for array, group in zip(received, offsets)]
        if chunk + 2 != chunks:
            result = (assemble(place, blocks, (reps, rows, columns), result),)
            blocks = []

    new_momentum = [finished[chunk][0] for chunk in sorted(range(chunks), key=begins.__getitem__)]

    return result[0].reshape(depth, columns), jnp.concatenate(new_momentum, axis=1)


def solution(mesh):
    sizes = (mesh.shape["rep"], mesh.shape["fsdp"])
    return jax.shard_map(
        functools.partial(per_device, sizes),
        mesh=mesh,
        in_specs=(
            P(None, "fsdp"),
            P("rep", "fsdp"),
            P("rep", None, "fsdp"),
            P("rep", None, "fsdp"),
            P("rep", "fsdp", None),
            P("rep", None, "fsdp"),
            P("rep", None, None),
        ),
        out_specs=(P(None, "fsdp"), P("rep", "fsdp")),
        check_vma=False,
    )
```

```python
import functools
import math
import jax
import jax.numpy as jnp
from jax import lax
from jax.experimental import pallas as pl
from jax.experimental.pallas import tpu as pltpu
from jax.sharding import PartitionSpec as P

F32 = jnp.float32
BF16 = jnp.bfloat16
WIRE = jnp.float16
WIRE_SCALE = 64.0
LANES = 128
SLABS = 4
PIECE = 8192
MIB = 1024 * 1024


def forward_kernel(part_ref, weights_ref, turned_ref, product_ref):
    depth = part_ref.shape[1]
    block = depth // SLABS
    product = jnp.zeros(product_ref.shape, F32)
    for begin in range(0, depth, block):
        place = pl.ds(begin, block)
        part = part_ref[:, place]
        product += jnp.dot(part, weights_ref[place, :], preferred_element_type=F32)
        turned_ref[place, :] = part.T
    product_ref[...] = product


def forward(part, weights):
    rows, depth = part.shape
    columns = weights.shape[1]
    vmem = pl.BlockSpec(memory_space=pltpu.VMEM)
    return pl.pallas_call(
        forward_kernel,
        in_specs=[vmem, vmem],
        out_specs=[vmem, vmem],
        out_shape=[
            jax.ShapeDtypeStruct((depth, rows), BF16),
            jax.ShapeDtypeStruct((rows, columns), F32),
        ],
        compiler_params=pltpu.CompilerParams(vmem_limit_bytes=8 * MIB),
        cost_estimate=pl.CostEstimate(
            flops=2 * rows * depth * columns,
            bytes_accessed=2 * depth * columns + 4 * rows * depth,
            transcendentals=0,
        ),
        name="forward",
    )(part, weights)


def pinned(array):
    return pltpu.with_memory_space_constraint(array, pltpu.HBM)


def changed_place(mine, slab, pair, pairs):
    offset = lax.bitwise_xor(slab * pairs + pair, mine // 2)
    bits = (SLABS * pairs).bit_length() - 1
    place = jnp.int32(0)
    for bit in range(bits):
        place = place * 2 + lax.rem(lax.shift_right_logical(offset, bit), 2)
    return place


def inner_kernel(
    tokens,
    kept,
    mine_ref,
    low_ref,
    high_ref,
    low_turned_ref,
    high_turned_ref,
    start_ref,
    first_ref,
    second_ref,
    low_product_ref,
    high_product_ref,
    target_ref,
    count_ref,
    *rest,
):
    *rest, first_state, second_state, output_state, residual_state, gradient_state, rounded_state = rest
    change_refs, weights_state = (rest[:-1], rest[-1]) if kept else (rest, None)
    send_refs, keep_refs = change_refs[::2], change_refs[1::2]
    step = pl.program_id(0)
    slab = pl.program_id(1)
    pairs, cores, rows, _ = start_ref.shape
    mine = mine_ref[0]
    core = lax.rem(mine, cores)
    height = PIECE // start_ref.shape[-1]
    pieces = [pl.ds(begin, height) for begin in range(0, rows, height)]
    slots = [(slot, *divmod(slot, cores)) for slot in range(pairs * cores)]
    held = gradient_state.shape[0]

    def weigh(output, which):
        residual = ((output - target_ref[...].astype(F32)) / tokens).astype(BF16)
        residual_state[...] = (residual.astype(F32) * count_ref[which]).astype(BF16)

    def descend(first, second, weights):
        root = second * lax.rsqrt(second)
        below = (100.0 * math.sqrt(0.05)) * root + 1e-06
        return 0.99 * weights - first * lax.rsqrt(below * below)

    def differentiate(pair, which, slot):
        turned = jnp.concatenate(
            [low_turned_ref[slab, pair, which], high_turned_ref[slab, pair, which]], axis=1
        )
        gradient_state[slot % held] = jnp.dot(
            turned, residual_state[...], preferred_element_type=F32
        )

    def project(slot):
        begin = (slab * pairs * cores + slot) * rows
        place = pl.ds(pl.multiple_of(begin, rows), rows)
        picked = jnp.concatenate([low_ref[:, place], high_ref[:, place]], axis=0)
        return jnp.dot(picked, rounded_state[slot % held], preferred_element_type=F32)

    @pl.when((step == 0) & (slab == 0))
    def _():
        weigh(jnp.concatenate([low_product_ref[...], high_product_ref[...]], axis=0), 0)
        output_state[...] = jnp.zeros_like(output_state)

    @pl.when((step == 1) & (slab == 0))
    def _():
        weigh(output_state[...], 1)

    @pl.when(step == 0)
    def _():
        differentiate(0, 0, 0)
        for slot, pair, which in slots:
            if slot + 1 < len(slots):
                ahead, *place = slots[slot + 1]
                differentiate(*place, ahead)
            for piece in pieces:
                gradient = gradient_state[slot % held, piece]
                first = 9.0 * first_ref[pair, which, piece] + gradient
                second = 19.0 * second_ref[pair, which, piece] + gradient * gradient
                weights = descend(first, second, start_ref[pair, which, piece].astype(F32))
                first_state[slab, pair, which, piece] = first
                second_state[slab, pair, which, piece] = second
                if kept:
                    weights_state[slab, pair, which, piece] = weights
                rounded_state[slot % held, piece] = weights.astype(BF16)
            output_state[...] += project(slot)

    @pl.when(step == 1)
    def _():
        sides = ((1 - core, send_refs), (core, keep_refs))
        differentiate(0, sides[0][0], 0)
        for slot, pair, side in slots:
            if slot + 1 < len(slots):
                ahead, next_pair, next_side = slots[slot + 1]
                differentiate(next_pair, sides[next_side][0], ahead)
            which, out_refs = sides[side]
            place = changed_place(mine, slab, pair, pairs)
            for piece in pieces:
                gradient = gradient_state[slot % held, piece]
                first = first_state[slab, pair, which, piece]
                second = second_state[slab, pair, which, piece]
                start = start_ref[pair, which, piece].astype(F32)
                if kept:
                    weights = weights_state[slab, pair, which, piece]
                else:
                    weights = descend(first, second, start)
                first = 0.9 * first + gradient
                second = 0.95 * second + gradient * gradient
                change = (start - descend(first, second, weights)) * WIRE_SCALE
                for index, out_ref in enumerate(out_refs):
                    part = out_ref.shape[-1]
                    out_ref[place, piece] = change[:, index * part : (index + 1) * part]


def inner(call, width, part, mine, banks, turned, start, first, second, products, target, count, tokens):
    slabs, pairs, cores, rows, _ = start.shape
    half, depth = banks[0].shape

    def held(step, slab):
        return jnp.where(step == 0, slab, slabs - 1)

    whole = pl.BlockSpec(memory_space=pltpu.VMEM)
    tile = (None, pairs, cores, rows, width)
    state = pl.BlockSpec(tile, lambda s, z, c: (held(s, z), 0, 0, 0, call))
    product = pl.BlockSpec((half, width), lambda s, z, c: (0, call))
    change = jax.ShapeDtypeStruct((slabs * pairs, rows, part), F32)
    outputs = 2 * (width // part)
    kept = width == part
    elements = depth * width
    return pl.pallas_call(
        functools.partial(inner_kernel, float(tokens), kept),
        grid_spec=pltpu.PrefetchScalarGridSpec(
            num_scalar_prefetch=1,
            grid=(2, slabs),
            in_specs=[whole] * 4
            + [
                pl.BlockSpec(tile, lambda s, z, c: (z, 0, 0, 0, call)),
                state,
                state,
                product,
                product,
                pl.BlockSpec((2 * half, width), lambda s, z, c: (0, call)),
                pl.BlockSpec(count.shape, lambda s, z, c: (0, 0, 0)),
            ],
            out_specs=[whole] * outputs,
            scratch_shapes=[pltpu.VMEM((slabs, pairs, cores, rows, width), F32)] * (2 + kept)
            + [
                pltpu.VMEM((2 * half, width), F32),
                pltpu.VMEM((2 * half, width), BF16),
                pltpu.VMEM((2, rows, width), F32),
                pltpu.VMEM((2, rows, width), BF16),
            ],
        ),
        out_shape=[change] * outputs,
        compiler_params=pltpu.CompilerParams(vmem_limit_bytes=32 * MIB),
        cost_estimate=pl.CostEstimate(
            flops=12 * half * elements,
            bytes_accessed=20 * elements,
            transcendentals=6 * elements,
        ),
        name="inner",
    )(mine, *banks, *turned, pinned(start), pinned(first), pinned(second), *products, target, count)


def assemble_kernel(begins, offsets, place_ref, *refs):
    out_ref, semaphore = refs[-2:]
    width = refs[0].shape[-1]
    mine = place_ref[0]
    copies = []
    for ref, begin, group in zip(refs, begins, offsets):
        for entry, offset in enumerate(group):
            copies.append(
                pltpu.make_async_copy(
                    ref.at[entry],
                    out_ref.at[lax.bitwise_xor(mine, offset), :, pl.ds(begin, width)],
                    semaphore.at[len(copies)],
                )
            )
    for copy in copies:
        copy.start()
    for copy in copies:
        copy.wait()


def assemble(place, blocks, shape, before):
    begins, received, offsets = zip(*blocks)
    vmem = pl.BlockSpec(memory_space=pltpu.VMEM)
    return pl.pallas_call(
        functools.partial(assemble_kernel, begins, offsets),
        in_specs=[pl.BlockSpec(memory_space=pltpu.SMEM)]
        + [vmem] * len(received)
        + [pl.BlockSpec(memory_space=pl.ANY)] * len(before),
        out_specs=pl.BlockSpec(memory_space=pl.ANY),
        out_shape=jax.ShapeDtypeStruct(shape, BF16),
        input_output_aliases={1 + len(received): 0} if before else {},
        scratch_shapes=[pltpu.SemaphoreType.DMA((sum(map(len, offsets)),))],
        compiler_params=pltpu.CompilerParams(vmem_limit_bytes=12 * MIB),
        cost_estimate=pl.CostEstimate(
            flops=0, bytes_accessed=4 * sum(array.size for array in received), transcendentals=0
        ),
        name="assemble",
    )(place, *received, *before)


def tied(first, second):
    return lax.optimization_barrier((first, second))


def per_device(sizes, global_weights, momentum, first_moment, second_moment, hidden_bank, target_bank, token_ids):
    reps, shards = sizes
    bits = reps.bit_length() - 1
    depth, columns = global_weights.shape
    rows = depth // reps
    store = hidden_bank.shape[1] * shards
    half = store // 2
    ids = token_ids[0]
    tokens = ids.shape[1]
    width = min(columns, LANES)
    chunks = columns // width
    mine = lax.axis_index("rep")

    def swapped(array, offset):
        pairs = [(index, index ^ offset) for index in range(reps)]
        return lax.ppermute(array, "rep", pairs)

    spans = [[0, 1 << bit] for bit in range(1, bits)]

    cut = (SLABS, reps // (2 * SLABS), 2, rows, columns)
    start = global_weights.reshape(cut)
    first = first_moment.reshape(cut)
    second = second_moment.reshape(cut)

    own_bank = hidden_bank[0]
    target = target_bank[0]
    count = jnp.sum(
        ids[:, :, None] == jnp.arange(store, dtype=ids.dtype)[None, None, :], axis=1
    ).astype(F32)
    if shards == 2:
        banks = (own_bank, lax.ppermute(own_bank, "fsdp", [(0, 1), (1, 0)]))
        swap = lax.axis_index("fsdp") == 1
        target = jnp.where(swap, jnp.roll(target, half, axis=0), target)
        count = jnp.where(swap, jnp.roll(count, half, axis=1), count)
    else:
        whole = lax.all_gather(own_bank, "fsdp", axis=0, tiled=True)
        banks = (whole[:half], whole[half:])
    count = count[:, :, None]

    place = mine.reshape(1).astype(jnp.int32)
    if chunks == 4:
        calls = [(2 * width, width), (0, 2 * width), (3 * width, width)]
    else:
        calls = [(begin, width) for begin in range(0, columns, width)]
    begins = [begin + part for begin, wide in calls for part in range(0, wide, width)]

    def start_rows(owner):
        return lax.dynamic_slice_in_dim(global_weights, owner * rows, rows, 0)

    pair_start = jnp.stack([start_rows(mine), start_rows(mine ^ spans[-1][1])])
    shares = [
        tied(momentum[:, begin : begin + width], pair_start[:, :, begin : begin + width])
        for begin in begins
    ]

    own = forward(banks[0], global_weights)
    received, (shares, own) = tied(banks[1], (shares, own))
    turned, products = zip(own, forward(received, global_weights))
    banks = (banks[0], received)
    turned = [array.reshape(cut[:4] + (half,)) for array in turned]

    def parted(terms, span):
        size = terms[0].shape[0] // len(span)
        parts = [[term[begin : begin + size] for term in terms] for begin in range(0, size * len(span), size)]
        outgoing = [sum(term.astype(F32) for term in part).astype(WIRE) for part in parts[1:]]
        return outgoing, parts[0]

    def sent(outgoing, span):
        return [swapped(array, offset) for array, offset in zip(outgoing, span[1:])]

    result = ()

    def chain(chunk, keep, arrived):
        terms = [keep, arrived]
        for span in spans[:-1]:
            outgoing, terms = parted(terms, span)
            outgoing = yield outgoing
            arrived = yield sent(outgoing, span)
            terms = terms + arrived
        scale = WIRE_SCALE * reps
        momentum_share, starts = shares[chunk]
        total = sum(term.astype(F32) for term in terms)
        pushed = (0.81 / 1.9 * scale) * momentum_share
        rounded = jnp.stack([total[0] + pushed, total[1]]).astype(WIRE)
        rounded = lax.optimization_barrier((yield rounded))
        arrived, = yield sent([rounded], spans[-1])
        moved = 0.9 * momentum_share + (total[0] + arrived[1].astype(F32)) * (1.0 / scale)
        both = rounded.astype(F32) + arrived[::-1].astype(F32)
        stack = (starts.astype(F32) - (1.33 / scale) * both).astype(BF16)
        offsets = list(spans[-1])
        stack = yield stack
        back = spans[:-1] if chunk % 2 else spans[-2::-1]
        for span in back[:-1]:
            arrived = yield sent([stack], span)
            offsets = [offset ^ far for far in span for offset in offsets]
            stack = yield jnp.concatenate([stack] + arrived)
        across, = yield sent([stack], back[-1])
        ends = [0, back[-1][1], 1, back[-1][1] ^ 1]
        finished[chunk] = (moved, stack, across, [[offset ^ end for offset in offsets] for end in ends])
        yield ()

    finished = {}
    running = {}
    formed = {}

    def move_on(which, behind=()):
        which = [chunk for chunk in which if chunk not in finished]
        arrived = {chunk: running[chunk].send(formed[chunk]) for chunk in which}
        arrived, _ = tied(arrived, [formed[chunk] for chunk in behind])
        for chunk in which:
            formed[chunk] = running[chunk].send(arrived[chunk])

    token = place
    fresh = range(0)
    later = {}
    for begin, wide in calls:
        changes = inner(
            begin // wide, wide, width, token, banks, turned, start, first, second, products, target, count, tokens
        )
        sends = [send.astype(WIRE) for send in changes[::2]]
        if fresh:
            move_on(range(fresh[0] + 1))
            for chunk in fresh[1:]:
                keep, arrived = later.pop(chunk)
                arrived, _ = tied(arrived, [formed[other] for other in range(fresh[0] + 1)])
                running[chunk] = chain(chunk, keep, arrived)
                formed[chunk] = next(running[chunk])
            sends, _ = tied(sends, [formed[chunk] for chunk in range(fresh.stop)])
        fresh = range(fresh.stop, fresh.stop + wide // width)
        for chunk, send, keep in zip(fresh, sends, changes[1::2]):
            later[chunk] = (keep, swapped(send, 1))
        running[fresh[0]] = chain(fresh[0], *later.pop(fresh[0]))
        formed[fresh[0]] = next(running[fresh[0]])
        if fresh.stop < chunks:
            formed, token = tied(formed, token)
    if chunks == 4:
        before = 3
        for which in (1, 0, 2, 3, 0, 1, 2):
            move_on([which], behind=[before])
            before = which
    for chunk in range(chunks):
        while chunk not in finished:
            move_on([chunk])

    blocks = []
    for chunk in range(chunks):
        _, stack, across, offsets = finished[chunk]
        if chunk == 1 and result:
            across, *result = tied(across, result[0])
        received = [stack, across, swapped(stack, 1), swapped(across, 1)]
        blocks += [(begins[chunk], array, group) for array, group in zip(received, offsets)]
        if chunk + 2 != chunks:
            result = (assemble(place, blocks, (reps, rows, columns), result),)
            blocks = []

    new_momentum = [finished[chunk][0] for chunk in sorted(range(chunks), key=begins.__getitem__)]

    return result[0].reshape(depth, columns), jnp.concatenate(new_momentum, axis=1)


def solution(mesh):
    sizes = (mesh.shape["rep"], mesh.shape["fsdp"])
    return jax.shard_map(
        functools.partial(per_device, sizes),
        mesh=mesh,
        in_specs=(
            P(None, "fsdp"),
            P("rep", "fsdp"),
            P("rep", None, "fsdp"),
            P("rep", None, "fsdp"),
            P("rep", "fsdp", None),
            P("rep", None, "fsdp"),
            P("rep", None, None),
        ),
        out_specs=(P(None, "fsdp"), P("rep", "fsdp")),
        check_vma=False,
    )
```

```python
import functools
import math
import jax
import jax.numpy as jnp
from jax import lax
from jax.experimental import pallas as pl
from jax.experimental.pallas import tpu as pltpu
from jax.sharding import PartitionSpec as P

F32 = jnp.float32
BF16 = jnp.bfloat16
WIRE = jnp.float16
WIRE_SCALE = 64.0
LANES = 128
SLABS = 4
PIECE = 8192
MIB = 1024 * 1024


def forward_kernel(part_ref, weights_ref, turned_ref, product_ref):
    depth = part_ref.shape[1]
    block = depth // SLABS
    product = jnp.zeros(product_ref.shape, F32)
    for begin in range(0, depth, block):
        place = pl.ds(begin, block)
        part = part_ref[:, place]
        product += jnp.dot(part, weights_ref[place, :], preferred_element_type=F32)
        turned_ref[place, :] = part.T
    product_ref[...] = product


def forward(part, weights):
    rows, depth = part.shape
    columns = weights.shape[1]
    vmem = pl.BlockSpec(memory_space=pltpu.VMEM)
    return pl.pallas_call(
        forward_kernel,
        in_specs=[vmem, vmem],
        out_specs=[vmem, vmem],
        out_shape=[
            jax.ShapeDtypeStruct((depth, rows), BF16),
            jax.ShapeDtypeStruct((rows, columns), F32),
        ],
        compiler_params=pltpu.CompilerParams(vmem_limit_bytes=8 * MIB),
        cost_estimate=pl.CostEstimate(
            flops=2 * rows * depth * columns,
            bytes_accessed=2 * depth * columns + 4 * rows * depth,
            transcendentals=0,
        ),
        name="forward",
    )(part, weights)


def pinned(array):
    return pltpu.with_memory_space_constraint(array, pltpu.HBM)


def changed_place(mine, slab, pair, pairs, order):
    offset = lax.bitwise_xor(slab * pairs + pair, mine // 2)
    place = jnp.int32(0)
    for bit in order:
        place = place * 2 + lax.rem(lax.shift_right_logical(offset, bit), 2)
    return place


def inner_kernel(
    tokens,
    kept,
    orders,
    mine_ref,
    low_ref,
    high_ref,
    low_turned_ref,
    high_turned_ref,
    start_ref,
    first_ref,
    second_ref,
    low_product_ref,
    high_product_ref,
    target_ref,
    count_ref,
    *rest,
):
    *rest, first_state, second_state, output_state, residual_state, gradient_state, rounded_state = rest
    change_refs, weights_state = (rest[:-1], rest[-1]) if kept else (rest, None)
    send_refs, keep_refs = change_refs[::2], change_refs[1::2]
    step = pl.program_id(0)
    slab = pl.program_id(1)
    pairs, cores, rows, _ = start_ref.shape
    mine = mine_ref[0]
    core = lax.rem(mine, cores)
    height = PIECE // start_ref.shape[-1]
    pieces = [pl.ds(begin, height) for begin in range(0, rows, height)]
    slots = [(slot, *divmod(slot, cores)) for slot in range(pairs * cores)]
    held = gradient_state.shape[0]

    def weigh(output, which):
        residual = ((output - target_ref[...].astype(F32)) / tokens).astype(BF16)
        residual_state[...] = (residual.astype(F32) * count_ref[which]).astype(BF16)

    def descend(first, second, weights):
        root = second * lax.rsqrt(second)
        below = (100.0 * math.sqrt(0.05)) * root + 1e-06
        return 0.99 * weights - first * lax.rsqrt(below * below)

    def differentiate(pair, which, slot):
        turned = jnp.concatenate(
            [low_turned_ref[slab, pair, which], high_turned_ref[slab, pair, which]], axis=1
        )
        gradient_state[slot % held] = jnp.dot(
            turned, residual_state[...], preferred_element_type=F32
        )

    def project(slot):
        begin = (slab * pairs * cores + slot) * rows
        place = pl.ds(pl.multiple_of(begin, rows), rows)
        picked = jnp.concatenate([low_ref[:, place], high_ref[:, place]], axis=0)
        return jnp.dot(picked, rounded_state[slot % held], preferred_element_type=F32)

    @pl.when((step == 0) & (slab == 0))
    def _():
        weigh(jnp.concatenate([low_product_ref[...], high_product_ref[...]], axis=0), 0)
        output_state[...] = jnp.zeros_like(output_state)

    @pl.when((step == 1) & (slab == 0))
    def _():
        weigh(output_state[...], 1)

    @pl.when(step == 0)
    def _():
        differentiate(0, 0, 0)
        for slot, pair, which in slots:
            if slot + 1 < len(slots):
                ahead, *place = slots[slot + 1]
                differentiate(*place, ahead)
            for piece in pieces:
                gradient = gradient_state[slot % held, piece]
                first = 9.0 * first_ref[pair, which, piece] + gradient
                second = 19.0 * second_ref[pair, which, piece] + gradient * gradient
                weights = descend(first, second, start_ref[pair, which, piece].astype(F32))
                first_state[slab, pair, which, piece] = first
                second_state[slab, pair, which, piece] = second
                if kept:
                    weights_state[slab, pair, which, piece] = weights
                rounded_state[slot % held, piece] = weights.astype(BF16)
            output_state[...] += project(slot)

    @pl.when(step == 1)
    def _():
        sides = ((1 - core, send_refs), (core, keep_refs))
        differentiate(0, sides[0][0], 0)
        for slot, pair, side in slots:
            if slot + 1 < len(slots):
                ahead, next_pair, next_side = slots[slot + 1]
                differentiate(next_pair, sides[next_side][0], ahead)
            which, out_refs = sides[side]
            places = [changed_place(mine, slab, pair, pairs, order) for order in orders]
            for piece in pieces:
                gradient = gradient_state[slot % held, piece]
                first = first_state[slab, pair, which, piece]
                second = second_state[slab, pair, which, piece]
                start = start_ref[pair, which, piece].astype(F32)
                if kept:
                    weights = weights_state[slab, pair, which, piece]
                else:
                    weights = descend(first, second, start)
                first = 0.9 * first + gradient
                second = 0.95 * second + gradient * gradient
                change = (start - descend(first, second, weights)) * WIRE_SCALE
                for index, out_ref in enumerate(out_refs):
                    part = out_ref.shape[-1]
                    out_ref[places[index], piece] = change[:, index * part : (index + 1) * part]


def inner(call, width, part, orders, mine, banks, turned, start, first, second, products, target, count, tokens):
    slabs, pairs, cores, rows, _ = start.shape
    half, depth = banks[0].shape

    def held(step, slab):
        return jnp.where(step == 0, slab, slabs - 1)

    whole = pl.BlockSpec(memory_space=pltpu.VMEM)
    tile = (None, pairs, cores, rows, width)
    state = pl.BlockSpec(tile, lambda s, z, c: (held(s, z), 0, 0, 0, call))
    product = pl.BlockSpec((half, width), lambda s, z, c: (0, call))
    change = jax.ShapeDtypeStruct((slabs * pairs, rows, part), F32)
    outputs = 2 * (width // part)
    kept = width == part
    elements = depth * width
    return pl.pallas_call(
        functools.partial(inner_kernel, float(tokens), kept, orders),
        grid_spec=pltpu.PrefetchScalarGridSpec(
            num_scalar_prefetch=1,
            grid=(2, slabs),
            in_specs=[whole] * 4
            + [
                pl.BlockSpec(tile, lambda s, z, c: (z, 0, 0, 0, call)),
                state,
                state,
                product,
                product,
                pl.BlockSpec((2 * half, width), lambda s, z, c: (0, call)),
                pl.BlockSpec(count.shape, lambda s, z, c: (0, 0, 0)),
            ],
            out_specs=[whole] * outputs,
            scratch_shapes=[pltpu.VMEM((slabs, pairs, cores, rows, width), F32)] * (2 + kept)
            + [
                pltpu.VMEM((2 * half, width), F32),
                pltpu.VMEM((2 * half, width), BF16),
                pltpu.VMEM((2, rows, width), F32),
                pltpu.VMEM((2, rows, width), BF16),
            ],
        ),
        out_shape=[change] * outputs,
        compiler_params=pltpu.CompilerParams(vmem_limit_bytes=32 * MIB),
        cost_estimate=pl.CostEstimate(
            flops=12 * half * elements,
            bytes_accessed=20 * elements,
            transcendentals=6 * elements,
        ),
        name="inner",
    )(mine, *banks, *turned, pinned(start), pinned(first), pinned(second), *products, target, count)


def assemble_kernel(begins, offsets, place_ref, *refs):
    out_ref, semaphore = refs[-2:]
    width = refs[0].shape[-1]
    mine = place_ref[0]
    copies = []
    for ref, begin, group in zip(refs, begins, offsets):
        for entry, offset in enumerate(group):
            copies.append(
                pltpu.make_async_copy(
                    ref.at[entry],
                    out_ref.at[lax.bitwise_xor(mine, offset), :, pl.ds(begin, width)],
                    semaphore.at[len(copies)],
                )
            )
    for copy in copies:
        copy.start()
    for copy in copies:
        copy.wait()


def assemble(place, blocks, shape, before):
    begins, received, offsets = zip(*blocks)
    vmem = pl.BlockSpec(memory_space=pltpu.VMEM)
    return pl.pallas_call(
        functools.partial(assemble_kernel, begins, offsets),
        in_specs=[pl.BlockSpec(memory_space=pltpu.SMEM)]
        + [vmem] * len(received)
        + [pl.BlockSpec(memory_space=pl.ANY)] * len(before),
        out_specs=pl.BlockSpec(memory_space=pl.ANY),
        out_shape=jax.ShapeDtypeStruct(shape, BF16),
        input_output_aliases={1 + len(received): 0} if before else {},
        scratch_shapes=[pltpu.SemaphoreType.DMA((sum(map(len, offsets)),))],
        compiler_params=pltpu.CompilerParams(vmem_limit_bytes=12 * MIB),
        cost_estimate=pl.CostEstimate(
            flops=0, bytes_accessed=4 * sum(array.size for array in received), transcendentals=0
        ),
        name="assemble",
    )(place, *received, *before)


def tied(first, second):
    return lax.optimization_barrier((first, second))


def per_device(sizes, global_weights, momentum, first_moment, second_moment, hidden_bank, target_bank, token_ids):
    reps, shards = sizes
    bits = reps.bit_length() - 1
    depth, columns = global_weights.shape
    rows = depth // reps
    store = hidden_bank.shape[1] * shards
    half = store // 2
    ids = token_ids[0]
    tokens = ids.shape[1]
    width = min(columns, LANES)
    chunks = columns // width
    mine = lax.axis_index("rep")

    def swapped(array, offset):
        pairs = [(index, index ^ offset) for index in range(reps)]
        return lax.ppermute(array, "rep", pairs)

    spans = [[0, 1 << bit] for bit in range(1, bits)]

    cut = (SLABS, reps // (2 * SLABS), 2, rows, columns)
    start = global_weights.reshape(cut)
    first = first_moment.reshape(cut)
    second = second_moment.reshape(cut)

    own_bank = hidden_bank[0]
    target = target_bank[0]
    count = jnp.sum(
        ids[:, :, None] == jnp.arange(store, dtype=ids.dtype)[None, None, :], axis=1
    ).astype(F32)
    if shards == 2:
        banks = (own_bank, lax.ppermute(own_bank, "fsdp", [(0, 1), (1, 0)]))
        swap = lax.axis_index("fsdp") == 1
        target = jnp.where(swap, jnp.roll(target, half, axis=0), target)
        count = jnp.where(swap, jnp.roll(count, half, axis=1), count)
    else:
        whole = lax.all_gather(own_bank, "fsdp", axis=0, tiled=True)
        banks = (whole[:half], whole[half:])
    count = count[:, :, None]

    place = mine.reshape(1).astype(jnp.int32)
    if chunks == 4:
        calls = [(2 * width, width), (0, 2 * width), (3 * width, width)]
    else:
        calls = [(begin, width) for begin in range(0, columns, width)]
    begins = [begin + part for begin, wide in calls for part in range(0, wide, width)]

    def start_rows(owner):
        return lax.dynamic_slice_in_dim(global_weights, owner * rows, rows, 0)

    pair_start = jnp.stack([start_rows(mine), start_rows(mine ^ spans[-1][1])])
    shares = [
        tied(momentum[:, begin : begin + width], pair_start[:, :, begin : begin + width])
        for begin in begins
    ]

    own = forward(banks[0], global_weights)
    received, (shares, own) = tied(banks[1], (shares, own))
    turned, products = zip(own, forward(received, global_weights))
    banks = (banks[0], received)
    turned = [array.reshape(cut[:4] + (half,)) for array in turned]

    def parted(terms, span):
        size = terms[0].shape[0] // len(span)
        parts = [[term[begin : begin + size] for term in terms] for begin in range(0, size * len(span), size)]
        outgoing = [sum(term.astype(F32) for term in part).astype(WIRE) for part in parts[1:]]
        return outgoing, parts[0]

    def sent(outgoing, span):
        return [swapped(array, offset) for array, offset in zip(outgoing, span[1:])]

    result = ()

    def order_of(chunk):
        order = list(range(len(spans)))
        return [1, 0] + order[2:] if chunk == 2 else order

    def chain(chunk, keep, arrived):
        terms = [keep, arrived]
        for span in [spans[bit] for bit in order_of(chunk)][:-1]:
            outgoing, terms = parted(terms, span)
            outgoing = yield outgoing
            arrived = yield sent(outgoing, span)
            terms = terms + arrived
        scale = WIRE_SCALE * reps
        momentum_share, starts = shares[chunk]
        total = sum(term.astype(F32) for term in terms)
        pushed = (0.81 / 1.9 * scale) * momentum_share
        rounded = jnp.stack([total[0] + pushed, total[1]]).astype(WIRE)
        rounded = lax.optimization_barrier((yield rounded))
        arrived, = yield sent([rounded], spans[-1])
        moved = 0.9 * momentum_share + (total[0] + arrived[1].astype(F32)) * (1.0 / scale)
        both = rounded.astype(F32) + arrived[::-1].astype(F32)
        stack = (starts.astype(F32) - (1.33 / scale) * both).astype(BF16)
        offsets = list(spans[-1])
        stack = yield stack
        back = spans[:-1] if chunk % 2 else spans[-2::-1]
        for span in back[:-1]:
            arrived = yield sent([stack], span)
            offsets = [offset ^ far for far in span for offset in offsets]
            stack = yield jnp.concatenate([stack] + arrived)
        across, = yield sent([stack], back[-1])
        ends = [0, back[-1][1], 1, back[-1][1] ^ 1]
        finished[chunk] = (moved, stack, across, [[offset ^ end for offset in offsets] for end in ends])
        yield ()

    finished = {}
    running = {}
    formed = {}

    def move_on(which, behind=()):
        which = [chunk for chunk in which if chunk not in finished]
        arrived = {chunk: running[chunk].send(formed[chunk]) for chunk in which}
        arrived, _ = tied(arrived, [formed[chunk] for chunk in behind])
        for chunk in which:
            formed[chunk] = running[chunk].send(arrived[chunk])

    token = place
    fresh = range(0)
    later = {}
    for begin, wide in calls:
        changes = inner(
            begin // wide,
            wide,
            width,
            [order_of(chunk) for chunk in range(fresh.stop, fresh.stop + wide // width)],
            token,
            banks,
            turned,
            start,
            first,
            second,
            products,
            target,
            count,
            tokens,
        )
        sends = [send.astype(WIRE) for send in changes[::2]]
        if fresh:
            move_on(range(fresh[0] + 1))
            for chunk in fresh[1:]:
                keep, arrived = later.pop(chunk)
                arrived, _ = tied(arrived, [formed[other] for other in range(fresh[0] + 1)])
                running[chunk] = chain(chunk, keep, arrived)
                formed[chunk] = next(running[chunk])
            sends, _ = tied(sends, [formed[chunk] for chunk in range(fresh.stop)])
        fresh = range(fresh.stop, fresh.stop + wide // width)
        for chunk, send, keep in zip(fresh, sends, changes[1::2]):
            later[chunk] = (keep, swapped(send, 1))
        running[fresh[0]] = chain(fresh[0], *later.pop(fresh[0]))
        formed[fresh[0]] = next(running[fresh[0]])
        if fresh.stop < chunks:
            formed, token = tied(formed, token)
    if chunks == 4:
        before = 3
        for which in (1, 0, 3, 2, 0, 1, 3, 2):
            move_on([which], behind=[before])
            before = which
    for chunk in range(chunks):
        while chunk not in finished:
            move_on([chunk])

    blocks = []
    for chunk in range(chunks):
        _, stack, across, offsets = finished[chunk]
        if chunk == 1 and result:
            across, *result = tied(across, result[0])
        received = [stack, across, swapped(stack, 1), swapped(across, 1)]
        blocks += [(begins[chunk], array, group) for array, group in zip(received, offsets)]
        if chunk + 2 != chunks:
            result = (assemble(place, blocks, (reps, rows, columns), result),)
            blocks = []

    new_momentum = [finished[chunk][0] for chunk in sorted(range(chunks), key=begins.__getitem__)]

    return result[0].reshape(depth, columns), jnp.concatenate(new_momentum, axis=1)


def solution(mesh):
    sizes = (mesh.shape["rep"], mesh.shape["fsdp"])
    return jax.shard_map(
        functools.partial(per_device, sizes),
        mesh=mesh,
        in_specs=(
            P(None, "fsdp"),
            P("rep", "fsdp"),
            P("rep", None, "fsdp"),
            P("rep", None, "fsdp"),
            P("rep", "fsdp", None),
            P("rep", None, "fsdp"),
            P("rep", None, None),
        ),
        out_specs=(P(None, "fsdp"), P("rep", "fsdp")),
        check_vma=False,
    )
```

```python
import functools
import math
import jax
import jax.numpy as jnp
from jax import lax
from jax.experimental import pallas as pl
from jax.experimental.pallas import tpu as pltpu
from jax.sharding import PartitionSpec as P

F32 = jnp.float32
BF16 = jnp.bfloat16
WIRE = jnp.float16
WIRE_SCALE = 64.0
LANES = 128
SLABS = 4
PIECE = 8192
MIB = 1024 * 1024


def forward_kernel(part_ref, weights_ref, turned_ref, product_ref):
    depth = part_ref.shape[1]
    block = depth // SLABS
    product = jnp.zeros(product_ref.shape, F32)
    for begin in range(0, depth, block):
        place = pl.ds(begin, block)
        part = part_ref[:, place]
        product += jnp.dot(part, weights_ref[place, :], preferred_element_type=F32)
        turned_ref[place, :] = part.T
    product_ref[...] = product


def forward(part, weights):
    rows, depth = part.shape
    columns = weights.shape[1]
    vmem = pl.BlockSpec(memory_space=pltpu.VMEM)
    return pl.pallas_call(
        forward_kernel,
        in_specs=[vmem, vmem],
        out_specs=[vmem, vmem],
        out_shape=[
            jax.ShapeDtypeStruct((depth, rows), BF16),
            jax.ShapeDtypeStruct((rows, columns), F32),
        ],
        compiler_params=pltpu.CompilerParams(vmem_limit_bytes=8 * MIB),
        cost_estimate=pl.CostEstimate(
            flops=2 * rows * depth * columns,
            bytes_accessed=2 * depth * columns + 4 * rows * depth,
            transcendentals=0,
        ),
        name="forward",
    )(part, weights)


def pinned(array):
    return pltpu.with_memory_space_constraint(array, pltpu.HBM)


def fetch_kernel(chunk, first_ref, second_ref, first_out, second_out, semaphore):
    width = first_out.shape[-1]
    columns = pl.ds(chunk * width, width)
    copies = [
        pltpu.make_async_copy(source.at[..., columns], target, semaphore.at[index])
        for index, (source, target) in enumerate(((first_ref, first_out), (second_ref, second_out)))
    ]
    for copy in copies:
        copy.start()
    for copy in copies:
        copy.wait()


def fetch(chunk, width, first, second):
    out = jax.ShapeDtypeStruct(first.shape[:-1] + (width,), F32)
    return pl.pallas_call(
        functools.partial(fetch_kernel, chunk),
        in_specs=[pl.BlockSpec(memory_space=pl.ANY)] * 2,
        out_specs=[pl.BlockSpec(memory_space=pltpu.VMEM)] * 2,
        out_shape=[out, out],
        scratch_shapes=[pltpu.SemaphoreType.DMA((2,))],
        compiler_params=pltpu.CompilerParams(vmem_limit_bytes=MIB),
        name="fetch",
    )(pinned(first), pinned(second))


def changed_place(mine, slab, pair, pairs):
    offset = lax.bitwise_xor(slab * pairs + pair, mine // 2)
    bits = (SLABS * pairs).bit_length() - 1
    place = jnp.int32(0)
    for bit in range(bits):
        place = place * 2 + lax.rem(lax.shift_right_logical(offset, bit), 2)
    return place


def inner_kernel(
    tokens,
    kept,
    fetched,
    mine_ref,
    low_ref,
    high_ref,
    low_turned_ref,
    high_turned_ref,
    start_ref,
    first_ref,
    second_ref,
    low_product_ref,
    high_product_ref,
    target_ref,
    count_ref,
    *rest,
):
    *rest, first_state, second_state, output_state, residual_state, gradient_state, rounded_state = rest
    change_refs, weights_state = (rest[:-1], rest[-1]) if kept else (rest, None)
    send_refs, keep_refs = change_refs[::2], change_refs[1::2]
    step = pl.program_id(0)
    slab = pl.program_id(1)
    if fetched:
        first_ref, second_ref = first_ref.at[slab], second_ref.at[slab]
    pairs, cores, rows, _ = start_ref.shape
    mine = mine_ref[0]
    core = lax.rem(mine, cores)
    height = PIECE // start_ref.shape[-1]
    pieces = [pl.ds(begin, height) for begin in range(0, rows, height)]
    slots = [(slot, *divmod(slot, cores)) for slot in range(pairs * cores)]
    held = gradient_state.shape[0]

    def weigh(output, which):
        residual = ((output - target_ref[...].astype(F32)) / tokens).astype(BF16)
        residual_state[...] = (residual.astype(F32) * count_ref[which]).astype(BF16)

    def descend(first, second, weights):
        root = second * lax.rsqrt(second)
        below = (100.0 * math.sqrt(0.05)) * root + 1e-06
        return 0.99 * weights - first * lax.rsqrt(below * below)

    def differentiate(pair, which, slot):
        turned = jnp.concatenate(
            [low_turned_ref[slab, pair, which], high_turned_ref[slab, pair, which]], axis=1
        )
        gradient_state[slot % held] = jnp.dot(
            turned, residual_state[...], preferred_element_type=F32
        )

    def project(slot):
        begin = (slab * pairs * cores + slot) * rows
        place = pl.ds(pl.multiple_of(begin, rows), rows)
        picked = jnp.concatenate([low_ref[:, place], high_ref[:, place]], axis=0)
        return jnp.dot(picked, rounded_state[slot % held], preferred_element_type=F32)

    @pl.when((step == 0) & (slab == 0))
    def _():
        weigh(jnp.concatenate([low_product_ref[...], high_product_ref[...]], axis=0), 0)
        output_state[...] = jnp.zeros_like(output_state)

    @pl.when((step == 1) & (slab == 0))
    def _():
        weigh(output_state[...], 1)

    @pl.when(step == 0)
    def _():
        differentiate(0, 0, 0)
        for slot, pair, which in slots:
            if slot + 1 < len(slots):
                ahead, *place = slots[slot + 1]
                differentiate(*place, ahead)
            for piece in pieces:
                gradient = gradient_state[slot % held, piece]
                first = 9.0 * first_ref[pair, which, piece] + gradient
                second = 19.0 * second_ref[pair, which, piece] + gradient * gradient
                weights = descend(first, second, start_ref[pair, which, piece].astype(F32))
                first_state[slab, pair, which, piece] = first
                second_state[slab, pair, which, piece] = second
                if kept:
                    weights_state[slab, pair, which, piece] = weights
                rounded_state[slot % held, piece] = weights.astype(BF16)
            output_state[...] += project(slot)

    @pl.when(step == 1)
    def _():
        sides = ((1 - core, send_refs), (core, keep_refs))
        differentiate(0, sides[0][0], 0)
        for slot, pair, side in slots:
            if slot + 1 < len(slots):
                ahead, next_pair, next_side = slots[slot + 1]
                differentiate(next_pair, sides[next_side][0], ahead)
            which, out_refs = sides[side]
            place = changed_place(mine, slab, pair, pairs)
            for piece in pieces:
                gradient = gradient_state[slot % held, piece]
                first = first_state[slab, pair, which, piece]
                second = second_state[slab, pair, which, piece]
                start = start_ref[pair, which, piece].astype(F32)
                if kept:
                    weights = weights_state[slab, pair, which, piece]
                else:
                    weights = descend(first, second, start)
                first = 0.9 * first + gradient
                second = 0.95 * second + gradient * gradient
                change = (start - descend(first, second, weights)) * WIRE_SCALE
                for index, out_ref in enumerate(out_refs):
                    part = out_ref.shape[-1]
                    out_ref[place, piece] = change[:, index * part : (index + 1) * part]


def inner(call, width, part, fetched, mine, banks, turned, start, first, second, products, target, count, tokens):
    slabs, pairs, cores, rows, _ = start.shape
    half, depth = banks[0].shape

    def held(step, slab):
        return jnp.where(step == 0, slab, slabs - 1)

    whole = pl.BlockSpec(memory_space=pltpu.VMEM)
    tile = (None, pairs, cores, rows, width)
    state = pl.BlockSpec(tile, lambda s, z, c: (held(s, z), 0, 0, 0, call))
    product = pl.BlockSpec((half, width), lambda s, z, c: (0, call))
    change = jax.ShapeDtypeStruct((slabs * pairs, rows, part), F32)
    outputs = 2 * (width // part)
    kept = width == part
    elements = depth * width
    states = (first, second) if fetched else (pinned(first), pinned(second))
    return pl.pallas_call(
        functools.partial(inner_kernel, float(tokens), kept, fetched),
        grid_spec=pltpu.PrefetchScalarGridSpec(
            num_scalar_prefetch=1,
            grid=(2, slabs),
            in_specs=[whole] * 4
            + [
                pl.BlockSpec(tile, lambda s, z, c: (z, 0, 0, 0, call)),
                whole if fetched else state,
                whole if fetched else state,
                product,
                product,
                pl.BlockSpec((2 * half, width), lambda s, z, c: (0, call)),
                pl.BlockSpec(count.shape, lambda s, z, c: (0, 0, 0)),
            ],
            out_specs=[whole] * outputs,
            scratch_shapes=[pltpu.VMEM((slabs, pairs, cores, rows, width), F32)] * (2 + kept)
            + [
                pltpu.VMEM((2 * half, width), F32),
                pltpu.VMEM((2 * half, width), BF16),
                pltpu.VMEM((2, rows, width), F32),
                pltpu.VMEM((2, rows, width), BF16),
            ],
        ),
        out_shape=[change] * outputs,
        compiler_params=pltpu.CompilerParams(vmem_limit_bytes=(22 if kept else 32) * MIB),
        cost_estimate=pl.CostEstimate(
            flops=12 * half * elements,
            bytes_accessed=20 * elements,
            transcendentals=6 * elements,
        ),
        name="inner",
    )(mine, *banks, *turned, pinned(start), *states, *products, target, count)


def assemble_kernel(begins, offsets, place_ref, *refs):
    out_ref, semaphore = refs[-2:]
    width = refs[0].shape[-1]
    mine = place_ref[0]
    copies = []
    for ref, begin, group in zip(refs, begins, offsets):
        for entry, offset in enumerate(group):
            copies.append(
                pltpu.make_async_copy(
                    ref.at[entry],
                    out_ref.at[lax.bitwise_xor(mine, offset), :, pl.ds(begin, width)],
                    semaphore.at[len(copies)],
                )
            )
    for copy in copies:
        copy.start()
    for copy in copies:
        copy.wait()


def assemble(place, blocks, shape, before):
    begins, received, offsets = zip(*blocks)
    vmem = pl.BlockSpec(memory_space=pltpu.VMEM)
    return pl.pallas_call(
        functools.partial(assemble_kernel, begins, offsets),
        in_specs=[pl.BlockSpec(memory_space=pltpu.SMEM)]
        + [vmem] * len(received)
        + [pl.BlockSpec(memory_space=pl.ANY)] * len(before),
        out_specs=pl.BlockSpec(memory_space=pl.ANY),
        out_shape=jax.ShapeDtypeStruct(shape, BF16),
        input_output_aliases={1 + len(received): 0} if before else {},
        scratch_shapes=[pltpu.SemaphoreType.DMA((sum(map(len, offsets)),))],
        compiler_params=pltpu.CompilerParams(vmem_limit_bytes=12 * MIB),
        cost_estimate=pl.CostEstimate(
            flops=0, bytes_accessed=4 * sum(array.size for array in received), transcendentals=0
        ),
        name="assemble",
    )(place, *received, *before)


def tied(first, second):
    return lax.optimization_barrier((first, second))


def per_device(sizes, global_weights, momentum, first_moment, second_moment, hidden_bank, target_bank, token_ids):
    reps, shards = sizes
    bits = reps.bit_length() - 1
    depth, columns = global_weights.shape
    rows = depth // reps
    store = hidden_bank.shape[1] * shards
    half = store // 2
    ids = token_ids[0]
    tokens = ids.shape[1]
    width = min(columns, LANES)
    chunks = columns // width
    mine = lax.axis_index("rep")

    def swapped(array, offset):
        pairs = [(index, index ^ offset) for index in range(reps)]
        return lax.ppermute(array, "rep", pairs)

    spans = [[0, 1 << bit] for bit in range(1, bits)]

    cut = (SLABS, reps // (2 * SLABS), 2, rows, columns)
    start = global_weights.reshape(cut)
    first = first_moment.reshape(cut)
    second = second_moment.reshape(cut)

    own_bank = hidden_bank[0]
    target = target_bank[0]
    count = jnp.sum(
        ids[:, :, None] == jnp.arange(store, dtype=ids.dtype)[None, None, :], axis=1
    ).astype(F32)
    if shards == 2:
        banks = (own_bank, lax.ppermute(own_bank, "fsdp", [(0, 1), (1, 0)]))
        swap = lax.axis_index("fsdp") == 1
        target = jnp.where(swap, jnp.roll(target, half, axis=0), target)
        count = jnp.where(swap, jnp.roll(count, half, axis=1), count)
    else:
        whole = lax.all_gather(own_bank, "fsdp", axis=0, tiled=True)
        banks = (whole[:half], whole[half:])
    count = count[:, :, None]

    place = mine.reshape(1).astype(jnp.int32)
    if chunks == 4:
        calls = [(2 * width, width), (0, 2 * width), (3 * width, width)]
    else:
        calls = [(begin, width) for begin in range(0, columns, width)]
    begins = [begin + part for begin, wide in calls for part in range(0, wide, width)]

    def start_rows(owner):
        return lax.dynamic_slice_in_dim(global_weights, owner * rows, rows, 0)

    pair_start = jnp.stack([start_rows(mine), start_rows(mine ^ spans[-1][1])])
    shares = [
        tied(momentum[:, begin : begin + width], pair_start[:, :, begin : begin + width])
        for begin in begins
    ]

    own = forward(banks[0], global_weights)
    early = fetch(calls[0][0] // width, width, first, second)
    received, (shares, own, early) = tied(banks[1], (shares, own, early))
    turned, products = zip(own, forward(received, global_weights))
    banks = (banks[0], received)
    turned = [array.reshape(cut[:4] + (half,)) for array in turned]

    def parted(terms, span):
        size = terms[0].shape[0] // len(span)
        parts = [[term[begin : begin + size] for term in terms] for begin in range(0, size * len(span), size)]
        outgoing = [sum(term.astype(F32) for term in part).astype(WIRE) for part in parts[1:]]
        return outgoing, parts[0]

    def sent(outgoing, span):
        return [swapped(array, offset) for array, offset in zip(outgoing, span[1:])]

    result = ()

    def chain(chunk, keep, arrived):
        terms = [keep, arrived]
        for span in spans[:-1]:
            outgoing, terms = parted(terms, span)
            outgoing = yield outgoing
            arrived = yield sent(outgoing, span)
            terms = terms + arrived
        scale = WIRE_SCALE * reps
        momentum_share, starts = shares[chunk]
        total = sum(term.astype(F32) for term in terms)
        pushed = (0.81 / 1.9 * scale) * momentum_share
        rounded = jnp.stack([total[0] + pushed, total[1]]).astype(WIRE)
        rounded = lax.optimization_barrier((yield rounded))
        arrived, = yield sent([rounded], spans[-1])
        moved = 0.9 * momentum_share + (total[0] + arrived[1].astype(F32)) * (1.0 / scale)
        both = rounded.astype(F32) + arrived[::-1].astype(F32)
        stack = (starts.astype(F32) - (1.33 / scale) * both).astype(BF16)
        offsets = list(spans[-1])
        stack = yield stack
        back = spans[:-1] if chunk % 2 else spans[-2::-1]
        for span in back[:-1]:
            arrived = yield sent([stack], span)
            offsets = [offset ^ far for far in span for offset in offsets]
            stack = yield jnp.concatenate([stack] + arrived)
        across, = yield sent([stack], back[-1])
        ends = [0, back[-1][1], 1, back[-1][1] ^ 1]
        finished[chunk] = (moved, stack, across, [[offset ^ end for offset in offsets] for end in ends])
        yield ()

    finished = {}
    running = {}
    formed = {}

    def move_on(which, behind=()):
        which = [chunk for chunk in which if chunk not in finished]
        arrived = {chunk: running[chunk].send(formed[chunk]) for chunk in which}
        arrived, _ = tied(arrived, [formed[chunk] for chunk in behind])
        for chunk in which:
            formed[chunk] = running[chunk].send(arrived[chunk])

    token = place
    fresh = range(0)
    later = {}
    for begin, wide in calls:
        states = (first, second) if fresh else early
        changes = inner(
            begin // wide, wide, width, not fresh, token, banks, turned, start, *states, products, target, count, tokens
        )
        sends = [send.astype(WIRE) for send in changes[::2]]
        if fresh:
            move_on(range(fresh[0] + 1))
            for chunk in fresh[1:]:
                keep, arrived = later.pop(chunk)
                arrived, _ = tied(arrived, [formed[other] for other in range(fresh[0] + 1)])
                running[chunk] = chain(chunk, keep, arrived)
                formed[chunk] = next(running[chunk])
            sends, _ = tied(sends, [formed[chunk] for chunk in range(fresh.stop)])
        fresh = range(fresh.stop, fresh.stop + wide // width)
        for chunk, send, keep in zip(fresh, sends, changes[1::2]):
            later[chunk] = (keep, swapped(send, 1))
        running[fresh[0]] = chain(fresh[0], *later.pop(fresh[0]))
        formed[fresh[0]] = next(running[fresh[0]])
        if fresh.stop < chunks:
            formed, token = tied(formed, token)
    if chunks == 4:
        before = 3
        for which in (1, 0, 2, 3, 0, 1, 2):
            move_on([which], behind=[before])
            before = which
    for chunk in range(chunks):
        while chunk not in finished:
            move_on([chunk])

    blocks = []
    for chunk in range(chunks):
        _, stack, across, offsets = finished[chunk]
        if chunk == 1 and result:
            across, *result = tied(across, result[0])
        received = [stack, across, swapped(stack, 1), swapped(across, 1)]
        blocks += [(begins[chunk], array, group) for array, group in zip(received, offsets)]
        if chunk + 2 != chunks:
            result = (assemble(place, blocks, (reps, rows, columns), result),)
            blocks = []

    new_momentum = [finished[chunk][0] for chunk in sorted(range(chunks), key=begins.__getitem__)]

    return result[0].reshape(depth, columns), jnp.concatenate(new_momentum, axis=1)


def solution(mesh):
    sizes = (mesh.shape["rep"], mesh.shape["fsdp"])
    return jax.shard_map(
        functools.partial(per_device, sizes),
        mesh=mesh,
        in_specs=(
            P(None, "fsdp"),
            P("rep", "fsdp"),
            P("rep", None, "fsdp"),
            P("rep", None, "fsdp"),
            P("rep", "fsdp", None),
            P("rep", None, "fsdp"),
            P("rep", None, None),
        ),
        out_specs=(P(None, "fsdp"), P("rep", "fsdp")),
        check_vma=False,
    )
```
